256 devices in a mesh: grp: 4 (over x), gx: 8 (over z), gy: 8 (over y, core).
Axes of the slice: x: 4, y: 4, z: 8, core: 2. Of those that a mesh axis runs over, the one named last changes fastest.
Arguments:
- air: float32 [3, 80, 512, 1024], P(None, None, ('grp', 'gx'), 'gy'), may hold values from -6 to 6
- level_set: float32 [8192, 128, 128], P(('grp', 'gx', 'gy')), may hold values from -12 to 12
- fuel: int32 [8192, 128, 128], P(('grp', 'gx', 'gy')), may hold values from 0 to 12
- tile_list: int32 [4, 64, 32], P('grp'), may hold values from -1 to 2047, as said below
Outputs:
- air_next: float32 [3, 80, 512, 1024], P(None, None, ('grp', 'gx'), 'gy')
- level_set_next: float32 [8192, 128, 128], P(('grp', 'gx', 'gy'))
The draws below stay inside these ranges and needn't reach their ends.
Inputs may be any that keep to these rules, and one draw needn't show every extreme that they name: `tile_list`: in each band, every device's live slots come first and name tiles over distinct devices of the band; no tile is named twice; some device of each band has all 32 slots live; a tile t lies over device t // 32 of the band (index gx * 8 + gy).
All inputs are finite; a program needn't handle non-finite values.
Results may differ from the reference program's by a relative error of at most 0.0003.
Values sent between devices are 32-bit elements; how exact they have to be, the bound alone decides.
No kernel may reach another device: no remote copies, remote signals or barrier semaphores. Data moves between devices by JAX's collectives and lax.ppermute only.
A program may use at most 128 MiB of HBM per device.

```python
import jax
import jax.numpy as jnp
import numpy as np
from jax import lax

LEV = 80
TX = 16
TY = 128
SUB = 4
CELLS = 128
TILES_DEV = 32
GROUP = 64
FSLOTS = 32
NX = 512
NY = 1024
N_GRP = 4
N_GX = 8
N_GY = 8


def draw_tile_list(key, part):
    key = jax.random.fold_in(key, 11)
    subkeys = jax.random.split(key, 4)
    band_keys = jax.random.split(subkeys[0], N_GRP)
    offsets = jax.vmap(lambda band_key: jax.random.permutation(band_key, GROUP)[:FSLOTS])(band_keys)
    fire_ids = jnp.arange(GROUP, dtype=jnp.int32)[None, :, None]
    source = (fire_ids + offsets[:, None, :]) % GROUP
    spread = TILES_DEV // FSLOTS
    pick_tile = jax.random.randint(subkeys[1], (N_GRP, GROUP, FSLOTS), 0, spread)
    slot_ids = jnp.arange(FSLOTS, dtype=jnp.int32)[None, None, :]
    tile_id = source * TILES_DEV + slot_ids * spread + pick_tile
    counts = jax.random.randint(subkeys[2], (N_GRP, GROUP), FSLOTS - FSLOTS // 4, FSLOTS + 1)
    fullest = jax.random.randint(subkeys[3], (N_GRP,), 0, GROUP)
    counts = jnp.where(jnp.arange(GROUP)[None, :] == fullest[:, None], FSLOTS, counts)
    is_live = slot_ids < counts[:, :, None]
    return jnp.where(is_live, tile_id, -1).astype(jnp.int32)


def touch_ends(entries, key, low, high):
    shape = entries.shape
    index_at = [jax.random.randint(jax.random.fold_in(key, axis), (), 0, shape[axis]) for axis in range(len(shape))]
    entries = entries.at[tuple(index_at)].set(low)
    longest = shape.index(max(shape))
    index_at[longest] = (index_at[longest] + 1) % shape[longest]
    return entries.at[tuple(index_at)].set(high)


def shard_levels(rng, extent, cuts, least, largest):
    loudness, own = 1.0, jax.random.fold_in(rng, 6)
    for axis_at, blocks in cuts:
        heights = jnp.exp(jax.random.uniform(jax.random.fold_in(own, axis_at), (blocks,), jnp.float32, least / len(cuts), largest / len(cuts)))
        loudness = loudness * jnp.repeat(heights, extent[axis_at] // blocks).reshape([-1 if axis == axis_at else 1 for axis in range(len(extent))])
    return loudness


def centred(rng, extent, scale, reach, cuts=(), kind=jnp.bfloat16):
    values = jax.random.normal(rng, extent, jnp.float32) * scale
    if len(cuts) > 0:
        values = shard_levels(rng, extent, cuts, -0.22, 0.18) * values
    return jnp.clip(values, min=-reach, max=reach).astype(kind)


def setup_inputs(seed: int = 0) -> dict:
    seeds = jax.random.split(jax.random.key(seed), 5)
    return {
        "air": centred(seeds[0], (3, LEV, NX, NY), 1.0, 6.0, ((2, 32), (3, 8)), jnp.float32),
        "level_set": centred(seeds[1], (N_GRP * GROUP * FSLOTS, CELLS, CELLS), 3.0, 12.0, ((0, 256),), jnp.float32),
        "fuel": touch_ends(jax.random.randint(seeds[2], (N_GRP * GROUP * FSLOTS, CELLS, CELLS), 0, 13), jax.random.fold_in(seeds[2], 1), 0, 12).astype(jnp.int32),
        "tile_list": draw_tile_list(jax.random.fold_in(seeds[4], 71), 0),
    }


spread_rates = np.array([0.3, 0.5, 0.9, 1.2, 0.6, 0.4, 0.7, 0.35, 0.25, 0.45, 0.55, 0.8, 1.0], np.float32)
heat_yields = np.array([1.0, 2.5, 4.0, 3.0, 1.5, 2.0, 5.0, 1.2, 0.8, 3.5, 2.2, 4.5, 2.8], np.float32)
smoke_yields = np.array([0.5, 1.5, 2.5, 1.0, 3.0, 0.8, 2.0, 1.8, 0.6, 2.6, 1.1, 3.4, 1.4], np.float32)
courant = 0.1
viscosity = 0.1
buoyancy = 0.5
source_step = 0.5
fire_time = 0.1
wind_gain = 0.3

def lookup(category, table):
    result = jnp.zeros(category.shape, jnp.float32)
    for position in range(13):
        result = jnp.where(category == position, jnp.float32(table[position]), result)
    return result

def weights_table(cells, refine):
    spots = (jnp.arange(cells, dtype=jnp.float32) + 0.5) / refine + 0.5
    knots = jnp.arange(10, dtype=jnp.float32)
    return jnp.maximum(0.0, 1.0 - jnp.abs(spots[:, None] - knots[None, :]))

def fire_advance(phase, category, window, active):
    cells = phase.shape[0]
    refine = cells // 8
    table = weights_table(cells, refine)
    highest = lax.Precision.HIGHEST
    row_wind = jnp.dot(jnp.dot(table, window[0], precision=highest), table.T, precision=highest)
    col_wind = jnp.dot(jnp.dot(table, window[1], precision=highest), table.T, precision=highest)
    base_rate = lookup(category, spread_rates)
    for substep in range(SUB):
        padded = jnp.pad(phase, 1, mode='edge')
        back_row = phase - padded[:-2, 1:-1]
        ahead_row = padded[2:, 1:-1] - phase
        back_col = phase - padded[1:-1, :-2]
        ahead_col = padded[1:-1, 2:] - phase
        upwind = jnp.maximum(back_row, 0.0) ** 2 + jnp.minimum(ahead_row, 0.0) ** 2 + jnp.maximum(back_col, 0.0) ** 2 + jnp.minimum(ahead_col, 0.0) ** 2
        slope_row = 0.5 * (back_row + ahead_row)
        slope_col = 0.5 * (back_col + ahead_col)
        length = jnp.maximum(jnp.sqrt(slope_row * slope_row + slope_col * slope_col), 1.0)
        along = (row_wind * slope_row + col_wind * slope_col) / length
        rate = base_rate * (1.0 + wind_gain * jnp.maximum(along, 0.0))
        phase = phase - fire_time * rate * jnp.sqrt(upwind)
    burning = jax.nn.sigmoid(-phase)
    heat = (lookup(category, heat_yields) * burning).reshape(8, refine, 8, refine).mean(axis=(1, 3))
    smoke = (lookup(category, smoke_yields) * burning).reshape(8, refine, 8, refine).mean(axis=(1, 3))
    return (phase, jnp.concatenate([heat.reshape(64), smoke.reshape(64)]) * active)

def centre(field):
    return field[..., 1:-1, 1:-1]

def laplace(field):
    return field[..., 2:, 1:-1] + field[..., :-2, 1:-1] + field[..., 1:-1, 2:] + field[..., 1:-1, :-2] - 4.0 * centre(field)

def atmosphere(padded, heat_padded, emission):
    levels = padded.shape[1]
    profile = jnp.exp(-jnp.arange(levels, dtype=jnp.float32) * 8.0 / levels)[:, None, None]
    row_wind = centre(padded[0])
    col_wind = centre(padded[1])
    tracer = padded[2]
    middle = centre(tracer)
    upwind = jnp.maximum(row_wind, 0.0) * (middle - tracer[:, :-2, 1:-1]) + jnp.minimum(row_wind, 0.0) * (tracer[:, 2:, 1:-1] - middle) + jnp.maximum(col_wind, 0.0) * (middle - tracer[:, 1:-1, :-2]) + jnp.minimum(col_wind, 0.0) * (tracer[:, 1:-1, 2:] - middle)
    smoke_next = middle - courant * upwind + source_step * profile * emission
    heat_row = 0.5 * (heat_padded[2:, 1:-1] - heat_padded[:-2, 1:-1])
    heat_col = 0.5 * (heat_padded[1:-1, 2:] - heat_padded[1:-1, :-2])
    row_next = row_wind + viscosity * laplace(padded[0]) + buoyancy * profile * heat_row
    col_next = col_wind + viscosity * laplace(padded[1]) + buoyancy * profile * heat_col
    return jnp.stack([row_next, col_next, smoke_next])

def reference(air, level_set, fuel, tile_list):
    padded = jnp.pad(air, ((0, 0), (0, 0), (1, 1), (1, 1)))
    surface = padded[0:2, 0]
    listed = tile_list.reshape(-1)
    active = (listed >= 0).astype(jnp.float32)
    tile_id = jnp.maximum(listed, 0)
    band_id = jnp.arange(listed.shape[0], dtype=jnp.int32) // (GROUP * FSLOTS)
    owner = tile_id // TILES_DEV
    local_tile = tile_id % TILES_DEV
    tile_cols = TY // 8
    row_start = ((band_id * N_GX + owner // N_GY) * TX + local_tile // tile_cols * 8).astype(jnp.int32)
    col_start = (owner % N_GY * TY + local_tile % tile_cols * 8).astype(jnp.int32)

    def cut_window(row_at, col_at):
        return lax.dynamic_slice(surface, (jnp.int32(0), row_at, col_at), (2, 10, 10))
    windows = jax.vmap(cut_window)(row_start, col_start) * active[:, None, None, None]

    def advance_one(packed):
        return fire_advance(packed[0], packed[1], packed[2], packed[3])
    phases, fluxes = lax.map(advance_one, (level_set, fuel, windows, active))
    fluxes = fluxes.reshape(-1, 2, 8, 8)
    eight = jnp.arange(8, dtype=jnp.int32)
    row_index = row_start[:, None, None] + eight[None, :, None]
    col_index = col_start[:, None, None] + eight[None, None, :]
    heat = jnp.zeros((NX, NY), jnp.float32).at[row_index, col_index].add(fluxes[:, 0])
    emission = jnp.zeros((NX, NY), jnp.float32).at[row_index, col_index].add(fluxes[:, 1])
    heat_padded = jnp.pad(heat, 1)
    return (atmosphere(padded, heat_padded, emission), phases)
```

```python
import jax
import jax.numpy as jnp
import numpy as np
from jax import lax
from jax.experimental import pallas as pl
from jax.experimental.pallas import tpu as pltpu
from jax.sharding import PartitionSpec as P

SUB = 4
LEV = 80
N_GRP, N_GX, N_GY = 4, 8, 8

spread_rates = np.array(
    [0.3, 0.5, 0.9, 1.2, 0.6, 0.4, 0.7, 0.35, 0.25, 0.45, 0.55, 0.8, 1.0], np.float32
)
heat_yields = np.array(
    [1.0, 2.5, 4.0, 3.0, 1.5, 2.0, 5.0, 1.2, 0.8, 3.5, 2.2, 4.5, 2.8], np.float32
)
smoke_yields = np.array(
    [0.5, 1.5, 2.5, 1.0, 3.0, 0.8, 2.0, 1.8, 0.6, 2.6, 1.1, 3.4, 1.4], np.float32
)
courant = 0.1
viscosity = 0.1
buoyancy = 0.5
source_step = 0.5
fire_time = 0.1
wind_gain = 0.3

F32 = jnp.float32
BF16 = jnp.bfloat16
VMEM = pl.BlockSpec(memory_space=pltpu.VMEM)
SMEM = pl.BlockSpec(memory_space=pltpu.SMEM)
ANY = pl.BlockSpec(memory_space=pl.ANY)


def room(mib):
    return pltpu.CompilerParams(vmem_limit_bytes=mib * 1024 * 1024)


def shape(*dims, dtype=F32):
    return jax.ShapeDtypeStruct(dims, dtype)


def cost(flops, moved):
    return pl.CostEstimate(flops=flops, bytes_accessed=moved, transcendentals=0)


def lanes_of(rows=8):
    return lax.broadcasted_iota(jnp.int32, (rows, 128), 1)


def sublanes_of(rows=8):
    return lax.broadcasted_iota(jnp.int32, (rows, 128), 0)


def halves(value):
    high = value.astype(BF16).astype(F32)
    return high, value - high


def spread_line(line, row, low, high, rims):
    lane, sub = lanes_of(), sublanes_of()
    line = jnp.broadcast_to(line, (8, 128))
    here = (lane >= 12 * row) & (lane < 12 * row + 10)
    fanned = pltpu.roll(line, 0, 1, stride=8, stride_axis=0)
    first = pltpu.roll(fanned, (12 * row + 73) % 128, 1)
    second = pltpu.roll(fanned, (12 * row + 9) % 128, 1)
    low = jnp.where(here & ((sub < 7) | (lane > 12 * row)), first, low)
    high = jnp.where(here & ((sub > 0) | (lane < 12 * row + 9)), second, high)
    edges = pltpu.roll(line, (12 * row + 11) % 128, 1)
    rims = jnp.where((lane == 12 * row + 10 + sub) & (sub < 2), edges, rims)
    return low, high, rims


def table_kernel(surf_ref, tile_ref):
    none = jnp.zeros((8, 128), F32)
    for comp in range(2):
        lanes = slice(128 * comp, 128 * comp + 128)
        field = surf_ref[comp] * wind_gain
        for half in range(2):
            low = high = rims = none
            for row in range(10):
                at = 8 * half + row - 1
                if 0 <= at < 16:
                    low, high, rims = spread_line(field[at : at + 1], row, low, high, rims)
            tile_ref[16 * half : 16 * half + 8, lanes] = low
            tile_ref[16 * half + 8 : 16 * half + 16, lanes] = high
            tile_ref[40 + 8 * half : 48 + 8 * half, lanes] = rims
        tile_ref[32:40, lanes] = none


def windows_kernel(
    pick_ref, table_ref, above_ref, below_ref, left_ref, out_ref, token_ref, tile_ref
):
    token_ref[...] = jnp.zeros((8, 128), F32) + left_ref[0:1, 0:128] * 0.0
    tile_ref[...] = table_ref[...]
    for comp in range(2):
        lanes = slice(128 * comp, 128 * comp + 128)
        line_at = slice(LEV * comp, LEV * comp + 1)
        for half, (ref, row) in enumerate(((above_ref, 0), (below_ref, 9))):
            places = (
                slice(16 * half, 16 * half + 8),
                slice(16 * half + 8, 16 * half + 16),
                slice(40 + 8 * half, 48 + 8 * half),
            )
            old = [tile_ref[rows, lanes] for rows in places]
            fresh = spread_line(ref[line_at, :] * wind_gain, row, *old)
            for rows, value in zip(places, fresh):
                tile_ref[rows, lanes] = value

    def one(at, carry):
        for spot in range(16):
            fire = 16 * at + spot
            picks = pick_ref[fire]
            own = tile_ref[pl.ds(picks & 63, 1), :]
            rim_right = tile_ref[pl.ds((picks >> 6) & 63, 1), :]
            rim_left = tile_ref[pl.ds(picks >> 12, 1), :]
            out_ref[fire] = own + (rim_right + rim_left)
        return carry

    lax.fori_loop(0, 4, one, 0)


def fire_kernel(
    slots_ref, phase_in, fuel_in, recv_ref, words_ref, wcol_ref, spread_ref,
    left_in, right_in, token_in, out_ref, msg_ref, left_out, right_out,
    phase_ref, fuel_ref, done_ref, column_ref, sums_ref, means_ref, bag_ref, *rest,
):
    buffers, sem, sem_in = rest[:-2], rest[-2], rest[-1]
    sides = [buffers[at::2] for at in range(2)]
    left_out[...] = left_in[...]
    right_out[...] = right_in[...]
    loads = []
    for at, (low, high) in enumerate(((0, 2), (2, 8), (8, 32))):
        some = pl.ds(low, high - low)
        loads.append(
            (
                pltpu.make_async_copy(phase_in.at[some], phase_ref.at[some], sem_in.at[at]),
                pltpu.make_async_copy(fuel_in.at[some], fuel_ref.at[some], sem_in.at[3 + at]),
            )
        )
        for load in loads[-1]:
            load.start()
    lane24 = lanes_of(24)
    knot = sublanes_of(24)
    knot = (knot & 7) + (knot >> 3)
    unfold = (lane24 >= 12 * knot) & (lane24 < 12 * knot + 12)
    place = lax.broadcasted_iota(jnp.int32, (1, 128), 1) % 12
    words = words_ref[...]
    row8, lane8 = sublanes_of(), lanes_of()

    def place_of(slot):
        tile = slots_ref[slot]
        return jnp.maximum(tile, 0) >> 5, jnp.maximum(tile, 0) & 15, tile >= 0

    def columns(at, carry):
        parts = []
        for spot in range(4):
            owner, col, live = place_of(4 * at + spot)
            gy = owner & (N_GY - 1)
            left = jnp.maximum(owner - 1, 0)
            right = jnp.minimum(owner + 1, N_GX * N_GY - 1)
            left_rim = (place == 10) & ((col == 0) & (gy > 0))
            right_rim = (place == 11) & ((col == 15) & (gy < N_GY - 1))
            for comp in range(2):
                lanes = slice(128 * comp, 128 * comp + 128)
                line = jnp.where(place < 10, recv_ref[owner, :, lanes], 0.0)
                line = jnp.where(left_rim, recv_ref[left, :, lanes], line)
                line = jnp.where(right_rim, recv_ref[right, :, lanes], line)
                line = jnp.where(live, line, 0.0)
                parts.append(jnp.where(unfold, jnp.broadcast_to(line, (24, 128)), 0.0))
        high, low = halves(jnp.concatenate(parts, axis=0))
        both = jnp.dot(high.astype(BF16), wcol_ref[...], preferred_element_type=F32) + jnp.dot(
            low.astype(BF16), wcol_ref[...], preferred_element_type=F32
        )
        for spot in range(4):
            column_ref[4 * at + spot] = both[48 * spot : 48 * spot + 48]
        return carry

    def result(slot):
        return pltpu.make_async_copy(done_ref.at[slot], out_ref.at[slot], sem.at[slot])

    def block(at):
        return slice(8 * at, 8 * at + 8)

    def store(target, at, values):
        field, behind, beyond = target
        turned = [pltpu.roll(value, 1, 1) for value in values]
        for k, value in enumerate(values):
            field[block(at + k), :] = value
        backs = [jnp.where(lane8 == 0, 0.0, x - y) for x, y in zip(values, turned)]
        aheads = [pltpu.roll(back, 127, 1) for back in backs]
        for k, (back, ahead) in enumerate(zip(backs, aheads)):
            behind[block(at + k), :] = back
            beyond[block(at + k), :] = ahead

    def begin(slot, side):
        gust, rate, word = side[:3]
        runs = [column_ref[slot, 8 * at : 8 * at + 8, :] for at in range(6)]
        steps = [runs[at + 1] - runs[at] for at in (0, 1, 3, 4)]
        for first in range(0, 16, 8):
            blocks = range(first, first + 8)
            places = [pl.ds(j, 8, stride=16) for j in blocks]
            fuels = [fuel_ref[slot, there, :] for there in places]
            packed = [
                jnp.take_along_axis(words, fuel, axis=1, mode="promise_in_bounds")
                for fuel in fuels
            ]
            store(side[3:6], first, [phase_ref[slot, there, :] for there in places])
            bases = [(x & 31).astype(F32) * np.float32(0.05 * fire_time) for x in packed]
            for j, x, base in zip(blocks, packed, bases):
                rate[block(j), :] = base
                word[block(j), :] = x
            low = first // 8
            for comp in range(2):
                run, step = runs[3 * comp + low], steps[2 * comp + low]
                parts = [np.float32((j + 0.5) / 16 + 0.5 - low) for j in blocks]
                winds = [run + part * step for part in parts]
                for j, wind, base in zip(blocks, winds, bases):
                    gust[block(16 * comp + j), :] = wind * base

    def advance(side, source, keep):
        gust, rate = side[:2]
        field, behind, beyond = source
        edge = field[block(0), :] - pltpu.roll(field[block(15), :], 1, 0)
        edge = jnp.where(row8 == 0, 0.0, edge)
        last = pltpu.roll(edge, 7, 0)
        for first in range(0, 16, 8):
            blocks = range(first, first + 8)
            fields = [field[block(j), :] for j in range(first, min(first + 9, 16))]
            aheads = [y - x for x, y in zip(fields, fields[1:])]
            if first == 8:
                aheads.append(last)
            backs = [edge] + aheads[:-1]
            edge = aheads[-1]
            side_backs = [behind[block(j), :] for j in blocks]
            side_aheads = [beyond[block(j), :] for j in blocks]
            a = [jnp.maximum(x, 0.0) for x in backs]
            b = [jnp.minimum(x, 0.0) for x in aheads]
            upwinds = [x * x + y * y for x, y in zip(a, b)]
            c = [jnp.maximum(x, 0.0) for x in side_backs]
            d = [jnp.minimum(x, 0.0) for x in side_aheads]
            upwinds = [u + (x * x + y * y) for u, x, y in zip(upwinds, c, d)]
            inverses = [lax.rsqrt(jnp.maximum(u, 1e-36)) for u in upwinds]
            row_slopes = [x + y for x, y in zip(backs, aheads)]
            col_slopes = [x + y for x, y in zip(side_backs, side_aheads)]
            squares = [x * x + y * y for x, y in zip(row_slopes, col_slopes)]
            factors = [lax.rsqrt(jnp.maximum(x, 4.0)) for x in squares]
            along = [
                gust[block(j), :] * x + gust[block(16 + j), :] * y
                for j, x, y in zip(blocks, row_slopes, col_slopes)
            ]
            roots = [u * x for u, x in zip(upwinds, inverses)]
            speeds = [
                rate[block(j), :] + jnp.maximum(x * f, 0.0)
                for j, x, f in zip(blocks, along, factors)
            ]
            keep(first, [x - v * r for x, v, r in zip(fields, speeds, roots)])

    def finish(slot, side):
        word = side[2]
        sums = [[], []]

        def keep(first, values):
            for k, value in enumerate(values):
                done_ref[slot, pl.ds(first + k, 8, stride=16), :] = value
            burning = [jnp.exp(value) for value in values]
            burning = [1.0 / (1.0 + value) for value in burning]
            packed = [word[block(first + k), :] for k in range(8)]
            heats = [((x >> 5) & 63).astype(F32) * y for x, y in zip(packed, burning)]
            smokes = [(x >> 11).astype(F32) * y for x, y in zip(packed, burning)]
            for total, terms in zip(sums, (heats, smokes)):
                while len(terms) > 1:
                    terms = [x + y for x, y in zip(terms[::2], terms[1::2])]
                total.append(terms[0])

        advance(side, side[6:9], keep)
        result(slot).start()
        sums_ref[slot, :, 0:128] = sums[0][0] + sums[0][1]
        sums_ref[slot, :, 128:256] = sums[1][0] + sums[1][1]

    def into(target):
        return lambda first, values: store(target, first, values)

    lax.fori_loop(0, 8, columns, 0)

    def pair(at, carry):
        slot = 2 * at
        for start, some in zip((0, 1, 4), loads):

            @pl.when(at == start)
            def _():
                for load in some:
                    load.wait()

        for spot, side in enumerate(sides):
            begin(slot + spot, side)
        for step in range(SUB - 1):
            for side in sides:
                pair_of = (side[3:6], side[6:9])
                advance(side, pair_of[step % 2], into(pair_of[1 - step % 2]))
        for spot, side in enumerate(sides):
            finish(slot + spot, side)
        return carry

    lax.fori_loop(0, 16, pair, 0)
    high, low = halves(sums_ref[...].reshape(256, 256))
    spread = spread_ref[...]
    means_ref[...] = (
        jnp.dot(high.astype(BF16), spread, preferred_element_type=F32)
        + jnp.dot(low.astype(BF16), spread, preferred_element_type=F32)
    ) * np.float32(0.1 / 256)
    dense = means_ref[pl.ds(0, 32, stride=8), :]
    for row in range(1, 8):
        dense = dense + pltpu.roll(means_ref[pl.ds(row, 32, stride=8), :], 16 * row, 1)
    means_ref[0:32, :] = dense
    bag_ref[...] = jnp.zeros(bag_ref.shape, F32)
    spot = lax.broadcasted_iota(jnp.int32, (1, 128), 1) % 16
    own, beside = slice(0, 128), slice(128, 256)

    def send(slot, carry):
        owner, col, live = place_of(slot)
        gy = owner & (N_GY - 1)
        line = means_ref[pl.ds(slot, 1), :]
        bag_ref[jnp.where(live, owner, 64), :, own] = line
        to_left = live & (col == 0) & (gy > 0)
        to_right = live & (col == 15) & (gy < N_GY - 1)
        target = jnp.where(to_left, owner - 1, jnp.where(to_right, owner + 1, 64))
        kept = jnp.where(to_left, 0, 7)
        bag_ref[target, :, beside] = jnp.where(spot == kept, line, bag_ref[target, :, beside])
        return carry

    lax.fori_loop(0, 32, send, 0, unroll=4)
    msg_ref[...] = bag_ref[0:64]

    def settle(slot, carry):
        result(slot).wait()
        return carry

    lax.fori_loop(0, 32, settle, 0)


def place_kernel(where_ref, flux_ref, heat_ref, side_ref, smoke_ref, first_ref, last_ref):
    lane, sub = lanes_of(), sublanes_of()
    key = lane // 8
    heat_from = sub * 16 + lane % 8
    zero = jnp.zeros((8, 128), F32)

    def tile(at, lanes):
        fire = where_ref[at]
        line = flux_ref[jnp.maximum(fire, 0), :, lanes]
        return jnp.where(fire >= 0, jnp.broadcast_to(line, (8, 128)), 0.0)

    def find(value, index):
        return jnp.take_along_axis(value, index, axis=1, mode="promise_in_bounds")

    own, beside = slice(0, 128), slice(128, 256)
    for half in range(2):
        rows = slice(8 * half, 8 * half + 8)
        heat = smoke = zero
        for col in range(16):
            value = tile(16 * half + col, own)
            heat = jnp.where(key == col, find(value, heat_from), heat)
            smoke = jnp.where(key == col, find(value, heat_from + 8), smoke)
        rim_left = find(tile(32 + half, beside), heat_from)
        rim_right = find(tile(34 + half, beside), heat_from)
        left = pltpu.roll(jnp.where(lane == 127, rim_left, heat), 1, 1)
        right = pltpu.roll(jnp.where(lane == 0, rim_right, heat), 127, 1)
        heat_ref[rows, :] = heat
        smoke_ref[rows, :] = smoke
        side_ref[rows, :] = 0.5 * (right - left)
        if half == 0:
            first_ref[...] = heat[0:1]
        else:
            last_ref[...] = heat[7:8]


def rows_kernel(air_ref, first_ref, last_ref, surf_ref, sem):
    copies = (
        pltpu.make_async_copy(air_ref.at[:, 0, :], first_ref, sem.at[0]),
        pltpu.make_async_copy(air_ref.at[:, 15, :], last_ref, sem.at[1]),
        pltpu.make_async_copy(air_ref.at[0], surf_ref.at[0], sem.at[2]),
        pltpu.make_async_copy(air_ref.at[LEV], surf_ref.at[1], sem.at[3]),
    )
    for copy in copies:
        copy.start()
    for copy in copies:
        copy.wait()


def sides_kernel(air_ref, left_ref, right_ref):
    lane, sub = lanes_of(), sublanes_of()
    pick = jnp.where((lane == 127 * sub) & (sub < 2), 1.0, 0.0)
    picked = lax.dot_general(
        pick, air_ref[...].reshape(3 * LEV * 16, 128), (((1,), (1,)), ((), ())),
        precision=lax.Precision.HIGHEST, preferred_element_type=F32,
    )
    left_ref[...] = picked[0:1]
    right_ref[...] = picked[1:2]


def air_kernel(air_ref, above_ref, below_ref, token_in, out_ref, token_ref):
    token_ref[...] = token_in[...]
    lane = lax.broadcasted_iota(jnp.int32, (8, 16, 128), 2)
    row = lax.broadcasted_iota(jnp.int32, (8, 16, 128), 1)

    def chunk(at, carry):
        fields = []
        for part in range(3):
            start = part * LEV + at * 8
            mid = air_ref[pl.ds(start, 8)]
            above = above_ref[pl.ds(start, 8), :][:, None, :]
            below = below_ref[pl.ds(start, 8), :][:, None, :]
            up = jnp.where(row == 0, above, pltpu.roll(mid, 1, 1))
            down = jnp.where(row == 15, below, pltpu.roll(mid, 15, 1))
            left = jnp.where(lane == 0, 0.0, pltpu.roll(mid, 1, 2))
            right = jnp.where(lane == 127, 0.0, pltpu.roll(mid, 127, 2))
            fields.append((mid, up, down, left, right))
        for part in range(2):
            mid, up, down, left, right = fields[part]
            around = (up + down) + (left + right)
            out_ref[pl.ds(part * LEV + at * 8, 8)] = mid + viscosity * (around - 4.0 * mid)
        u, v = fields[0][0], fields[1][0]
        mid, up, down, left, right = fields[2]
        upwind = (
            jnp.maximum(u, 0.0) * (mid - up)
            + jnp.minimum(u, 0.0) * (down - mid)
            + jnp.maximum(v, 0.0) * (mid - left)
            + jnp.minimum(v, 0.0) * (right - mid)
        )
        out_ref[pl.ds(2 * LEV + at * 8, 8)] = mid - courant * upwind
        return carry

    lax.fori_loop(0, LEV // 8, chunk, 0)


def rims_kernel(part_ref, left_ref, right_ref, own_left_ref, own_right_ref, out_ref):
    sub, lane = sublanes_of(), lanes_of()
    expand = jnp.where((sub < 2) & (lane == 0), 1.0, 0.0) + jnp.where(
        (sub >= 2) & (sub < 4) & (lane == 127), 1.0, 0.0
    )
    expand = expand.astype(BF16)

    def chunk(at, carry):
        for part in range(3):
            spot = pl.ds(pl.multiple_of(part * (LEV * 16) + at * 128, 128), 128)
            left, right = left_ref[:, spot], right_ref[:, spot]
            if part < 2:
                left, right = viscosity * left, viscosity * right
            else:
                wind = pl.ds(pl.multiple_of(LEV * 16 + at * 128, 128), 128)
                left = courant * jnp.maximum(own_left_ref[:, wind], 0.0) * left
                right = -courant * jnp.minimum(own_right_ref[:, wind], 0.0) * right
            left_high, left_low = halves(left)
            right_high, right_low = halves(right)
            rims = jnp.where(sub == 0, left_high, 0.0)
            rims = jnp.where(sub == 1, left_low, rims)
            rims = jnp.where(sub == 2, right_high, rims)
            rims = jnp.where(sub == 3, right_low, rims)
            rim = lax.dot_general(
                rims.astype(BF16), expand, (((0,), (0,)), ((), ())), preferred_element_type=F32
            ).reshape(8, 16, 128)
            levels = pl.ds(part * LEV + at * 8, 8)
            out_ref[levels] = part_ref[levels] + rim
        return carry

    lax.fori_loop(0, LEV // 8, chunk, 0, unroll=2)


def final_kernel(part_ref, heat_ref, side_ref, smoke_ref, above_ref, below_ref, prof_ref, out_ref):
    heat = heat_ref[...]
    row = sublanes_of(16)
    up = jnp.where(row == 0, above_ref[...], pltpu.roll(heat, 1, 0))
    down = jnp.where(row == 15, below_ref[...], pltpu.roll(heat, 15, 0))
    sources = (0.5 * (down - up), side_ref[...], smoke_ref[...])

    def one(at, carry):
        for spot in range(4):
            level = 4 * at + spot
            weight = prof_ref[pl.ds(level, 1), :]
            for part in range(3):
                before = part_ref[part * LEV + level]
                out_ref[part * LEV + level] = before + weight * sources[part]
        return carry

    lax.fori_loop(0, LEV // 4, one, 0)


def constants():
    spots = (np.arange(128) + 0.5) / 16 + 0.5
    weights = np.maximum(0.0, 1.0 - np.abs(spots[:, None] - np.arange(10)[None, :]))
    wcol = np.zeros((128, 128), np.float32)
    for row in range(10):
        wcol[12 * row : 12 * row + 10, :] = weights.T
        wcol[12 * row + 10, :] = weights[:, 0]
        wcol[12 * row + 11, :] = weights[:, 9]
    spread = np.zeros((256, 128), np.float32)
    for c in range(128):
        spread[c, c // 16] = 1.0
        spread[128 + c, 8 + c // 16] = 1.0
    words = np.zeros((8, 128), np.int32)
    tables = (spread_rates * 20, heat_yields * 10, smoke_yields * 10)
    rates, heats, smokes = (np.rint(table).astype(np.int32) for table in tables)
    words[:, :13] = rates + 32 * heats + 2048 * smokes
    levels = np.arange(LEV, dtype=np.float32)
    profile = np.exp(-levels * np.float32(8.0) / np.float32(LEV))
    profile = np.broadcast_to((np.float32(0.5) * profile)[:, None], (LEV, 128))
    return wcol, spread, words, np.ascontiguousarray(profile)


def neighbours(last, first, axes, count):
    ends = count - 1
    before = lax.ppermute(last, axes, [(i, i + 1) for i in range(ends)])
    after = lax.ppermute(first, axes, [(i + 1, i) for i in range(ends)])
    return before, after


def on_device(air, level_set, fuel, tile_list):
    wcol, spread, words, profile = constants()
    rows = ("grp", "gx")
    my_gx, my_gy = lax.axis_index("gx"), lax.axis_index("gy")
    myself = my_gx * N_GY + my_gy
    levels = air.reshape(3 * LEV, 16, 128)

    first, last, surface = pl.pallas_call(
        rows_kernel,
        out_shape=(shape(3 * LEV, 128), shape(3 * LEV, 128), shape(2, 16, 128)),
        in_specs=[ANY], out_specs=(VMEM,) * 3, scratch_shapes=[pltpu.SemaphoreType.DMA((4,))],
        compiler_params=room(60), name="rows", cost_estimate=cost(10**5, 10**6),
    )(levels)
    air_above, air_below = neighbours(last, first, rows, N_GRP * N_GX)

    listed = tile_list[0]
    slots = lax.dynamic_index_in_dim(listed, myself, 0, keepdims=False)
    right_at = jnp.where(my_gy < N_GY - 1, (myself + 1) * 32, -64)
    left_at = jnp.where(my_gy > 0, (myself - 1) * 32 + 15, -64)
    own_tile = jnp.where(listed // 32 == myself, ((listed % 32) ^ 7) - 32, 0)
    own_tile = jnp.where(listed >= 0, own_tile, 0)
    own_row = jnp.min(own_tile, axis=1) + 32
    rim_right = jnp.where(listed == right_at, 8, jnp.where(listed == right_at + 16, 16, 0))
    rim_left = jnp.where(listed == left_at, 9, jnp.where(listed == left_at + 16, 17, 0))
    picks = own_row + jnp.max(rim_right, axis=1) * 64 + jnp.max(rim_left, axis=1) * 4096
    picks = picks + 32 * 64 + 32 * 4096
    beside = jnp.array([15, 31], jnp.int32)
    wanted = jnp.concatenate(
        [
            myself * 32 + jnp.arange(32, dtype=jnp.int32),
            jnp.where(my_gy > 0, (myself - 1) * 32 + beside, -2),
            jnp.where(my_gy < N_GY - 1, (myself + 1) * 32 + beside - 15, -2),
        ]
    )
    found = listed[None, :, :] == wanted[:, None, None]
    order = lax.broadcasted_iota(jnp.int32, found.shape, 1)
    where = jnp.max(jnp.where(found, order, -1), axis=(1, 2))

    left, right = pl.pallas_call(
        sides_kernel, out_shape=(shape(1, 3 * LEV * 16), shape(1, 3 * LEV * 16)),
        in_specs=[VMEM], out_specs=(VMEM,) * 2, compiler_params=room(4),
        name="sides", cost_estimate=cost(10**8, 2 * 10**6),
    )(levels)
    table = pl.pallas_call(
        table_kernel, out_shape=shape(56, 256), in_specs=[VMEM], out_specs=VMEM,
        compiler_params=room(2), name="table", cost_estimate=cost(10**6, 10**6),
    )(surface)
    windows, token = pl.pallas_call(
        windows_kernel,
        out_shape=(shape(N_GX * N_GY, 1, 256), shape(8, 128)),
        in_specs=[SMEM] + [VMEM] * 4, out_specs=(VMEM,) * 2,
        scratch_shapes=[pltpu.VMEM((56, 256), F32)],
        compiler_params=room(2), name="windows", cost_estimate=cost(10**6, 10**6),
    )(picks, table, air_above, air_below, left)
    windows = lax.all_to_all(windows, ("gx", "gy"), split_axis=0, concat_axis=0, tiled=True)
    moved, token = pl.pallas_call(
        air_kernel, out_shape=(shape(3 * LEV, 16, 128), shape(8, 128)),
        in_specs=[VMEM] * 4, out_specs=(VMEM, VMEM),
        compiler_params=room(8), name="air", cost_estimate=cost(2 * 10**8, 4 * 10**6),
    )(levels, air_above, air_below, token)

    phases, message, edge_left, edge_right = pl.pallas_call(
        fire_kernel,
        out_shape=(
            shape(32, 128, 128), shape(N_GX * N_GY, 1, 256),
            shape(1, 3 * LEV * 16), shape(1, 3 * LEV * 16),
        ),
        in_specs=[SMEM, ANY, ANY] + [VMEM] * 7, out_specs=(ANY, VMEM, VMEM, VMEM),
        scratch_shapes=[
            pltpu.VMEM((32, 128, 128), F32),
            pltpu.VMEM((32, 128, 128), jnp.int32),
            pltpu.VMEM((32, 128, 128), F32),
            pltpu.VMEM((32, 48, 128), F32),
            pltpu.VMEM((32, 8, 256), F32),
            pltpu.VMEM((256, 128), F32),
            pltpu.VMEM((72, 1, 256), F32),
        ]
        + [pltpu.VMEM((256, 128), F32)] * 2
        + [pltpu.VMEM((128, 128), F32)] * 2
        + [pltpu.VMEM((128, 128), jnp.int32)] * 2
        + [pltpu.VMEM((128, 128), F32)] * 12
        + [pltpu.SemaphoreType.DMA((32,)), pltpu.SemaphoreType.DMA((6,))],
        compiler_params=room(60), name="fire", cost_estimate=cost(10**9, 8 * 10**6),
    )(
        slots, level_set, fuel, windows, jnp.asarray(words), jnp.asarray(wcol, BF16),
        jnp.asarray(spread, BF16), left, right, token,
    )
    fluxes = lax.all_to_all(message, ("gx", "gy"), split_axis=0, concat_axis=0, tiled=True)
    air_left, air_right = neighbours(edge_right, edge_left, "gy", N_GY)
    rimmed = pl.pallas_call(
        rims_kernel, out_shape=shape(3 * LEV, 16, 128), in_specs=[VMEM] * 5, out_specs=VMEM,
        compiler_params=room(8), name="rims", cost_estimate=cost(2 * 10**8, 4 * 10**6),
    )(moved, air_left, air_right, left, right)
    heat, side, smoke, heat_first, heat_last = pl.pallas_call(
        place_kernel,
        out_shape=(shape(16, 128), shape(16, 128), shape(16, 128), shape(1, 128), shape(1, 128)),
        in_specs=[SMEM, VMEM], out_specs=(VMEM,) * 5, compiler_params=room(4),
        name="place", cost_estimate=cost(10**6, 10**6),
    )(where, fluxes)
    heat_above, heat_below = neighbours(heat_last, heat_first, rows, N_GRP * N_GX)
    result = pl.pallas_call(
        final_kernel, out_shape=shape(3 * LEV, 16, 128), in_specs=[VMEM] * 7, out_specs=VMEM,
        compiler_params=room(8), name="final", cost_estimate=cost(10**6, 4 * 10**6),
    )(
        rimmed, heat, side, smoke, heat_above, heat_below, jnp.asarray(profile)
    )
    return (result.reshape(3, LEV, 16, 128), phases)


def solution(mesh):
    in_specs = (
        P(None, None, ("grp", "gx"), "gy"),
        P(("grp", "gx", "gy"), None, None),
        P(("grp", "gx", "gy"), None, None),
        P("grp", None, None),
    )
    out_specs = (P(None, None, ("grp", "gx"), "gy"), P(("grp", "gx", "gy"), None, None))
    return jax.shard_map(
        on_device, mesh=mesh, in_specs=in_specs, out_specs=out_specs, check_vma=False
    )
```

```python
import jax
import jax.numpy as jnp
import numpy as np
from jax import lax
from jax.experimental import pallas as pl
from jax.experimental.pallas import tpu as pltpu
from jax.sharding import PartitionSpec as P

SUB = 4
LEV = 80
N_GRP, N_GX, N_GY = 4, 8, 8
WIDE = 2

spread_rates = np.array(
    [0.3, 0.5, 0.9, 1.2, 0.6, 0.4, 0.7, 0.35, 0.25, 0.45, 0.55, 0.8, 1.0], np.float32
)
heat_yields = np.array(
    [1.0, 2.5, 4.0, 3.0, 1.5, 2.0, 5.0, 1.2, 0.8, 3.5, 2.2, 4.5, 2.8], np.float32
)
smoke_yields = np.array(
    [0.5, 1.5, 2.5, 1.0, 3.0, 0.8, 2.0, 1.8, 0.6, 2.6, 1.1, 3.4, 1.4], np.float32
)
courant = 0.1
viscosity = 0.1
buoyancy = 0.5
source_step = 0.5
fire_time = 0.1
wind_gain = 0.3

F32 = jnp.float32
BF16 = jnp.bfloat16
VMEM = pl.BlockSpec(memory_space=pltpu.VMEM)
SMEM = pl.BlockSpec(memory_space=pltpu.SMEM)
HBM = pl.BlockSpec(memory_space=pltpu.HBM)


def room(mib):
    return pltpu.CompilerParams(vmem_limit_bytes=mib * 1024 * 1024)


def shape(*dims, dtype=F32):
    return jax.ShapeDtypeStruct(dims, dtype)


def cost(flops, moved):
    return pl.CostEstimate(flops=flops, bytes_accessed=moved, transcendentals=0)


def lanes_of(rows=8):
    return lax.broadcasted_iota(jnp.int32, (rows, 128), 1)


def sublanes_of(rows=8):
    return lax.broadcasted_iota(jnp.int32, (rows, 128), 0)


def halves(value):
    high = value.astype(BF16).astype(F32)
    return high, value - high


def spread_line(line, row, low, high, rims):
    lane, sub = lanes_of(), sublanes_of()
    line = jnp.broadcast_to(line, (8, 128))
    here = (lane >= 12 * row) & (lane < 12 * row + 10)
    fanned = pltpu.roll(line, 0, 1, stride=8, stride_axis=0)
    first = pltpu.roll(fanned, (12 * row + 73) % 128, 1)
    second = pltpu.roll(fanned, (12 * row + 9) % 128, 1)
    low = jnp.where(here & ((sub < 7) | (lane > 12 * row)), first, low)
    high = jnp.where(here & ((sub > 0) | (lane < 12 * row + 9)), second, high)
    edges = pltpu.roll(line, (12 * row + 11) % 128, 1)
    rims = jnp.where((lane == 12 * row + 10 + sub) & (sub < 2), edges, rims)
    return low, high, rims


def table_kernel(list_ref, surf_ref, tile_ref, choice_ref):
    gx, gy = lax.axis_index("gx"), lax.axis_index("gy")
    me = gx * N_GY + gy
    left, right = gy > 0, gy < N_GY - 1
    k = lax.broadcasted_iota(jnp.int32, (1, 128), 1)
    codes = jnp.where(k < 32, me * 32 + (k ^ 7), -5)
    singles = (
        (40, right, me + 1, 0), (41, left, me - 1, 15), (48, right, me + 1, 16),
        (49, left, me - 1, 31),
    )
    for at, there, device, tile in singles:
        codes = jnp.where((k == at) & there, device * 32 + tile, codes)
    listed = list_ref[0]
    choice = jnp.zeros((64, 128), F32)
    for slot in range(32):
        entry = jnp.broadcast_to(listed[:, slot : slot + 1], (64, 128))
        choice = jnp.where(entry == codes, 1.0, choice)
    choice_ref[...] = choice.astype(BF16)
    tile_ref[...] = jnp.zeros(tile_ref.shape, F32)
    none = jnp.zeros((8, 128), F32)
    for comp in range(2):
        lanes = slice(128 * comp, 128 * comp + 128)
        field = surf_ref[comp] * wind_gain
        for half in range(2):
            found = [none, none, none]
            for row in range(10):
                at = 8 * half + row - 1
                if 0 <= at < 16:
                    found = spread_line(field[at : at + 1], row, *found)
            tile_ref[16 * half : 16 * half + 8, lanes] = found[0]
            tile_ref[16 * half + 8 : 16 * half + 16, lanes] = found[1]
            tile_ref[40 + 8 * half : 48 + 8 * half, lanes] = found[2]


def windows_kernel(
    table_ref, choice_ref, above_ref, below_ref, left_ref, out_ref, token_ref, tile_ref, made_ref
):
    token_ref[...] = jnp.zeros((8, 128), F32) + left_ref[0:1, 0:128] * 0.0
    tile_ref[...] = table_ref[...]
    for comp in range(2):
        lanes = slice(128 * comp, 128 * comp + 128)
        line_at = slice(LEV * comp, LEV * comp + 1)
        for half, (ref, row) in enumerate(((above_ref, 0), (below_ref, 9))):
            places = (
                slice(16 * half, 16 * half + 8),
                slice(16 * half + 8, 16 * half + 16),
                slice(40 + 8 * half, 48 + 8 * half),
            )
            old = [tile_ref[rows, lanes] for rows in places]
            fresh = spread_line(ref[line_at, :] * wind_gain, row, *old)
            for rows, value in zip(places, fresh):
                tile_ref[rows, lanes] = value
    choice = choice_ref[...]
    high, low = halves(tile_ref[...])
    made_ref[...] = jnp.dot(choice, high.astype(BF16), preferred_element_type=F32) + jnp.dot(
        choice, low.astype(BF16), preferred_element_type=F32
    )
    for fire in range(N_GX * N_GY):
        out_ref[fire] = made_ref[fire : fire + 1, :]


def fire_kernel(
    list_ref, phase_in, fuel_in, recv_ref, words_ref, wcol_ref, spread_ref,
    left_in, right_in, token_in, out_ref, msg_ref, left_out, right_out,
    phase_ref, fuel_ref, done_ref, column_ref, sums_ref, means_ref, flat_ref, line_ref, *rest,
):
    buffers, sem, sem_in = rest[:-2], rest[-2], rest[-1]
    sides = [buffers[at::WIDE] for at in range(WIDE)]
    left_out[...] = left_in[...]
    right_out[...] = right_in[...]
    loads = []
    for at, (low, high) in enumerate(((0, 2), (2, 8), (8, 32))):
        some = pl.ds(low, high - low)
        loads.append(
            (
                pltpu.make_async_copy(phase_in.at[some], phase_ref.at[some], sem_in.at[at]),
                pltpu.make_async_copy(fuel_in.at[some], fuel_ref.at[some], sem_in.at[3 + at]),
            )
        )
        for load in loads[-1]:
            load.start()
    lane24 = lanes_of(24)
    knot = sublanes_of(24)
    knot = (knot & 7) + (knot >> 3)
    unfold = (lane24 >= 12 * knot) & (lane24 < 12 * knot + 12)
    place = lax.broadcasted_iota(jnp.int32, (64, 256), 1)
    place = (place & 127) % 12
    me = lax.axis_index("gx") * N_GY + lax.axis_index("gy")
    entries = jnp.broadcast_to(list_ref[0, pl.ds(me, 1), :].astype(F32), (32, 32))
    across = lax.broadcasted_iota(jnp.int32, (32, 32), 1)
    along_slots = lax.broadcasted_iota(jnp.int32, (32, 32), 0)
    tiles = jnp.sum(jnp.where(across == along_slots, entries, 0.0), axis=1, keepdims=True)
    words = words_ref[...]
    row8, lane8 = sublanes_of(), lanes_of()

    tiles = jnp.broadcast_to(tiles, (32, 256)).astype(jnp.int32)
    target = lax.broadcasted_iota(jnp.int32, (32, 256), 1)
    owner, col = tiles >> 5, tiles & 15
    from_left = (owner - 1 == target - 64) & (col == 0) & ((owner & 7) > 0)
    from_right = (owner + 1 == target - 128) & (col == 15) & ((owner & 7) < 7)
    from_left = from_left & (target >= 64) & (target < 128)
    from_right = from_right & (target >= 128) & (target < 192)
    taken = ((owner == target) & (target < 64)) | from_left | from_right
    taken = jnp.where(taken & (tiles >= 0), 1.0, 0.0).astype(BF16)
    for device in range(N_GX * N_GY):
        flat_ref[device : device + 1, :] = recv_ref[device]
    sent = flat_ref[...]
    sent = jnp.concatenate(
        [
            jnp.where(place < 10, sent, 0.0), jnp.where(place == 10, sent, 0.0),
            jnp.where(place == 11, sent, 0.0), jnp.zeros((64, 256), F32),
        ],
        axis=0,
    )
    high, low = halves(sent)
    lines = jnp.dot(taken, high.astype(BF16), preferred_element_type=F32) + jnp.dot(
        taken, low.astype(BF16), preferred_element_type=F32
    )
    line_ref[0:32, :] = lines[:, 0:128]
    line_ref[32:64, :] = lines[:, 128:256]

    def columns(at, carry):
        parts = []
        for spot in range(8):
            for comp in range(2):
                line = line_ref[pl.ds(32 * comp + 8 * at + spot, 1), :]
                parts.append(jnp.where(unfold, jnp.broadcast_to(line, (24, 128)), 0.0))
        high, low = halves(jnp.concatenate(parts, axis=0))
        both = jnp.dot(high.astype(BF16), wcol_ref[...], preferred_element_type=F32) + jnp.dot(
            low.astype(BF16), wcol_ref[...], preferred_element_type=F32
        )
        for spot in range(8):
            column_ref[8 * at + spot] = both[48 * spot : 48 * spot + 48]
        return carry

    def result(slot):
        return pltpu.make_async_copy(done_ref.at[slot], out_ref.at[slot], sem.at[slot])

    def block(at):
        return slice(8 * at, 8 * at + 8)

    def store(target, at, values):
        field, behind, beyond = target
        turned = [pltpu.roll(value, 1, 1) for value in values]
        for k, value in enumerate(values):
            field[block(at + k), :] = value
        backs = [jnp.where(lane8 == 0, 0.0, x - y) for x, y in zip(values, turned)]
        aheads = [pltpu.roll(back, 127, 1) for back in backs]
        for k, (back, ahead) in enumerate(zip(backs, aheads)):
            behind[block(at + k), :] = back
            beyond[block(at + k), :] = ahead

    def begin(slot, side):
        gust, rate, word = side[:3]
        runs = [column_ref[slot, 8 * at : 8 * at + 8, :] for at in range(6)]
        steps = [runs[at + 1] - runs[at] for at in (0, 1, 3, 4)]
        for first in range(0, 16, 8):
            blocks = range(first, first + 8)
            places = [pl.ds(j, 8, stride=16) for j in blocks]
            fuels = [fuel_ref[slot, there, :] for there in places]
            packed = [
                jnp.take_along_axis(words, fuel, axis=1, mode="promise_in_bounds")
                for fuel in fuels
            ]
            store(side[3:6], first, [phase_ref[slot, there, :] for there in places])
            bases = [(x & 31).astype(F32) * np.float32(0.05 * fire_time) for x in packed]
            for j, x, base in zip(blocks, packed, bases):
                rate[block(j), :] = base
                word[block(j), :] = x
            low = first // 8
            for comp in range(2):
                run, step = runs[3 * comp + low], steps[2 * comp + low]
                parts = [np.float32((j + 0.5) / 16 + 0.5 - low) for j in blocks]
                winds = [run + part * step for part in parts]
                for j, wind, base in zip(blocks, winds, bases):
                    gust[block(16 * comp + j), :] = wind * base

    def advance(side, source, keep):
        gust, rate = side[:2]
        field, behind, beyond = source
        edge = field[block(0), :] - pltpu.roll(field[block(15), :], 1, 0)
        edge = jnp.where(row8 == 0, 0.0, edge)
        last = pltpu.roll(edge, 7, 0)
        for first in range(0, 16, 8):
            blocks = range(first, first + 8)
            fields = [field[block(j), :] for j in range(first, min(first + 9, 16))]
            aheads = [y - x for x, y in zip(fields, fields[1:])]
            if first == 8:
                aheads.append(last)
            backs = [edge] + aheads[:-1]
            edge = aheads[-1]
            side_backs = [behind[block(j), :] for j in blocks]
            side_aheads = [beyond[block(j), :] for j in blocks]
            a = [jnp.maximum(x, 0.0) for x in backs]
            b = [jnp.minimum(x, 0.0) for x in aheads]
            upwinds = [x * x + y * y for x, y in zip(a, b)]
            c = [jnp.maximum(x, 0.0) for x in side_backs]
            d = [jnp.minimum(x, 0.0) for x in side_aheads]
            upwinds = [u + (x * x + y * y) for u, x, y in zip(upwinds, c, d)]
            inverses = [lax.rsqrt(jnp.maximum(u, 1e-36)) for u in upwinds]
            row_slopes = [x + y for x, y in zip(backs, aheads)]
            col_slopes = [x + y for x, y in zip(side_backs, side_aheads)]
            squares = [x * x + y * y for x, y in zip(row_slopes, col_slopes)]
            factors = [lax.rsqrt(jnp.maximum(x, 4.0)) for x in squares]
            along = [
                gust[block(j), :] * x + gust[block(16 + j), :] * y
                for j, x, y in zip(blocks, row_slopes, col_slopes)
            ]
            roots = [u * x for u, x in zip(upwinds, inverses)]
            speeds = [
                rate[block(j), :] + jnp.maximum(x * f, 0.0)
                for j, x, f in zip(blocks, along, factors)
            ]
            keep(first, [x - v * r for x, v, r in zip(fields, speeds, roots)])

    def finish(slot, side):
        word = side[2]
        sums = [[], []]

        def keep(first, values):
            for k, value in enumerate(values):
                done_ref[slot, pl.ds(first + k, 8, stride=16), :] = value
            burning = [jnp.exp(value) for value in values]
            burning = [1.0 / (1.0 + value) for value in burning]
            packed = [word[block(first + k), :] for k in range(8)]
            heats = [((x >> 5) & 63).astype(F32) * y for x, y in zip(packed, burning)]
            smokes = [(x >> 11).astype(F32) * y for x, y in zip(packed, burning)]
            for total, terms in zip(sums, (heats, smokes)):
                while len(terms) > 1:
                    terms = [x + y for x, y in zip(terms[::2], terms[1::2])]
                total.append(terms[0])

        advance(side, side[6:9], keep)
        result(slot).start()
        sums_ref[slot, :, 0:128] = sums[0][0] + sums[0][1]
        sums_ref[slot, :, 128:256] = sums[1][0] + sums[1][1]

    def into(target):
        return lambda first, values: store(target, first, values)

    lax.fori_loop(0, 4, columns, 0)

    def several(at, carry):
        slot = WIDE * at
        for start, some in zip((0, 2 // WIDE, 8 // WIDE), loads):

            @pl.when(at == start)
            def _():
                for load in some:
                    load.wait()

        for spot, side in enumerate(sides):
            begin(slot + spot, side)
        for step in range(SUB - 1):
            for side in sides:
                pair_of = (side[3:6], side[6:9])
                advance(side, pair_of[step % 2], into(pair_of[1 - step % 2]))
        for spot, side in enumerate(sides):
            finish(slot + spot, side)
        return carry

    lax.fori_loop(0, 32 // WIDE, several, 0)
    high, low = halves(sums_ref[...].reshape(256, 256))
    spread = spread_ref[...]
    means_ref[...] = (
        jnp.dot(high.astype(BF16), spread, preferred_element_type=F32)
        + jnp.dot(low.astype(BF16), spread, preferred_element_type=F32)
    ) * np.float32(0.1 / 256)
    dense = means_ref[pl.ds(0, 32, stride=8), :]
    for row in range(1, 8):
        dense = dense + pltpu.roll(means_ref[pl.ds(row, 32, stride=8), :], 16 * row, 1)
    tile_row = list_ref[0, pl.ds(me, 1), :]
    owners = jnp.broadcast_to(tile_row >> 5, (64, 32))
    col = jnp.broadcast_to(tile_row & 15, (64, 32))
    live = jnp.broadcast_to(tile_row, (64, 32)) >= 0
    device = lax.broadcasted_iota(jnp.int32, (64, 32), 0)
    to_left = live & (owners - 1 == device) & (col == 0) & ((owners & 7) > 0)
    to_right = live & (owners + 1 == device) & (col == 15) & ((owners & 7) < 7)
    spot = lax.broadcasted_iota(jnp.int32, (32, 128), 1) & 15
    picked = []
    for chosen, kept in (
        (live & (owners == device), None), (to_left, spot == 0), (to_right, spot == 7),
    ):
        chosen = jnp.where(chosen, 1.0, 0.0).astype(BF16)
        high, low = halves(dense if kept is None else jnp.where(kept, dense, 0.0))
        picked.append(
            jnp.dot(chosen, high.astype(BF16), preferred_element_type=F32)
            + jnp.dot(chosen, low.astype(BF16), preferred_element_type=F32)
        )
    flat_ref[:, 0:128] = picked[0]
    flat_ref[:, 128:256] = picked[1] + picked[2]
    for device in range(N_GX * N_GY):
        msg_ref[device] = flat_ref[device : device + 1, :]

    def settle(slot, carry):
        result(slot).wait()
        return carry

    lax.fori_loop(0, 32, settle, 0)


def place_kernel(where_ref, flux_ref, heat_ref, side_ref, smoke_ref, first_ref, last_ref):
    lane, sub = lanes_of(), sublanes_of()
    key = lane // 8
    heat_from = sub * 16 + lane % 8
    zero = jnp.zeros((8, 128), F32)

    def tile(at, lanes):
        fire = where_ref[at]
        line = flux_ref[jnp.maximum(fire, 0), :, lanes]
        return jnp.where(fire >= 0, jnp.broadcast_to(line, (8, 128)), 0.0)

    def find(value, index):
        return jnp.take_along_axis(value, index, axis=1, mode="promise_in_bounds")

    own, beside = slice(0, 128), slice(128, 256)
    for half in range(2):
        rows = slice(8 * half, 8 * half + 8)
        heat = smoke = zero
        for col in range(16):
            value = tile(16 * half + col, own)
            heat = jnp.where(key == col, find(value, heat_from), heat)
            smoke = jnp.where(key == col, find(value, heat_from + 8), smoke)
        rim_left = find(tile(32 + half, beside), heat_from)
        rim_right = find(tile(34 + half, beside), heat_from)
        left = pltpu.roll(jnp.where(lane == 127, rim_left, heat), 1, 1)
        right = pltpu.roll(jnp.where(lane == 0, rim_right, heat), 127, 1)
        heat_ref[rows, :] = heat
        smoke_ref[rows, :] = smoke
        side_ref[rows, :] = 0.5 * (right - left)
        if half == 0:
            first_ref[...] = heat[0:1]
        else:
            last_ref[...] = heat[7:8]


def rows_kernel(air_ref, first_ref, last_ref, surf_ref, sem):
    copies = (
        pltpu.make_async_copy(air_ref.at[:, 0, :], first_ref, sem.at[0]),
        pltpu.make_async_copy(air_ref.at[:, 15, :], last_ref, sem.at[1]),
        pltpu.make_async_copy(air_ref.at[0], surf_ref.at[0], sem.at[2]),
        pltpu.make_async_copy(air_ref.at[LEV], surf_ref.at[1], sem.at[3]),
    )
    for copy in copies:
        copy.start()
    for copy in copies:
        copy.wait()


def sides_kernel(air_ref, left_ref, right_ref):
    lane, sub = lanes_of(), sublanes_of()
    pick = jnp.where((lane == 127 * sub) & (sub < 2), 1.0, 0.0)
    picked = lax.dot_general(
        pick, air_ref[...].reshape(3 * LEV * 16, 128), (((1,), (1,)), ((), ())),
        precision=lax.Precision.HIGHEST, preferred_element_type=F32,
    )
    left_ref[...] = picked[0:1]
    right_ref[...] = picked[1:2]


def air_kernel(air_ref, above_ref, below_ref, token_in, out_ref, token_ref):
    token_ref[...] = token_in[...]
    lane = lax.broadcasted_iota(jnp.int32, (8, 16, 128), 2)
    row = lax.broadcasted_iota(jnp.int32, (8, 16, 128), 1)

    def chunk(at, carry):
        levels = pl.ds(8 * at, 8)
        fields = []
        for part in range(3):
            mid = air_ref[part, levels]
            above = above_ref[part, levels, :][:, None, :]
            below = below_ref[part, levels, :][:, None, :]
            up = jnp.where(row == 0, above, pltpu.roll(mid, 1, 1))
            down = jnp.where(row == 15, below, pltpu.roll(mid, 15, 1))
            left = jnp.where(lane == 0, 0.0, pltpu.roll(mid, 1, 2))
            right = jnp.where(lane == 127, 0.0, pltpu.roll(mid, 127, 2))
            fields.append((mid, up, down, left, right))
        for part in range(2):
            mid, up, down, left, right = fields[part]
            around = (up + down) + (left + right)
            out_ref[part, levels] = mid + viscosity * (around - 4.0 * mid)
        u, v = fields[0][0], fields[1][0]
        mid, up, down, left, right = fields[2]
        upwind = (
            jnp.maximum(u, 0.0) * (mid - up)
            + jnp.minimum(u, 0.0) * (down - mid)
            + jnp.maximum(v, 0.0) * (mid - left)
            + jnp.minimum(v, 0.0) * (right - mid)
        )
        out_ref[2, levels] = mid - courant * upwind
        return carry

    lax.fori_loop(0, 2, chunk, 0)


def rims_kernel(part_ref, left_ref, right_ref, own_left_ref, own_right_ref, out_ref):
    sub, lane = sublanes_of(), lanes_of()
    expand = jnp.where((sub < 2) & (lane == 0), 1.0, 0.0) + jnp.where(
        (sub >= 2) & (sub < 4) & (lane == 127), 1.0, 0.0
    )
    expand = expand.astype(BF16)

    def chunk(at, carry):
        for part in range(3):
            spot = pl.ds(pl.multiple_of(part * (LEV * 16) + at * 128, 128), 128)
            left, right = left_ref[:, spot], right_ref[:, spot]
            if part < 2:
                left, right = viscosity * left, viscosity * right
            else:
                wind = pl.ds(pl.multiple_of(LEV * 16 + at * 128, 128), 128)
                left = courant * jnp.maximum(own_left_ref[:, wind], 0.0) * left
                right = -courant * jnp.minimum(own_right_ref[:, wind], 0.0) * right
            left_high, left_low = halves(left)
            right_high, right_low = halves(right)
            rims = jnp.where(sub == 0, left_high, 0.0)
            rims = jnp.where(sub == 1, left_low, rims)
            rims = jnp.where(sub == 2, right_high, rims)
            rims = jnp.where(sub == 3, right_low, rims)
            rim = lax.dot_general(
                rims.astype(BF16), expand, (((0,), (0,)), ((), ())), preferred_element_type=F32
            ).reshape(8, 16, 128)
            levels = pl.ds(part * LEV + at * 8, 8)
            out_ref[levels] = part_ref[levels] + rim
        return carry

    lax.fori_loop(0, LEV // 8, chunk, 0, unroll=2)


def final_kernel(
    part_ref, heat_ref, side_ref, smoke_ref, above_ref, below_ref, prof_ref,
    out_ref, made_ref, sem,
):
    heat = heat_ref[...]
    row = sublanes_of(16)
    up = jnp.where(row == 0, above_ref[...], pltpu.roll(heat, 1, 0))
    down = jnp.where(row == 15, below_ref[...], pltpu.roll(heat, 15, 0))
    sources = (0.5 * (down - up), side_ref[...], smoke_ref[...])
    copies = []
    for part in range(3):
        for half in range(2):
            first = part * LEV + half * (LEV // 2)

            def one(at, carry):
                for spot in range(8):
                    level = half * (LEV // 2) + 8 * at + spot
                    weight = prof_ref[pl.ds(level, 1), :]
                    before = part_ref[part * LEV + level]
                    made_ref[part * LEV + level] = before + weight * sources[part]
                return carry

            lax.fori_loop(0, LEV // 16, one, 0)
            some = pl.ds(first, LEV // 2)
            copies.append(
                pltpu.make_async_copy(
                    made_ref.at[some], out_ref.at[some], sem.at[2 * part + half]
                )
            )
            copies[-1].start()
    for copy in copies:
        copy.wait()


def constants():
    spots = (np.arange(128) + 0.5) / 16 + 0.5
    weights = np.maximum(0.0, 1.0 - np.abs(spots[:, None] - np.arange(10)[None, :]))
    wcol = np.zeros((128, 128), np.float32)
    for row in range(10):
        wcol[12 * row : 12 * row + 10, :] = weights.T
        wcol[12 * row + 10, :] = weights[:, 0]
        wcol[12 * row + 11, :] = weights[:, 9]
    spread = np.zeros((256, 128), np.float32)
    for c in range(128):
        spread[c, c // 16] = 1.0
        spread[128 + c, 8 + c // 16] = 1.0
    words = np.zeros((8, 128), np.int32)
    tables = (spread_rates * 20, heat_yields * 10, smoke_yields * 10)
    rates, heats, smokes = (np.rint(table).astype(np.int32) for table in tables)
    words[:, :13] = rates + 32 * heats + 2048 * smokes
    levels = np.arange(LEV, dtype=np.float32)
    profile = np.exp(-levels * np.float32(8.0) / np.float32(LEV))
    profile = np.broadcast_to((np.float32(0.5) * profile)[:, None], (LEV, 128))
    return wcol, spread, words, np.ascontiguousarray(profile)


def neighbours(last, first, axes, count):
    ends = count - 1
    before = lax.ppermute(last, axes, [(i, i + 1) for i in range(ends)])
    after = lax.ppermute(first, axes, [(i + 1, i) for i in range(ends)])
    return before, after


def on_device(air, level_set, fuel, tile_list):
    wcol, spread, words, profile = constants()
    rows = ("grp", "gx")
    my_gx, my_gy = lax.axis_index("gx"), lax.axis_index("gy")
    myself = my_gx * N_GY + my_gy
    levels = air.reshape(3 * LEV, 16, 128)

    first, last, surface = pl.pallas_call(
        rows_kernel,
        out_shape=(shape(3 * LEV, 128), shape(3 * LEV, 128), shape(2, 16, 128)),
        in_specs=[HBM], out_specs=(VMEM,) * 3, scratch_shapes=[pltpu.SemaphoreType.DMA((4,))],
        compiler_params=room(60), name="rows", cost_estimate=cost(10**5, 10**6),
    )(levels)
    air_above, air_below = neighbours(last, first, rows, N_GRP * N_GX)

    listed = tile_list[0]
    beside = jnp.array([15, 31], jnp.int32)
    wanted = jnp.concatenate(
        [
            myself * 32 + jnp.arange(32, dtype=jnp.int32),
            jnp.where(my_gy > 0, (myself - 1) * 32 + beside, -2),
            jnp.where(my_gy < N_GY - 1, (myself + 1) * 32 + beside - 15, -2),
        ]
    )
    found = listed[None, :, :] == wanted[:, None, None]
    order = lax.broadcasted_iota(jnp.int32, found.shape, 1)
    where = jnp.max(jnp.where(found, order, -1), axis=(1, 2))

    left, right = pl.pallas_call(
        sides_kernel, out_shape=(shape(1, 3 * LEV * 16), shape(1, 3 * LEV * 16)),
        in_specs=[VMEM], out_specs=(VMEM,) * 2, compiler_params=room(4),
        name="sides", cost_estimate=cost(10**8, 2 * 10**6),
    )(levels)
    table, choice = pl.pallas_call(
        table_kernel, out_shape=(shape(128, 256), shape(64, 128, dtype=BF16)),
        in_specs=[VMEM, VMEM], out_specs=(VMEM, VMEM),
        compiler_params=room(2), name="table", cost_estimate=cost(10**6, 10**6),
    )(tile_list, surface)
    windows, token = pl.pallas_call(
        windows_kernel,
        out_shape=(shape(N_GX * N_GY, 1, 256), shape(8, 128)),
        in_specs=[VMEM] * 5, out_specs=(VMEM,) * 2,
        scratch_shapes=[pltpu.VMEM((128, 256), F32), pltpu.VMEM((64, 256), F32)],
        compiler_params=room(2), name="windows", cost_estimate=cost(10**6, 10**6),
    )(table, choice, air_above, air_below, left)
    windows = lax.all_to_all(windows, ("gx", "gy"), split_axis=0, concat_axis=0, tiled=True)
    per_block = pl.BlockSpec((3, 16, 16, 128), lambda i: (0, i, 0, 0))
    per_rows = pl.BlockSpec((3, 16, 128), lambda i: (0, i, 0))
    fixed = pl.BlockSpec((8, 128), lambda i: (0, 0))
    moved, token = pl.pallas_call(
        air_kernel, out_shape=(shape(3, LEV, 16, 128), shape(8, 128)), grid=(LEV // 16,),
        in_specs=[per_block, per_rows, per_rows, fixed], out_specs=(per_block, fixed),
        compiler_params=room(60), name="air", cost_estimate=cost(2 * 10**8, 4 * 10**6),
    )(air, air_above.reshape(3, LEV, 128), air_below.reshape(3, LEV, 128), token)
    moved = moved.reshape(3 * LEV, 16, 128)

    phases, message, edge_left, edge_right = pl.pallas_call(
        fire_kernel,
        out_shape=(
            shape(32, 128, 128), shape(N_GX * N_GY, 1, 256),
            shape(1, 3 * LEV * 16), shape(1, 3 * LEV * 16),
        ),
        in_specs=[VMEM, HBM, HBM] + [VMEM] * 7, out_specs=(HBM, VMEM, VMEM, VMEM),
        scratch_shapes=[
            pltpu.VMEM((32, 128, 128), F32),
            pltpu.VMEM((32, 128, 128), jnp.int32),
            pltpu.VMEM((32, 128, 128), F32),
            pltpu.VMEM((32, 48, 128), F32),
            pltpu.VMEM((32, 8, 256), F32),
            pltpu.VMEM((256, 128), F32),
            pltpu.VMEM((64, 256), F32),
            pltpu.VMEM((64, 128), F32),
        ]
        + [pltpu.VMEM((256, 128), F32)] * WIDE
        + [pltpu.VMEM((128, 128), F32)] * WIDE
        + [pltpu.VMEM((128, 128), jnp.int32)] * WIDE
        + [pltpu.VMEM((128, 128), F32)] * (6 * WIDE)
        + [pltpu.SemaphoreType.DMA((32,)), pltpu.SemaphoreType.DMA((6,))],
        compiler_params=room(60), name="fire", cost_estimate=cost(10**9, 8 * 10**6),
    )(
        tile_list, level_set, fuel, windows, jnp.asarray(words), jnp.asarray(wcol, BF16),
        jnp.asarray(spread, BF16), left, right, token,
    )
    fluxes = lax.all_to_all(message, ("gx", "gy"), split_axis=0, concat_axis=0, tiled=True)
    air_left, air_right = neighbours(edge_right, edge_left, "gy", N_GY)
    rimmed = pl.pallas_call(
        rims_kernel, out_shape=shape(3 * LEV, 16, 128), in_specs=[VMEM] * 5, out_specs=VMEM,
        compiler_params=room(8), name="rims", cost_estimate=cost(2 * 10**8, 4 * 10**6),
    )(moved, air_left, air_right, left, right)
    heat, side, smoke, heat_first, heat_last = pl.pallas_call(
        place_kernel,
        out_shape=(shape(16, 128), shape(16, 128), shape(16, 128), shape(1, 128), shape(1, 128)),
        in_specs=[SMEM, VMEM], out_specs=(VMEM,) * 5, compiler_params=room(4),
        name="place", cost_estimate=cost(10**6, 10**6),
    )(where, fluxes)
    heat_above, heat_below = neighbours(heat_last, heat_first, rows, N_GRP * N_GX)
    result = pl.pallas_call(
        final_kernel, out_shape=shape(3 * LEV, 16, 128), in_specs=[VMEM] * 7, out_specs=HBM,
        scratch_shapes=[pltpu.VMEM((3 * LEV, 16, 128), F32), pltpu.SemaphoreType.DMA((6,))],
        compiler_params=room(8), name="final", cost_estimate=cost(10**6, 4 * 10**6),
    )(
        rimmed, heat, side, smoke, heat_above, heat_below, jnp.asarray(profile)
    )
    return (result.reshape(3, LEV, 16, 128), phases)


def solution(mesh):
    in_specs = (
        P(None, None, ("grp", "gx"), "gy"),
        P(("grp", "gx", "gy"), None, None),
        P(("grp", "gx", "gy"), None, None),
        P("grp", None, None),
    )
    out_specs = (P(None, None, ("grp", "gx"), "gy"), P(("grp", "gx", "gy"), None, None))
    return jax.shard_map(
        on_device, mesh=mesh, in_specs=in_specs, out_specs=out_specs, check_vma=False
    )
```

```python
import jax
import jax.numpy as jnp
import numpy as np
from jax import lax
from jax.experimental import pallas as pl
from jax.experimental.pallas import tpu as pltpu
from jax.sharding import PartitionSpec as P

SUB = 4
LEV = 80
N_GRP, N_GX, N_GY = 4, 8, 8
WIDE = 2

spread_rates = np.array(
    [0.3, 0.5, 0.9, 1.2, 0.6, 0.4, 0.7, 0.35, 0.25, 0.45, 0.55, 0.8, 1.0], np.float32
)
heat_yields = np.array(
    [1.0, 2.5, 4.0, 3.0, 1.5, 2.0, 5.0, 1.2, 0.8, 3.5, 2.2, 4.5, 2.8], np.float32
)
smoke_yields = np.array(
    [0.5, 1.5, 2.5, 1.0, 3.0, 0.8, 2.0, 1.8, 0.6, 2.6, 1.1, 3.4, 1.4], np.float32
)
courant = 0.1
viscosity = 0.1
buoyancy = 0.5
source_step = 0.5
fire_time = 0.1
wind_gain = 0.3

F32 = jnp.float32
BF16 = jnp.bfloat16
VMEM = pl.BlockSpec(memory_space=pltpu.VMEM)
SMEM = pl.BlockSpec(memory_space=pltpu.SMEM)
HBM = pl.BlockSpec(memory_space=pltpu.HBM)


def room(mib):
    return pltpu.CompilerParams(vmem_limit_bytes=mib * 1024 * 1024)


def shape(*dims, dtype=F32):
    return jax.ShapeDtypeStruct(dims, dtype)


def cost(flops, moved):
    return pl.CostEstimate(flops=flops, bytes_accessed=moved, transcendentals=0)


def lanes_of(rows=8):
    return lax.broadcasted_iota(jnp.int32, (rows, 128), 1)


def sublanes_of(rows=8):
    return lax.broadcasted_iota(jnp.int32, (rows, 128), 0)


def halves(value):
    high = value.astype(BF16).astype(F32)
    return high, value - high


def spread_line(line, row, low, high, rims):
    lane, sub = lanes_of(), sublanes_of()
    line = jnp.broadcast_to(line, (8, 128))
    here = (lane >= 12 * row) & (lane < 12 * row + 10)
    fanned = pltpu.roll(line, 0, 1, stride=8, stride_axis=0)
    first = pltpu.roll(fanned, (12 * row + 73) % 128, 1)
    second = pltpu.roll(fanned, (12 * row + 9) % 128, 1)
    low = jnp.where(here & ((sub < 7) | (lane > 12 * row)), first, low)
    high = jnp.where(here & ((sub > 0) | (lane < 12 * row + 9)), second, high)
    edges = pltpu.roll(line, (12 * row + 11) % 128, 1)
    rims = jnp.where((lane == 12 * row + 10 + sub) & (sub < 2), edges, rims)
    return low, high, rims


def table_kernel(list_ref, air_ref, tile_ref, choice_ref, where_ref, surf_ref, sem):
    copies = [
        pltpu.make_async_copy(air_ref.at[LEV * comp], surf_ref.at[comp], sem.at[comp])
        for comp in range(2)
    ]
    for copy in copies:
        copy.start()
    gx, gy = lax.axis_index("gx"), lax.axis_index("gy")
    me = gx * N_GY + gy
    left, right = gy > 0, gy < N_GY - 1
    k = lax.broadcasted_iota(jnp.int32, (1, 128), 1)
    codes = jnp.where(k < 32, me * 32 + (k ^ 7), -5)
    singles = (
        (40, right, me + 1, 0), (41, left, me - 1, 15), (48, right, me + 1, 16),
        (49, left, me - 1, 31),
    )
    for at, there, device, tile in singles:
        codes = jnp.where((k == at) & there, device * 32 + tile, codes)
    listed = list_ref[0]
    choice = jnp.zeros((64, 128), F32)
    for slot in range(32):
        entry = jnp.broadcast_to(listed[:, slot : slot + 1], (64, 128))
        choice = jnp.where(entry == codes, 1.0, choice)
    choice_ref[...] = choice.astype(BF16)
    device = sublanes_of(64).astype(F32) + 1.0
    holder = jnp.sum(choice * device, axis=0, keepdims=True) - 1.0
    where_ref[...] = holder.astype(jnp.int32)
    tile_ref[...] = jnp.zeros(tile_ref.shape, F32)
    for copy in copies:
        copy.wait()
    none = jnp.zeros((8, 128), F32)
    for comp in range(2):
        lanes = slice(128 * comp, 128 * comp + 128)
        field = surf_ref[comp] * wind_gain
        for half in range(2):
            found = [none, none, none]
            for row in range(10):
                at = 8 * half + row - 1
                if 0 <= at < 16:
                    found = spread_line(field[at : at + 1], row, *found)
            tile_ref[16 * half : 16 * half + 8, lanes] = found[0]
            tile_ref[16 * half + 8 : 16 * half + 16, lanes] = found[1]
            tile_ref[40 + 8 * half : 48 + 8 * half, lanes] = found[2]


def windows_kernel(
    table_ref, choice_ref, above_ref, below_ref, left_ref, out_ref, token_ref, tile_ref, made_ref
):
    token_ref[...] = jnp.zeros((8, 128), F32) + left_ref[0:1, 0:128] * 0.0
    tile_ref[...] = table_ref[...]
    for comp in range(2):
        lanes = slice(128 * comp, 128 * comp + 128)
        line_at = slice(LEV * comp, LEV * comp + 1)
        for half, (ref, row) in enumerate(((above_ref, 0), (below_ref, 9))):
            places = (
                slice(16 * half, 16 * half + 8),
                slice(16 * half + 8, 16 * half + 16),
                slice(40 + 8 * half, 48 + 8 * half),
            )
            old = [tile_ref[rows, lanes] for rows in places]
            fresh = spread_line(ref[line_at, :] * wind_gain, row, *old)
            for rows, value in zip(places, fresh):
                tile_ref[rows, lanes] = value
    choice = choice_ref[...]
    high, low = halves(tile_ref[...])
    made_ref[...] = jnp.dot(choice, high.astype(BF16), preferred_element_type=F32) + jnp.dot(
        choice, low.astype(BF16), preferred_element_type=F32
    )
    for fire in range(N_GX * N_GY):
        out_ref[fire] = made_ref[fire : fire + 1, :]


def fire_kernel(
    list_ref, phase_in, fuel_in, recv_ref, words_ref, wcol_ref, spread_ref,
    left_in, right_in, token_in, out_ref, msg_ref, left_out, right_out,
    phase_ref, fuel_ref, done_ref, column_ref, sums_ref, means_ref, flat_ref, line_ref, *rest,
):
    buffers, sem, sem_in = rest[:-2], rest[-2], rest[-1]
    sides = [buffers[at::WIDE] for at in range(WIDE)]
    left_out[...] = left_in[...]
    right_out[...] = right_in[...]
    loads = []
    for at, (low, high) in enumerate(((0, 2), (2, 8), (8, 32))):
        some = pl.ds(low, high - low)
        loads.append(
            (
                pltpu.make_async_copy(phase_in.at[some], phase_ref.at[some], sem_in.at[at]),
                pltpu.make_async_copy(fuel_in.at[some], fuel_ref.at[some], sem_in.at[3 + at]),
            )
        )
        for load in loads[-1]:
            load.start()
    lane24 = lanes_of(24)
    knot = sublanes_of(24)
    knot = (knot & 7) + (knot >> 3)
    unfold = (lane24 >= 12 * knot) & (lane24 < 12 * knot + 12)
    place = lax.broadcasted_iota(jnp.int32, (64, 256), 1)
    place = (place & 127) % 12
    me = lax.axis_index("gx") * N_GY + lax.axis_index("gy")
    entries = jnp.broadcast_to(list_ref[0, pl.ds(me, 1), :].astype(F32), (32, 32))
    across = lax.broadcasted_iota(jnp.int32, (32, 32), 1)
    along_slots = lax.broadcasted_iota(jnp.int32, (32, 32), 0)
    tiles = jnp.sum(jnp.where(across == along_slots, entries, 0.0), axis=1, keepdims=True)
    words = words_ref[...]
    row8, lane8 = sublanes_of(), lanes_of()

    tiles = jnp.broadcast_to(tiles, (32, 256)).astype(jnp.int32)
    target = lax.broadcasted_iota(jnp.int32, (32, 256), 1)
    owner, col = tiles >> 5, tiles & 15
    from_left = (owner - 1 == target - 64) & (col == 0) & ((owner & 7) > 0)
    from_right = (owner + 1 == target - 128) & (col == 15) & ((owner & 7) < 7)
    from_left = from_left & (target >= 64) & (target < 128)
    from_right = from_right & (target >= 128) & (target < 192)
    taken = ((owner == target) & (target < 64)) | from_left | from_right
    taken = jnp.where(taken & (tiles >= 0), 1.0, 0.0).astype(BF16)
    for device in range(N_GX * N_GY):
        flat_ref[device : device + 1, :] = recv_ref[device]
    sent = flat_ref[...]
    sent = jnp.concatenate(
        [
            jnp.where(place < 10, sent, 0.0), jnp.where(place == 10, sent, 0.0),
            jnp.where(place == 11, sent, 0.0), jnp.zeros((64, 256), F32),
        ],
        axis=0,
    )
    high, low = halves(sent)
    lines = jnp.dot(taken, high.astype(BF16), preferred_element_type=F32) + jnp.dot(
        taken, low.astype(BF16), preferred_element_type=F32
    )
    line_ref[0:32, :] = lines[:, 0:128]
    line_ref[32:64, :] = lines[:, 128:256]

    def columns(at, carry):
        parts = []
        for spot in range(8):
            for comp in range(2):
                line = line_ref[pl.ds(32 * comp + 8 * at + spot, 1), :]
                parts.append(jnp.where(unfold, jnp.broadcast_to(line, (24, 128)), 0.0))
        high, low = halves(jnp.concatenate(parts, axis=0))
        both = jnp.dot(high.astype(BF16), wcol_ref[...], preferred_element_type=F32) + jnp.dot(
            low.astype(BF16), wcol_ref[...], preferred_element_type=F32
        )
        for spot in range(8):
            column_ref[8 * at + spot] = both[48 * spot : 48 * spot + 48]
        return carry

    def result(slot):
        return pltpu.make_async_copy(done_ref.at[slot], out_ref.at[slot], sem.at[slot])

    def block(at):
        return slice(8 * at, 8 * at + 8)

    def store(target, at, values):
        field, behind, beyond = target
        turned = [pltpu.roll(value, 1, 1) for value in values]
        for k, value in enumerate(values):
            field[block(at + k), :] = value
        backs = [jnp.where(lane8 == 0, 0.0, x - y) for x, y in zip(values, turned)]
        aheads = [pltpu.roll(back, 127, 1) for back in backs]
        for k, (back, ahead) in enumerate(zip(backs, aheads)):
            behind[block(at + k), :] = back
            beyond[block(at + k), :] = ahead

    def begin(slot, side):
        gust, rate, word = side[:3]
        runs = [column_ref[slot, 8 * at : 8 * at + 8, :] for at in range(6)]
        steps = [runs[at + 1] - runs[at] for at in (0, 1, 3, 4)]
        for first in range(0, 16, 8):
            blocks = range(first, first + 8)
            places = [pl.ds(j, 8, stride=16) for j in blocks]
            fuels = [fuel_ref[slot, there, :] for there in places]
            packed = [
                jnp.take_along_axis(words, fuel, axis=1, mode="promise_in_bounds")
                for fuel in fuels
            ]
            store(side[3:6], first, [phase_ref[slot, there, :] for there in places])
            bases = [(x & 31).astype(F32) * np.float32(0.05 * fire_time) for x in packed]
            for j, x, base in zip(blocks, packed, bases):
                rate[block(j), :] = base
                word[block(j), :] = x
            low = first // 8
            for comp in range(2):
                run, step = runs[3 * comp + low], steps[2 * comp + low]
                parts = [np.float32((j + 0.5) / 16 + 0.5 - low) for j in blocks]
                winds = [run + part * step for part in parts]
                for j, wind, base in zip(blocks, winds, bases):
                    gust[block(16 * comp + j), :] = wind * base

    def advance(side, source, keep):
        gust, rate = side[:2]
        field, behind, beyond = source
        edge = field[block(0), :] - pltpu.roll(field[block(15), :], 1, 0)
        edge = jnp.where(row8 == 0, 0.0, edge)
        last = pltpu.roll(edge, 7, 0)
        for first in range(0, 16, 4):
            blocks = range(first, first + 4)
            fields = [field[block(j), :] for j in range(first, min(first + 4 + 1, 16))]
            aheads = [y - x for x, y in zip(fields, fields[1:])]
            if first == 16 - 4:
                aheads.append(last)
            backs = [edge] + aheads[:-1]
            edge = aheads[-1]
            side_backs = [behind[block(j), :] for j in blocks]
            side_aheads = [beyond[block(j), :] for j in blocks]
            a = [jnp.maximum(x, 0.0) for x in backs]
            b = [jnp.minimum(x, 0.0) for x in aheads]
            upwinds = [x * x + y * y for x, y in zip(a, b)]
            c = [jnp.maximum(x, 0.0) for x in side_backs]
            d = [jnp.minimum(x, 0.0) for x in side_aheads]
            upwinds = [u + (x * x + y * y) for u, x, y in zip(upwinds, c, d)]
            inverses = [lax.rsqrt(jnp.maximum(u, 1e-36)) for u in upwinds]
            row_slopes = [x + y for x, y in zip(backs, aheads)]
            col_slopes = [x + y for x, y in zip(side_backs, side_aheads)]
            squares = [x * x + y * y for x, y in zip(row_slopes, col_slopes)]
            factors = [lax.rsqrt(jnp.maximum(x, 4.0)) for x in squares]
            along = [
                gust[block(j), :] * x + gust[block(16 + j), :] * y
                for j, x, y in zip(blocks, row_slopes, col_slopes)
            ]
            roots = [u * x for u, x in zip(upwinds, inverses)]
            speeds = [
                rate[block(j), :] + jnp.maximum(x * f, 0.0)
                for j, x, f in zip(blocks, along, factors)
            ]
            keep(first, [x - v * r for x, v, r in zip(fields, speeds, roots)])

    def finish(slot, side):
        word = side[2]
        sums = [[], []]

        def keep(first, values):
            for k, value in enumerate(values):
                done_ref[slot, pl.ds(first + k, 8, stride=16), :] = value
            burning = [jnp.exp(value) for value in values]
            burning = [1.0 / (1.0 + value) for value in burning]
            packed = [word[block(first + k), :] for k in range(len(values))]
            heats = [((x >> 5) & 63).astype(F32) * y for x, y in zip(packed, burning)]
            smokes = [(x >> 11).astype(F32) * y for x, y in zip(packed, burning)]
            for total, terms in zip(sums, (heats, smokes)):
                while len(terms) > 1:
                    terms = [x + y for x, y in zip(terms[::2], terms[1::2])]
                total.append(terms[0])

        advance(side, side[6:9], keep)
        result(slot).start()
        sums_ref[slot, :, 0:128] = sum(sums[0])
        sums_ref[slot, :, 128:256] = sum(sums[1])

    def into(target):
        return lambda first, values: store(target, first, values)

    lax.fori_loop(0, 4, columns, 0)

    def several(at, carry):
        slot = WIDE * at
        for start, some in zip((0, 2 // WIDE, 8 // WIDE), loads):

            @pl.when(at == start)
            def _():
                for load in some:
                    load.wait()

        for spot, side in enumerate(sides):
            begin(slot + spot, side)
        for step in range(SUB - 1):
            for side in sides:
                pair_of = (side[3:6], side[6:9])
                advance(side, pair_of[step % 2], into(pair_of[1 - step % 2]))
        for spot, side in enumerate(sides):
            finish(slot + spot, side)
        return carry

    lax.fori_loop(0, 32 // WIDE, several, 0)
    high, low = halves(sums_ref[...].reshape(256, 256))
    spread = spread_ref[...]
    means_ref[...] = (
        jnp.dot(high.astype(BF16), spread, preferred_element_type=F32)
        + jnp.dot(low.astype(BF16), spread, preferred_element_type=F32)
    ) * np.float32(0.1 / 256)
    dense = means_ref[pl.ds(0, 32, stride=8), :]
    for row in range(1, 8):
        dense = dense + pltpu.roll(means_ref[pl.ds(row, 32, stride=8), :], 16 * row, 1)
    tile_row = list_ref[0, pl.ds(me, 1), :]
    owners = jnp.broadcast_to(tile_row >> 5, (64, 32))
    col = jnp.broadcast_to(tile_row & 15, (64, 32))
    live = jnp.broadcast_to(tile_row, (64, 32)) >= 0
    device = lax.broadcasted_iota(jnp.int32, (64, 32), 0)
    to_left = live & (owners - 1 == device) & (col == 0) & ((owners & 7) > 0)
    to_right = live & (owners + 1 == device) & (col == 15) & ((owners & 7) < 7)
    spot = lax.broadcasted_iota(jnp.int32, (32, 128), 1) & 15
    picked = []
    for chosen, kept in (
        (live & (owners == device), None), (to_left, spot == 0), (to_right, spot == 7),
    ):
        chosen = jnp.where(chosen, 1.0, 0.0).astype(BF16)
        high, low = halves(dense if kept is None else jnp.where(kept, dense, 0.0))
        picked.append(
            jnp.dot(chosen, high.astype(BF16), preferred_element_type=F32)
            + jnp.dot(chosen, low.astype(BF16), preferred_element_type=F32)
        )
    flat_ref[:, 0:128] = picked[0]
    flat_ref[:, 128:256] = picked[1] + picked[2]
    for device in range(N_GX * N_GY):
        msg_ref[device] = flat_ref[device : device + 1, :]

    def settle(slot, carry):
        result(slot).wait()
        return carry

    lax.fori_loop(0, 32, settle, 0)


def place_kernel(where_ref, flux_ref, heat_ref, side_ref, smoke_ref, first_ref, last_ref):
    lane, sub = lanes_of(), sublanes_of()
    key = lane // 8
    heat_from = sub * 16 + lane % 8
    zero = jnp.zeros((8, 128), F32)

    def tile(at, lanes):
        fire = where_ref[0, at]
        line = flux_ref[jnp.maximum(fire, 0), :, lanes]
        return jnp.where(fire >= 0, jnp.broadcast_to(line, (8, 128)), 0.0)

    def find(value, index):
        return jnp.take_along_axis(value, index, axis=1, mode="promise_in_bounds")

    own, beside = slice(0, 128), slice(128, 256)
    for half in range(2):
        rows = slice(8 * half, 8 * half + 8)
        heat = smoke = zero
        for col in range(16):
            value = tile(16 * half + (col ^ 7), own)
            heat = jnp.where(key == col, find(value, heat_from), heat)
            smoke = jnp.where(key == col, find(value, heat_from + 8), smoke)
        rim_left = find(tile(41 + 8 * half, beside), heat_from)
        rim_right = find(tile(40 + 8 * half, beside), heat_from)
        left = pltpu.roll(jnp.where(lane == 127, rim_left, heat), 1, 1)
        right = pltpu.roll(jnp.where(lane == 0, rim_right, heat), 127, 1)
        heat_ref[rows, :] = heat
        smoke_ref[rows, :] = smoke
        side_ref[rows, :] = 0.5 * (right - left)
        if half == 0:
            first_ref[...] = heat[0:1]
        else:
            last_ref[...] = heat[7:8]


def rows_kernel(air_ref, first_ref, last_ref, sem):
    copies = (
        pltpu.make_async_copy(air_ref.at[:, 0, :], first_ref, sem.at[0]),
        pltpu.make_async_copy(air_ref.at[:, 15, :], last_ref, sem.at[1]),
    )
    for copy in copies:
        copy.start()
    for copy in copies:
        copy.wait()


def sides_kernel(air_ref, left_ref, right_ref):
    lane, sub = lanes_of(), sublanes_of()
    pick = jnp.where((lane == 127 * sub) & (sub < 2), 1.0, 0.0)
    columns = air_ref[...].reshape(3 * LEV * 16, 128)
    picked = 0.0
    for part in halves(columns):
        picked += lax.dot_general(
            pick.astype(BF16), part.astype(BF16), (((1,), (1,)), ((), ())),
            preferred_element_type=F32,
        )
    left_ref[...] = picked[0:1]
    right_ref[...] = picked[1:2]


def air_kernel(
    air_ref, above_ref, below_ref, left_ref, right_ref, token_in, out_ref, token_ref
):
    token_ref[...] = token_in[...]
    for side, ref in enumerate((left_ref, right_ref)):
        for at in range(30):
            level, line = 3 * LEV + 2 * side + at // 16, at % 16
            out_ref[level, line : line + 1, :] = ref[:, 128 * at : 128 * at + 128]
    lane = lax.broadcasted_iota(jnp.int32, (8, 16, 128), 2)
    row = lax.broadcasted_iota(jnp.int32, (8, 16, 128), 1)

    def chunk(at, carry):
        fields = []
        for part in range(3):
            start = part * LEV + at * 8
            mid = air_ref[pl.ds(start, 8)]
            above = above_ref[pl.ds(start, 8), :][:, None, :]
            below = below_ref[pl.ds(start, 8), :][:, None, :]
            up = jnp.where(row == 0, above, pltpu.roll(mid, 1, 1))
            down = jnp.where(row == 15, below, pltpu.roll(mid, 15, 1))
            left = jnp.where(lane == 0, 0.0, pltpu.roll(mid, 1, 2))
            right = jnp.where(lane == 127, 0.0, pltpu.roll(mid, 127, 2))
            fields.append((mid, up, down, left, right))
        for part in range(2):
            mid, up, down, left, right = fields[part]
            around = (up + down) + (left + right)
            out_ref[pl.ds(part * LEV + at * 8, 8)] = mid + viscosity * (around - 4.0 * mid)
        u, v = fields[0][0], fields[1][0]
        mid, up, down, left, right = fields[2]
        upwind = (
            jnp.maximum(u, 0.0) * (mid - up)
            + jnp.minimum(u, 0.0) * (down - mid)
            + jnp.maximum(v, 0.0) * (mid - left)
            + jnp.minimum(v, 0.0) * (right - mid)
        )
        out_ref[pl.ds(2 * LEV + at * 8, 8)] = mid - courant * upwind
        return carry

    lax.fori_loop(0, LEV // 8, chunk, 0)


def rims_kernel(part_ref, left_ref, right_ref, out_ref):
    sub, lane = sublanes_of(), lanes_of()
    expand = jnp.where((sub < 2) & (lane == 0), 1.0, 0.0) + jnp.where(
        (sub >= 2) & (sub < 4) & (lane == 127), 1.0, 0.0
    )
    expand = expand.astype(BF16)

    def chunk(at, carry):
        for part in range(3):
            spot = pl.ds(pl.multiple_of(part * (LEV * 16) + at * 128, 128), 128)
            left, right = left_ref[:, spot], right_ref[:, spot]
            if part < 2:
                left, right = viscosity * left, viscosity * right
            else:
                line = LEV // 8 + at
                level, line = 3 * LEV + (line >> 4), pl.ds(line & 15, 1)
                left = courant * jnp.maximum(part_ref[level, line, :], 0.0) * left
                right = -courant * jnp.minimum(part_ref[level + 2, line, :], 0.0) * right
            left_high, left_low = halves(left)
            right_high, right_low = halves(right)
            rims = jnp.where(sub == 0, left_high, 0.0)
            rims = jnp.where(sub == 1, left_low, rims)
            rims = jnp.where(sub == 2, right_high, rims)
            rims = jnp.where(sub == 3, right_low, rims)
            rim = lax.dot_general(
                rims.astype(BF16), expand, (((0,), (0,)), ((), ())), preferred_element_type=F32
            ).reshape(8, 16, 128)
            levels = pl.ds(part * LEV + at * 8, 8)
            out_ref[levels] = part_ref[levels] + rim
        return carry

    lax.fori_loop(0, LEV // 8, chunk, 0, unroll=2)


def final_kernel(
    part_ref, heat_ref, side_ref, smoke_ref, above_ref, below_ref, prof_ref,
    out_ref, made_ref, sem,
):
    heat = heat_ref[...]
    row = sublanes_of(16)
    up = jnp.where(row == 0, above_ref[...], pltpu.roll(heat, 1, 0))
    down = jnp.where(row == 15, below_ref[...], pltpu.roll(heat, 15, 0))
    sources = (0.5 * (down - up), side_ref[...], smoke_ref[...])
    copies = []
    for part in range(3):
        for half in range(2):
            first = part * LEV + half * (LEV // 2)

            def one(at, carry):
                for spot in range(8):
                    level = half * (LEV // 2) + 8 * at + spot
                    weight = prof_ref[pl.ds(level, 1), :]
                    before = part_ref[part * LEV + level]
                    made_ref[part * LEV + level] = before + weight * sources[part]
                return carry

            lax.fori_loop(0, LEV // 16, one, 0)
            some = pl.ds(first, LEV // 2)
            copies.append(
                pltpu.make_async_copy(
                    made_ref.at[some], out_ref.at[some], sem.at[2 * part + half]
                )
            )
            copies[-1].start()
    for copy in copies:
        copy.wait()


def constants():
    spots = (np.arange(128) + 0.5) / 16 + 0.5
    weights = np.maximum(0.0, 1.0 - np.abs(spots[:, None] - np.arange(10)[None, :]))
    wcol = np.zeros((128, 128), np.float32)
    for row in range(10):
        wcol[12 * row : 12 * row + 10, :] = weights.T
        wcol[12 * row + 10, :] = weights[:, 0]
        wcol[12 * row + 11, :] = weights[:, 9]
    spread = np.zeros((256, 128), np.float32)
    for c in range(128):
        spread[c, c // 16] = 1.0
        spread[128 + c, 8 + c // 16] = 1.0
    words = np.zeros((8, 128), np.int32)
    tables = (spread_rates * 20, heat_yields * 10, smoke_yields * 10)
    rates, heats, smokes = (np.rint(table).astype(np.int32) for table in tables)
    words[:, :13] = rates + 32 * heats + 2048 * smokes
    levels = np.arange(LEV, dtype=np.float32)
    profile = np.exp(-levels * np.float32(8.0) / np.float32(LEV))
    profile = np.broadcast_to((np.float32(0.5) * profile)[:, None], (LEV, 128))
    return wcol, spread, words, np.ascontiguousarray(profile)


def neighbours(last, first, axes, count):
    ends = count - 1
    before = lax.ppermute(last, axes, [(i, i + 1) for i in range(ends)])
    after = lax.ppermute(first, axes, [(i + 1, i) for i in range(ends)])
    return before, after


def on_device(air, level_set, fuel, tile_list):
    wcol, spread, words, profile = constants()
    rows = ("grp", "gx")
    levels = air.reshape(3 * LEV, 16, 128)

    first, last = pl.pallas_call(
        rows_kernel,
        out_shape=(shape(3 * LEV, 128), shape(3 * LEV, 128)),
        in_specs=[HBM], out_specs=(VMEM,) * 2, scratch_shapes=[pltpu.SemaphoreType.DMA((2,))],
        compiler_params=room(60), name="rows", cost_estimate=cost(10**5, 10**6),
    )(levels)
    air_above, air_below = neighbours(last, first, rows, N_GRP * N_GX)

    left, right = pl.pallas_call(
        sides_kernel, out_shape=(shape(1, 3 * LEV * 16), shape(1, 3 * LEV * 16)),
        in_specs=[VMEM], out_specs=(VMEM,) * 2, compiler_params=room(4),
        name="sides", cost_estimate=cost(10**8, 2 * 10**6),
    )(levels)
    table, choice, where = pl.pallas_call(
        table_kernel, out_shape=(
            shape(128, 256), shape(64, 128, dtype=BF16), shape(1, 128, dtype=jnp.int32)
        ),
        in_specs=[VMEM, HBM], out_specs=(VMEM,) * 3,
        scratch_shapes=[pltpu.VMEM((2, 16, 128), F32), pltpu.SemaphoreType.DMA((2,))],
        compiler_params=room(2), name="table", cost_estimate=cost(10**6, 10**6),
    )(tile_list, levels)
    windows, token = pl.pallas_call(
        windows_kernel,
        out_shape=(shape(N_GX * N_GY, 1, 256), shape(8, 128)),
        in_specs=[VMEM] * 5, out_specs=(VMEM,) * 2,
        scratch_shapes=[pltpu.VMEM((128, 256), F32), pltpu.VMEM((64, 256), F32)],
        compiler_params=room(2), name="windows", cost_estimate=cost(10**6, 10**6),
    )(table, choice, air_above, air_below, left)
    windows = lax.all_to_all(windows, ("gx", "gy"), split_axis=0, concat_axis=0, tiled=True)
    moved, token = pl.pallas_call(
        air_kernel, out_shape=(shape(3 * LEV + 4, 16, 128), shape(8, 128)),
        in_specs=[VMEM] * 6, out_specs=(VMEM, VMEM),
        compiler_params=room(8), name="air", cost_estimate=cost(2 * 10**8, 4 * 10**6),
    )(levels, air_above, air_below, left, right, token)

    phases, message, edge_left, edge_right = pl.pallas_call(
        fire_kernel,
        out_shape=(
            shape(32, 128, 128), shape(N_GX * N_GY, 1, 256),
            shape(1, 3 * LEV * 16), shape(1, 3 * LEV * 16),
        ),
        in_specs=[VMEM, HBM, HBM] + [VMEM] * 7, out_specs=(HBM, VMEM, VMEM, VMEM),
        scratch_shapes=[
            pltpu.VMEM((32, 128, 128), F32),
            pltpu.VMEM((32, 128, 128), jnp.int32),
            pltpu.VMEM((32, 128, 128), F32),
            pltpu.VMEM((32, 48, 128), F32),
            pltpu.VMEM((32, 8, 256), F32),
            pltpu.VMEM((256, 128), F32),
            pltpu.VMEM((64, 256), F32),
            pltpu.VMEM((64, 128), F32),
        ]
        + [pltpu.VMEM((256, 128), F32)] * WIDE
        + [pltpu.VMEM((128, 128), F32)] * WIDE
        + [pltpu.VMEM((128, 128), jnp.int32)] * WIDE
        + [pltpu.VMEM((128, 128), F32)] * (6 * WIDE)
        + [pltpu.SemaphoreType.DMA((32,)), pltpu.SemaphoreType.DMA((6,))],
        compiler_params=room(60), name="fire", cost_estimate=cost(10**9, 8 * 10**6),
    )(
        tile_list, level_set, fuel, windows, jnp.asarray(words), jnp.asarray(wcol, BF16),
        jnp.asarray(spread, BF16), left, right, token,
    )
    fluxes = lax.all_to_all(message, ("gx", "gy"), split_axis=0, concat_axis=0, tiled=True)
    air_left, air_right = neighbours(edge_right, edge_left, "gy", N_GY)
    rimmed = pl.pallas_call(
        rims_kernel, out_shape=shape(3 * LEV, 16, 128), in_specs=[VMEM] * 3, out_specs=VMEM,
        compiler_params=room(8), name="rims", cost_estimate=cost(2 * 10**8, 4 * 10**6),
    )(moved, air_left, air_right)
    heat, side, smoke, heat_first, heat_last = pl.pallas_call(
        place_kernel,
        out_shape=(shape(16, 128), shape(16, 128), shape(16, 128), shape(1, 128), shape(1, 128)),
        in_specs=[SMEM, VMEM], out_specs=(VMEM,) * 5, compiler_params=room(4),
        name="place", cost_estimate=cost(10**6, 10**6),
    )(where, fluxes)
    heat_above, heat_below = neighbours(heat_last, heat_first, rows, N_GRP * N_GX)
    result = pl.pallas_call(
        final_kernel, out_shape=shape(3 * LEV, 16, 128), in_specs=[VMEM] * 7, out_specs=HBM,
        scratch_shapes=[pltpu.VMEM((3 * LEV, 16, 128), F32), pltpu.SemaphoreType.DMA((6,))],
        compiler_params=room(8), name="final", cost_estimate=cost(10**6, 4 * 10**6),
    )(
        rimmed, heat, side, smoke, heat_above, heat_below, jnp.asarray(profile)
    )
    return (result.reshape(3, LEV, 16, 128), phases)


def solution(mesh):
    in_specs = (
        P(None, None, ("grp", "gx"), "gy"),
        P(("grp", "gx", "gy"), None, None),
        P(("grp", "gx", "gy"), None, None),
        P("grp", None, None),
    )
    out_specs = (P(None, None, ("grp", "gx"), "gy"), P(("grp", "gx", "gy"), None, None))
    return jax.shard_map(
        on_device, mesh=mesh, in_specs=in_specs, out_specs=out_specs, check_vma=False
    )
```

```python
import jax
import jax.numpy as jnp
import numpy as np
from jax import lax
from jax.experimental import pallas as pl
from jax.experimental.pallas import tpu as pltpu
from jax.sharding import PartitionSpec as P

SUB = 4
LEV = 80
N_GRP, N_GX, N_GY = 4, 8, 8
WIDE = 2

spread_rates = np.array(
    [0.3, 0.5, 0.9, 1.2, 0.6, 0.4, 0.7, 0.35, 0.25, 0.45, 0.55, 0.8, 1.0], np.float32
)
heat_yields = np.array(
    [1.0, 2.5, 4.0, 3.0, 1.5, 2.0, 5.0, 1.2, 0.8, 3.5, 2.2, 4.5, 2.8], np.float32
)
smoke_yields = np.array(
    [0.5, 1.5, 2.5, 1.0, 3.0, 0.8, 2.0, 1.8, 0.6, 2.6, 1.1, 3.4, 1.4], np.float32
)
courant = 0.1
viscosity = 0.1
buoyancy = 0.5
source_step = 0.5
fire_time = 0.1
wind_gain = 0.3

F32 = jnp.float32
BF16 = jnp.bfloat16
VMEM = pl.BlockSpec(memory_space=pltpu.VMEM)
SMEM = pl.BlockSpec(memory_space=pltpu.SMEM)
HBM = pl.BlockSpec(memory_space=pltpu.HBM)


def room(mib):
    return pltpu.CompilerParams(vmem_limit_bytes=mib * 1024 * 1024)


def shape(*dims, dtype=F32):
    return jax.ShapeDtypeStruct(dims, dtype)


def cost(flops, moved):
    return pl.CostEstimate(flops=flops, bytes_accessed=moved, transcendentals=0)


def lanes_of(rows=8):
    return lax.broadcasted_iota(jnp.int32, (rows, 128), 1)


def sublanes_of(rows=8):
    return lax.broadcasted_iota(jnp.int32, (rows, 128), 0)


def halves(value):
    high = value.astype(BF16).astype(F32)
    return high, value - high


def spread_line(line, row, low, high, rims):
    lane, sub = lanes_of(), sublanes_of()
    line = jnp.broadcast_to(line, (8, 128))
    here = (lane >= 12 * row) & (lane < 12 * row + 10)
    fanned = pltpu.roll(line, 0, 1, stride=8, stride_axis=0)
    first = pltpu.roll(fanned, (12 * row + 73) % 128, 1)
    second = pltpu.roll(fanned, (12 * row + 9) % 128, 1)
    low = jnp.where(here & ((sub < 7) | (lane > 12 * row)), first, low)
    high = jnp.where(here & ((sub > 0) | (lane < 12 * row + 9)), second, high)
    edges = pltpu.roll(line, (12 * row + 11) % 128, 1)
    rims = jnp.where((lane == 12 * row + 10 + sub) & (sub < 2), edges, rims)
    return low, high, rims


def table_kernel(list_ref, air_ref, tile_ref, choice_ref, where_ref, surf_ref, sem):
    copies = [
        pltpu.make_async_copy(air_ref.at[LEV * comp], surf_ref.at[comp], sem.at[comp])
        for comp in range(2)
    ]
    for copy in copies:
        copy.start()
    gx, gy = lax.axis_index("gx"), lax.axis_index("gy")
    me = gx * N_GY + gy
    left, right = gy > 0, gy < N_GY - 1
    k = lax.broadcasted_iota(jnp.int32, (1, 128), 1)
    codes = jnp.where(k < 32, me * 32 + (k ^ 7), -5)
    singles = (
        (40, right, me + 1, 0), (41, left, me - 1, 15), (48, right, me + 1, 16),
        (49, left, me - 1, 31),
    )
    for at, there, device, tile in singles:
        codes = jnp.where((k == at) & there, device * 32 + tile, codes)
    listed = list_ref[0]
    choice = jnp.zeros((64, 128), F32)
    for slot in range(32):
        entry = jnp.broadcast_to(listed[:, slot : slot + 1], (64, 128))
        choice = jnp.where(entry == codes, 1.0, choice)
    choice_ref[...] = choice.astype(BF16)
    device = sublanes_of(64).astype(F32) + 1.0
    holder = jnp.sum(choice * device, axis=0, keepdims=True) - 1.0
    where_ref[...] = holder.astype(jnp.int32)
    tile_ref[...] = jnp.zeros(tile_ref.shape, F32)
    for copy in copies:
        copy.wait()
    none = jnp.zeros((8, 128), F32)
    for comp in range(2):
        lanes = slice(128 * comp, 128 * comp + 128)
        field = surf_ref[comp] * wind_gain
        for half in range(2):
            found = [none, none, none]
            for row in range(10):
                at = 8 * half + row - 1
                if 0 <= at < 16:
                    found = spread_line(field[at : at + 1], row, *found)
            tile_ref[16 * half : 16 * half + 8, lanes] = found[0]
            tile_ref[16 * half + 8 : 16 * half + 16, lanes] = found[1]
            tile_ref[40 + 8 * half : 48 + 8 * half, lanes] = found[2]


def windows_kernel(
    table_ref, choice_ref, above_ref, below_ref, left_ref, out_ref, token_ref, tile_ref, made_ref
):
    token_ref[...] = jnp.zeros((8, 128), F32) + left_ref[0:1, 0:128] * 0.0
    tile_ref[...] = table_ref[...]
    for comp in range(2):
        lanes = slice(128 * comp, 128 * comp + 128)
        line_at = slice(LEV * comp, LEV * comp + 1)
        for half, (ref, row) in enumerate(((above_ref, 0), (below_ref, 9))):
            places = (
                slice(16 * half, 16 * half + 8),
                slice(16 * half + 8, 16 * half + 16),
                slice(40 + 8 * half, 48 + 8 * half),
            )
            old = [tile_ref[rows, lanes] for rows in places]
            fresh = spread_line(ref[line_at, :] * wind_gain, row, *old)
            for rows, value in zip(places, fresh):
                tile_ref[rows, lanes] = value
    choice = choice_ref[...]
    high, low = halves(tile_ref[...])
    made_ref[...] = jnp.dot(choice, high.astype(BF16), preferred_element_type=F32) + jnp.dot(
        choice, low.astype(BF16), preferred_element_type=F32
    )
    for fire in range(N_GX * N_GY):
        out_ref[fire] = made_ref[fire : fire + 1, :]


def fire_kernel(
    list_ref, phase_in, fuel_in, recv_in, words_ref, wcol_ref, spread_ref,
    left_in, right_in, token_in, out_ref, msg_ref, left_out, right_out,
    recv_ref, phase_ref, fuel_ref, done_ref, column_ref, sums_ref, means_ref, flat_ref, line_ref,
    *rest,
):
    buffers, sem, sem_in = rest[:-2], rest[-2], rest[-1]
    sides = [buffers[at::WIDE] for at in range(WIDE)]
    left_out[...] = left_in[...]
    right_out[...] = right_in[...]
    arrival = pltpu.make_async_copy(recv_in, recv_ref, sem_in.at[6])
    arrival.start()
    loads = []
    for at, (low, high) in enumerate(((0, 2), (2, 8), (8, 32))):
        some = pl.ds(low, high - low)
        loads.append(
            (
                pltpu.make_async_copy(phase_in.at[some], phase_ref.at[some], sem_in.at[at]),
                pltpu.make_async_copy(fuel_in.at[some], fuel_ref.at[some], sem_in.at[3 + at]),
            )
        )
        for load in loads[-1]:
            load.start()
    lane24 = lanes_of(24)
    knot = sublanes_of(24)
    knot = (knot & 7) + (knot >> 3)
    unfold = (lane24 >= 12 * knot) & (lane24 < 12 * knot + 12)
    place = lax.broadcasted_iota(jnp.int32, (64, 256), 1)
    place = (place & 127) % 12
    me = lax.axis_index("gx") * N_GY + lax.axis_index("gy")
    entries = jnp.broadcast_to(list_ref[0, pl.ds(me, 1), :].astype(F32), (32, 32))
    across = lax.broadcasted_iota(jnp.int32, (32, 32), 1)
    along_slots = lax.broadcasted_iota(jnp.int32, (32, 32), 0)
    tiles = jnp.sum(jnp.where(across == along_slots, entries, 0.0), axis=1, keepdims=True)
    words = words_ref[...]
    row8, lane8 = sublanes_of(), lanes_of()

    tiles = jnp.broadcast_to(tiles, (32, 256)).astype(jnp.int32)
    target = lax.broadcasted_iota(jnp.int32, (32, 256), 1)
    owner, col = tiles >> 5, tiles & 15
    from_left = (owner - 1 == target - 64) & (col == 0) & ((owner & 7) > 0)
    from_right = (owner + 1 == target - 128) & (col == 15) & ((owner & 7) < 7)
    from_left = from_left & (target >= 64) & (target < 128)
    from_right = from_right & (target >= 128) & (target < 192)
    taken = ((owner == target) & (target < 64)) | from_left | from_right
    taken = jnp.where(taken & (tiles >= 0), 1.0, 0.0).astype(BF16)
    arrival.wait()
    for device in range(N_GX * N_GY):
        flat_ref[device : device + 1, :] = recv_ref[device]
    sent = flat_ref[...]
    sent = jnp.concatenate(
        [
            jnp.where(place < 10, sent, 0.0), jnp.where(place == 10, sent, 0.0),
            jnp.where(place == 11, sent, 0.0), jnp.zeros((64, 256), F32),
        ],
        axis=0,
    )
    high, low = halves(sent)
    lines = jnp.dot(taken, high.astype(BF16), preferred_element_type=F32) + jnp.dot(
        taken, low.astype(BF16), preferred_element_type=F32
    )
    line_ref[0:32, :] = lines[:, 0:128]
    line_ref[32:64, :] = lines[:, 128:256]

    def columns(at, carry):
        parts = []
        for spot in range(8):
            for comp in range(2):
                line = line_ref[pl.ds(32 * comp + 8 * at + spot, 1), :]
                parts.append(jnp.where(unfold, jnp.broadcast_to(line, (24, 128)), 0.0))
        high, low = halves(jnp.concatenate(parts, axis=0))
        both = jnp.dot(high.astype(BF16), wcol_ref[...], preferred_element_type=F32) + jnp.dot(
            low.astype(BF16), wcol_ref[...], preferred_element_type=F32
        )
        for spot in range(8):
            column_ref[8 * at + spot] = both[48 * spot : 48 * spot + 48]
        return carry

    def result(slot):
        return pltpu.make_async_copy(done_ref.at[slot], out_ref.at[slot], sem.at[slot])

    def block(at):
        return slice(8 * at, 8 * at + 8)

    def store(target, at, values):
        field, behind, beyond = target
        turned = [pltpu.roll(value, 1, 1) for value in values]
        for k, value in enumerate(values):
            field[block(at + k), :] = value
        backs = [jnp.where(lane8 == 0, 0.0, x - y) for x, y in zip(values, turned)]
        aheads = [pltpu.roll(back, 127, 1) for back in backs]
        for k, (back, ahead) in enumerate(zip(backs, aheads)):
            behind[block(at + k), :] = back
            beyond[block(at + k), :] = ahead

    def begin(slot, side):
        gust, rate, word = side[:3]
        runs = [column_ref[slot, 8 * at : 8 * at + 8, :] for at in range(6)]
        steps = [runs[at + 1] - runs[at] for at in (0, 1, 3, 4)]
        for first in range(0, 16, 8):
            blocks = range(first, first + 8)
            places = [pl.ds(j, 8, stride=16) for j in blocks]
            fuels = [fuel_ref[slot, there, :] for there in places]
            packed = [
                jnp.take_along_axis(words, fuel, axis=1, mode="promise_in_bounds")
                for fuel in fuels
            ]
            store(side[3:6], first, [phase_ref[slot, there, :] for there in places])
            bases = [(x & 31).astype(F32) * np.float32(0.05 * fire_time) for x in packed]
            for j, x, base in zip(blocks, packed, bases):
                rate[block(j), :] = base
                word[block(j), :] = x
            low = first // 8
            for comp in range(2):
                run, step = runs[3 * comp + low], steps[2 * comp + low]
                parts = [np.float32((j + 0.5) / 16 + 0.5 - low) for j in blocks]
                winds = [run + part * step for part in parts]
                for j, wind, base in zip(blocks, winds, bases):
                    gust[block(16 * comp + j), :] = wind * base

    def advance(side, source, keep):
        gust, rate = side[:2]
        field, behind, beyond = source
        edge = field[block(0), :] - pltpu.roll(field[block(15), :], 1, 0)
        edge = jnp.where(row8 == 0, 0.0, edge)
        last = pltpu.roll(edge, 7, 0)
        for first in range(0, 16, 4):
            blocks = range(first, first + 4)
            fields = [field[block(j), :] for j in range(first, min(first + 4 + 1, 16))]
            aheads = [y - x for x, y in zip(fields, fields[1:])]
            if first == 16 - 4:
                aheads.append(last)
            backs = [edge] + aheads[:-1]
            edge = aheads[-1]
            side_backs = [behind[block(j), :] for j in blocks]
            side_aheads = [beyond[block(j), :] for j in blocks]
            a = [jnp.maximum(x, 0.0) for x in backs]
            b = [jnp.minimum(x, 0.0) for x in aheads]
            upwinds = [x * x + y * y for x, y in zip(a, b)]
            c = [jnp.maximum(x, 0.0) for x in side_backs]
            d = [jnp.minimum(x, 0.0) for x in side_aheads]
            upwinds = [u + (x * x + y * y) for u, x, y in zip(upwinds, c, d)]
            inverses = [lax.rsqrt(jnp.maximum(u, 1e-36)) for u in upwinds]
            row_slopes = [x + y for x, y in zip(backs, aheads)]
            col_slopes = [x + y for x, y in zip(side_backs, side_aheads)]
            squares = [x * x + y * y for x, y in zip(row_slopes, col_slopes)]
            factors = [lax.rsqrt(jnp.maximum(x, 4.0)) for x in squares]
            along = [
                gust[block(j), :] * x + gust[block(16 + j), :] * y
                for j, x, y in zip(blocks, row_slopes, col_slopes)
            ]
            roots = [u * x for u, x in zip(upwinds, inverses)]
            speeds = [
                rate[block(j), :] + jnp.maximum(x * f, 0.0)
                for j, x, f in zip(blocks, along, factors)
            ]
            keep(first, [x - v * r for x, v, r in zip(fields, speeds, roots)])

    def finish(slot, side):
        word = side[2]
        sums = [[], []]

        def keep(first, values):
            for k, value in enumerate(values):
                done_ref[slot, pl.ds(first + k, 8, stride=16), :] = value
            burning = [jnp.exp(value) for value in values]
            burning = [1.0 + value for value in burning]
            guesses = [pl.reciprocal(value, approx=True) for value in burning]
            burning = [y * (2.0 - x * y) for x, y in zip(burning, guesses)]
            packed = [word[block(first + k), :] for k in range(len(values))]
            heats = [((x >> 5) & 63).astype(F32) * y for x, y in zip(packed, burning)]
            smokes = [(x >> 11).astype(F32) * y for x, y in zip(packed, burning)]
            for total, terms in zip(sums, (heats, smokes)):
                while len(terms) > 1:
                    terms = [x + y for x, y in zip(terms[::2], terms[1::2])]
                total.append(terms[0])

        advance(side, side[6:9], keep)
        result(slot).start()
        sums_ref[slot, :, 0:128] = sum(sums[0])
        sums_ref[slot, :, 128:256] = sum(sums[1])

    def into(target):
        return lambda first, values: store(target, first, values)

    lax.fori_loop(0, 4, columns, 0)

    def several(at, carry):
        slot = WIDE * at
        for start, some in zip((0, 2 // WIDE, 8 // WIDE), loads):

            @pl.when(at == start)
            def _():
                for load in some:
                    load.wait()

        for spot, side in enumerate(sides):
            begin(slot + spot, side)
        for step in range(SUB - 1):
            for side in sides:
                pair_of = (side[3:6], side[6:9])
                advance(side, pair_of[step % 2], into(pair_of[1 - step % 2]))
        for spot, side in enumerate(sides):
            finish(slot + spot, side)
        return carry

    lax.fori_loop(0, 32 // WIDE, several, 0)
    high, low = halves(sums_ref[...].reshape(256, 256))
    spread = spread_ref[...]
    means_ref[...] = (
        jnp.dot(high.astype(BF16), spread, preferred_element_type=F32)
        + jnp.dot(low.astype(BF16), spread, preferred_element_type=F32)
    ) * np.float32(0.1 / 256)
    dense = means_ref[pl.ds(0, 32, stride=8), :]
    for row in range(1, 8):
        dense = dense + pltpu.roll(means_ref[pl.ds(row, 32, stride=8), :], 16 * row, 1)
    tile_row = list_ref[0, pl.ds(me, 1), :]
    owners = jnp.broadcast_to(tile_row >> 5, (64, 32))
    col = jnp.broadcast_to(tile_row & 15, (64, 32))
    live = jnp.broadcast_to(tile_row, (64, 32)) >= 0
    device = lax.broadcasted_iota(jnp.int32, (64, 32), 0)
    to_left = live & (owners - 1 == device) & (col == 0) & ((owners & 7) > 0)
    to_right = live & (owners + 1 == device) & (col == 15) & ((owners & 7) < 7)
    spot = lax.broadcasted_iota(jnp.int32, (32, 128), 1) & 15
    picked = []
    for chosen, kept in (
        (live & (owners == device), None), (to_left, spot == 0), (to_right, spot == 7),
    ):
        chosen = jnp.where(chosen, 1.0, 0.0).astype(BF16)
        high, low = halves(dense if kept is None else jnp.where(kept, dense, 0.0))
        picked.append(
            jnp.dot(chosen, high.astype(BF16), preferred_element_type=F32)
            + jnp.dot(chosen, low.astype(BF16), preferred_element_type=F32)
        )
    flat_ref[:, 0:128] = picked[0]
    flat_ref[:, 128:256] = picked[1] + picked[2]
    for device in range(N_GX * N_GY):
        msg_ref[device] = flat_ref[device : device + 1, :]

    def settle(slot, carry):
        result(slot).wait()
        return carry

    lax.fori_loop(0, 32, settle, 0)


def place_kernel(where_ref, flux_ref, heat_ref, side_ref, smoke_ref, first_ref, last_ref):
    lane, sub = lanes_of(), sublanes_of()
    key = lane // 8
    heat_from = sub * 16 + lane % 8
    zero = jnp.zeros((8, 128), F32)

    def tile(at, lanes):
        fire = where_ref[0, at]
        line = flux_ref[jnp.maximum(fire, 0), :, lanes]
        return jnp.where(fire >= 0, jnp.broadcast_to(line, (8, 128)), 0.0)

    def find(value, index):
        return jnp.take_along_axis(value, index, axis=1, mode="promise_in_bounds")

    own, beside = slice(0, 128), slice(128, 256)
    for half in range(2):
        rows = slice(8 * half, 8 * half + 8)
        heat = smoke = zero
        for col in range(16):
            value = tile(16 * half + (col ^ 7), own)
            heat = jnp.where(key == col, find(value, heat_from), heat)
            smoke = jnp.where(key == col, find(value, heat_from + 8), smoke)
        rim_left = find(tile(41 + 8 * half, beside), heat_from)
        rim_right = find(tile(40 + 8 * half, beside), heat_from)
        left = pltpu.roll(jnp.where(lane == 127, rim_left, heat), 1, 1)
        right = pltpu.roll(jnp.where(lane == 0, rim_right, heat), 127, 1)
        heat_ref[rows, :] = heat
        smoke_ref[rows, :] = smoke
        side_ref[rows, :] = 0.5 * (right - left)
        if half == 0:
            first_ref[...] = heat[0:1]
        else:
            last_ref[...] = heat[7:8]


def rows_kernel(air_ref, first_ref, last_ref, sem):
    copies = (
        pltpu.make_async_copy(air_ref.at[:, 0, :], first_ref, sem.at[0]),
        pltpu.make_async_copy(air_ref.at[:, 15, :], last_ref, sem.at[1]),
    )
    for copy in copies:
        copy.start()
    for copy in copies:
        copy.wait()


def sides_kernel(air_ref, left_ref, right_ref):
    lane, sub = lanes_of(), sublanes_of()
    pick = jnp.where((lane == 127 * sub) & (sub < 2), 1.0, 0.0)
    columns = air_ref[...].reshape(3 * LEV * 16, 128)
    picked = 0.0
    for part in halves(columns):
        picked += lax.dot_general(
            pick.astype(BF16), part.astype(BF16), (((1,), (1,)), ((), ())),
            preferred_element_type=F32,
        )
    left_ref[...] = picked[0:1]
    right_ref[...] = picked[1:2]


def air_kernel(
    air_ref, above_ref, below_ref, left_ref, right_ref, token_in, out_ref, token_ref
):
    token_ref[...] = token_in[...]
    for side, ref in enumerate((left_ref, right_ref)):
        for at in range(30):
            level, line = 3 * LEV + 2 * side + at // 16, at % 16
            out_ref[level, line : line + 1, :] = ref[:, 128 * at : 128 * at + 128]
    lane = lax.broadcasted_iota(jnp.int32, (8, 16, 128), 2)
    row = lax.broadcasted_iota(jnp.int32, (8, 16, 128), 1)

    def chunk(at, carry):
        fields = []
        for part in range(3):
            start = part * LEV + at * 8
            mid = air_ref[pl.ds(start, 8)]
            above = above_ref[pl.ds(start, 8), :][:, None, :]
            below = below_ref[pl.ds(start, 8), :][:, None, :]
            up = jnp.where(row == 0, above, pltpu.roll(mid, 1, 1))
            down = jnp.where(row == 15, below, pltpu.roll(mid, 15, 1))
            left = jnp.where(lane == 0, 0.0, pltpu.roll(mid, 1, 2))
            right = jnp.where(lane == 127, 0.0, pltpu.roll(mid, 127, 2))
            fields.append((mid, up, down, left, right))
        for part in range(2):
            mid, up, down, left, right = fields[part]
            around = (up + down) + (left + right)
            out_ref[pl.ds(part * LEV + at * 8, 8)] = mid + viscosity * (around - 4.0 * mid)
        u, v = fields[0][0], fields[1][0]
        mid, up, down, left, right = fields[2]
        upwind = (
            jnp.maximum(u, 0.0) * (mid - up)
            + jnp.minimum(u, 0.0) * (down - mid)
            + jnp.maximum(v, 0.0) * (mid - left)
            + jnp.minimum(v, 0.0) * (right - mid)
        )
        out_ref[pl.ds(2 * LEV + at * 8, 8)] = mid - courant * upwind
        return carry

    lax.fori_loop(0, LEV // 8, chunk, 0)


def rims_kernel(part_ref, left_ref, right_ref, out_ref):
    sub, lane = sublanes_of(), lanes_of()
    expand = jnp.where((sub < 2) & (lane == 0), 1.0, 0.0) + jnp.where(
        (sub >= 2) & (sub < 4) & (lane == 127), 1.0, 0.0
    )
    expand = expand.astype(BF16)

    def chunk(at, carry):
        for part in range(3):
            spot = pl.ds(pl.multiple_of(part * (LEV * 16) + at * 128, 128), 128)
            left, right = left_ref[:, spot], right_ref[:, spot]
            if part < 2:
                left, right = viscosity * left, viscosity * right
            else:
                line = LEV // 8 + at
                level, line = 3 * LEV + (line >> 4), pl.ds(line & 15, 1)
                left = courant * jnp.maximum(part_ref[level, line, :], 0.0) * left
                right = -courant * jnp.minimum(part_ref[level + 2, line, :], 0.0) * right
            left_high, left_low = halves(left)
            right_high, right_low = halves(right)
            rims = jnp.where(sub == 0, left_high, 0.0)
            rims = jnp.where(sub == 1, left_low, rims)
            rims = jnp.where(sub == 2, right_high, rims)
            rims = jnp.where(sub == 3, right_low, rims)
            rim = lax.dot_general(
                rims.astype(BF16), expand, (((0,), (0,)), ((), ())), preferred_element_type=F32
            ).reshape(8, 16, 128)
            levels = pl.ds(part * LEV + at * 8, 8)
            out_ref[levels] = part_ref[levels] + rim
        return carry

    lax.fori_loop(0, LEV // 8, chunk, 0, unroll=2)


def final_kernel(
    part_ref, heat_ref, side_ref, smoke_ref, above_ref, below_ref, prof_ref,
    out_ref, made_ref, sem,
):
    heat = heat_ref[...]
    row = sublanes_of(16)
    up = jnp.where(row == 0, above_ref[...], pltpu.roll(heat, 1, 0))
    down = jnp.where(row == 15, below_ref[...], pltpu.roll(heat, 15, 0))
    sources = (0.5 * (down - up), side_ref[...], smoke_ref[...])
    copies = []
    for part in range(3):
        for half in range(2):
            first = part * LEV + half * (LEV // 2)

            def one(at, carry):
                for spot in range(8):
                    level = half * (LEV // 2) + 8 * at + spot
                    weight = prof_ref[pl.ds(level, 1), :]
                    before = part_ref[part * LEV + level]
                    made_ref[part * LEV + level] = before + weight * sources[part]
                return carry

            lax.fori_loop(0, LEV // 16, one, 0)
            some = pl.ds(first, LEV // 2)
            copies.append(
                pltpu.make_async_copy(
                    made_ref.at[some], out_ref.at[some], sem.at[2 * part + half]
                )
            )
            copies[-1].start()
    for copy in copies:
        copy.wait()


def constants():
    spots = (np.arange(128) + 0.5) / 16 + 0.5
    weights = np.maximum(0.0, 1.0 - np.abs(spots[:, None] - np.arange(10)[None, :]))
    wcol = np.zeros((128, 128), np.float32)
    for row in range(10):
        wcol[12 * row : 12 * row + 10, :] = weights.T
        wcol[12 * row + 10, :] = weights[:, 0]
        wcol[12 * row + 11, :] = weights[:, 9]
    spread = np.zeros((256, 128), np.float32)
    for c in range(128):
        spread[c, c // 16] = 1.0
        spread[128 + c, 8 + c // 16] = 1.0
    words = np.zeros((8, 128), np.int32)
    tables = (spread_rates * 20, heat_yields * 10, smoke_yields * 10)
    rates, heats, smokes = (np.rint(table).astype(np.int32) for table in tables)
    words[:, :13] = rates + 32 * heats + 2048 * smokes
    levels = np.arange(LEV, dtype=np.float32)
    profile = np.exp(-levels * np.float32(8.0) / np.float32(LEV))
    profile = np.broadcast_to((np.float32(0.5) * profile)[:, None], (LEV, 128))
    return wcol, spread, words, np.ascontiguousarray(profile)


def neighbours(last, first, axes, count):
    ends = count - 1
    before = lax.ppermute(last, axes, [(i, i + 1) for i in range(ends)])
    after = lax.ppermute(first, axes, [(i + 1, i) for i in range(ends)])
    return before, after


def on_device(air, level_set, fuel, tile_list):
    wcol, spread, words, profile = constants()
    rows = ("grp", "gx")
    levels = air.reshape(3 * LEV, 16, 128)

    first, last = pl.pallas_call(
        rows_kernel,
        out_shape=(shape(3 * LEV, 128), shape(3 * LEV, 128)),
        in_specs=[HBM], out_specs=(VMEM,) * 2, scratch_shapes=[pltpu.SemaphoreType.DMA((2,))],
        compiler_params=room(60), name="rows", cost_estimate=cost(10**5, 10**6),
    )(levels)
    air_above, air_below = neighbours(last, first, rows, N_GRP * N_GX)

    left, right = pl.pallas_call(
        sides_kernel, out_shape=(shape(1, 3 * LEV * 16), shape(1, 3 * LEV * 16)),
        in_specs=[VMEM], out_specs=(VMEM,) * 2, compiler_params=room(4),
        name="sides", cost_estimate=cost(10**8, 2 * 10**6),
    )(levels)
    table, choice, where = pl.pallas_call(
        table_kernel, out_shape=(
            shape(128, 256), shape(64, 128, dtype=BF16), shape(1, 128, dtype=jnp.int32)
        ),
        in_specs=[VMEM, HBM], out_specs=(VMEM,) * 3,
        scratch_shapes=[pltpu.VMEM((2, 16, 128), F32), pltpu.SemaphoreType.DMA((2,))],
        compiler_params=room(2), name="table", cost_estimate=cost(10**6, 10**6),
    )(tile_list, levels)
    windows, token = pl.pallas_call(
        windows_kernel,
        out_shape=(shape(N_GX * N_GY, 1, 256), shape(8, 128)),
        in_specs=[VMEM] * 5, out_specs=(VMEM,) * 2,
        scratch_shapes=[pltpu.VMEM((128, 256), F32), pltpu.VMEM((64, 256), F32)],
        compiler_params=room(2), name="windows", cost_estimate=cost(10**6, 10**6),
    )(table, choice, air_above, air_below, left)
    windows = lax.all_to_all(windows, ("gx", "gy"), split_axis=0, concat_axis=0, tiled=True)
    moved, token = pl.pallas_call(
        air_kernel, out_shape=(shape(3 * LEV + 4, 16, 128), shape(8, 128)),
        in_specs=[VMEM] * 6, out_specs=(VMEM, VMEM),
        compiler_params=room(8), name="air", cost_estimate=cost(2 * 10**8, 4 * 10**6),
    )(levels, air_above, air_below, left, right, token)

    phases, message, edge_left, edge_right = pl.pallas_call(
        fire_kernel,
        out_shape=(
            shape(32, 128, 128), shape(N_GX * N_GY, 1, 256),
            shape(1, 3 * LEV * 16), shape(1, 3 * LEV * 16),
        ),
        in_specs=[VMEM, HBM, HBM, HBM] + [VMEM] * 6, out_specs=(HBM, VMEM, VMEM, VMEM),
        scratch_shapes=[
            pltpu.VMEM((N_GX * N_GY, 1, 256), F32),
            pltpu.VMEM((32, 128, 128), F32),
            pltpu.VMEM((32, 128, 128), jnp.int32),
            pltpu.VMEM((32, 128, 128), F32),
            pltpu.VMEM((32, 48, 128), F32),
            pltpu.VMEM((32, 8, 256), F32),
            pltpu.VMEM((256, 128), F32),
            pltpu.VMEM((64, 256), F32),
            pltpu.VMEM((64, 128), F32),
        ]
        + [pltpu.VMEM((256, 128), F32)] * WIDE
        + [pltpu.VMEM((128, 128), F32)] * WIDE
        + [pltpu.VMEM((128, 128), jnp.int32)] * WIDE
        + [pltpu.VMEM((128, 128), F32)] * (6 * WIDE)
        + [pltpu.SemaphoreType.DMA((32,)), pltpu.SemaphoreType.DMA((7,))],
        compiler_params=room(60), name="fire", cost_estimate=cost(10**9, 8 * 10**6),
    )(
        tile_list, level_set, fuel, windows, jnp.asarray(words), jnp.asarray(wcol, BF16),
        jnp.asarray(spread, BF16), left, right, token,
    )
    fluxes = lax.all_to_all(message, ("gx", "gy"), split_axis=0, concat_axis=0, tiled=True)
    air_left, air_right = neighbours(edge_right, edge_left, "gy", N_GY)
    rimmed = pl.pallas_call(
        rims_kernel, out_shape=shape(3 * LEV, 16, 128), in_specs=[VMEM] * 3, out_specs=VMEM,
        compiler_params=room(8), name="rims", cost_estimate=cost(2 * 10**8, 4 * 10**6),
    )(moved, air_left, air_right)
    heat, side, smoke, heat_first, heat_last = pl.pallas_call(
        place_kernel,
        out_shape=(shape(16, 128), shape(16, 128), shape(16, 128), shape(1, 128), shape(1, 128)),
        in_specs=[SMEM, VMEM], out_specs=(VMEM,) * 5, compiler_params=room(4),
        name="place", cost_estimate=cost(10**6, 10**6),
    )(where, fluxes)
    heat_above, heat_below = neighbours(heat_last, heat_first, rows, N_GRP * N_GX)
    result = pl.pallas_call(
        final_kernel, out_shape=shape(3 * LEV, 16, 128), in_specs=[VMEM] * 7, out_specs=HBM,
        scratch_shapes=[pltpu.VMEM((3 * LEV, 16, 128), F32), pltpu.SemaphoreType.DMA((6,))],
        compiler_params=room(8), name="final", cost_estimate=cost(10**6, 4 * 10**6),
    )(
        rimmed, heat, side, smoke, heat_above, heat_below, jnp.asarray(profile)
    )
    return (result.reshape(3, LEV, 16, 128), phases)


def solution(mesh):
    in_specs = (
        P(None, None, ("grp", "gx"), "gy"),
        P(("grp", "gx", "gy"), None, None),
        P(("grp", "gx", "gy"), None, None),
        P("grp", None, None),
    )
    out_specs = (P(None, None, ("grp", "gx"), "gy"), P(("grp", "gx", "gy"), None, None))
    return jax.shard_map(
        on_device, mesh=mesh, in_specs=in_specs, out_specs=out_specs, check_vma=False
    )
```

```python
import jax
import jax.numpy as jnp
import numpy as np
from jax import lax
from jax.experimental import pallas as pl
from jax.experimental.pallas import tpu as pltpu
from jax.sharding import PartitionSpec as P

SUB = 4
LEV = 80
N_GRP, N_GX, N_GY = 4, 8, 8
WIDE = 2

spread_rates = np.array(
    [0.3, 0.5, 0.9, 1.2, 0.6, 0.4, 0.7, 0.35, 0.25, 0.45, 0.55, 0.8, 1.0], np.float32
)
heat_yields = np.array(
    [1.0, 2.5, 4.0, 3.0, 1.5, 2.0, 5.0, 1.2, 0.8, 3.5, 2.2, 4.5, 2.8], np.float32
)
smoke_yields = np.array(
    [0.5, 1.5, 2.5, 1.0, 3.0, 0.8, 2.0, 1.8, 0.6, 2.6, 1.1, 3.4, 1.4], np.float32
)
courant = 0.1
viscosity = 0.1
buoyancy = 0.5
source_step = 0.5
fire_time = 0.1
wind_gain = 0.3

F32 = jnp.float32
BF16 = jnp.bfloat16
VMEM = pl.BlockSpec(memory_space=pltpu.VMEM)
SMEM = pl.BlockSpec(memory_space=pltpu.SMEM)
HBM = pl.BlockSpec(memory_space=pltpu.HBM)


def room(mib):
    return pltpu.CompilerParams(vmem_limit_bytes=mib * 1024 * 1024)


def shape(*dims, dtype=F32):
    return jax.ShapeDtypeStruct(dims, dtype)


def cost(flops, moved):
    return pl.CostEstimate(flops=flops, bytes_accessed=moved, transcendentals=0)


def lanes_of(rows=8):
    return lax.broadcasted_iota(jnp.int32, (rows, 128), 1)


def sublanes_of(rows=8):
    return lax.broadcasted_iota(jnp.int32, (rows, 128), 0)


def halves(value):
    high = value.astype(BF16).astype(F32)
    return high, value - high


def spread_line(line, row, low, high, rims):
    lane, sub = lanes_of(), sublanes_of()
    line = jnp.broadcast_to(line, (8, 128))
    here = (lane >= 12 * row) & (lane < 12 * row + 10)
    fanned = pltpu.roll(line, 0, 1, stride=8, stride_axis=0)
    first = pltpu.roll(fanned, (12 * row + 73) % 128, 1)
    second = pltpu.roll(fanned, (12 * row + 9) % 128, 1)
    low = jnp.where(here & ((sub < 7) | (lane > 12 * row)), first, low)
    high = jnp.where(here & ((sub > 0) | (lane < 12 * row + 9)), second, high)
    edges = pltpu.roll(line, (12 * row + 11) % 128, 1)
    rims = jnp.where((lane == 12 * row + 10 + sub) & (sub < 2), edges, rims)
    return low, high, rims


def table_kernel(list_ref, air_ref, tile_ref, choice_ref, where_ref, surf_ref, sem):
    copies = [
        pltpu.make_async_copy(air_ref.at[LEV * comp], surf_ref.at[comp], sem.at[comp])
        for comp in range(2)
    ]
    for copy in copies:
        copy.start()
    gx, gy = lax.axis_index("gx"), lax.axis_index("gy")
    me = gx * N_GY + gy
    left, right = gy > 0, gy < N_GY - 1
    k = lax.broadcasted_iota(jnp.int32, (1, 128), 1)
    codes = jnp.where(k < 32, me * 32 + (k ^ 7), -5)
    singles = (
        (40, right, me + 1, 0), (41, left, me - 1, 15), (48, right, me + 1, 16),
        (49, left, me - 1, 31),
    )
    for at, there, device, tile in singles:
        codes = jnp.where((k == at) & there, device * 32 + tile, codes)
    listed = list_ref[0]
    choice = jnp.zeros((64, 128), F32)
    for slot in range(32):
        entry = jnp.broadcast_to(listed[:, slot : slot + 1], (64, 128))
        choice = jnp.where(entry == codes, 1.0, choice)
    choice_ref[...] = choice.astype(BF16)
    device = sublanes_of(64).astype(F32) + 1.0
    holder = jnp.sum(choice * device, axis=0, keepdims=True) - 1.0
    where_ref[...] = holder.astype(jnp.int32)
    tile_ref[...] = jnp.zeros(tile_ref.shape, F32)
    for copy in copies:
        copy.wait()
    none = jnp.zeros((8, 128), F32)
    for comp in range(2):
        lanes = slice(128 * comp, 128 * comp + 128)
        field = surf_ref[comp] * wind_gain
        for half in range(2):
            found = [none, none, none]
            for row in range(10):
                at = 8 * half + row - 1
                if 0 <= at < 16:
                    found = spread_line(field[at : at + 1], row, *found)
            tile_ref[16 * half : 16 * half + 8, lanes] = found[0]
            tile_ref[16 * half + 8 : 16 * half + 16, lanes] = found[1]
            tile_ref[40 + 8 * half : 48 + 8 * half, lanes] = found[2]


def windows_kernel(
    table_ref, choice_ref, above_ref, below_ref, left_ref, out_ref, token_ref, tile_ref, made_ref
):
    token_ref[...] = jnp.zeros((8, 128), F32) + left_ref[0:1, 0:128] * 0.0
    tile_ref[...] = table_ref[...]
    for comp in range(2):
        lanes = slice(128 * comp, 128 * comp + 128)
        line_at = slice(LEV * comp, LEV * comp + 1)
        for half, (ref, row) in enumerate(((above_ref, 0), (below_ref, 9))):
            places = (
                slice(16 * half, 16 * half + 8),
                slice(16 * half + 8, 16 * half + 16),
                slice(40 + 8 * half, 48 + 8 * half),
            )
            old = [tile_ref[rows, lanes] for rows in places]
            fresh = spread_line(ref[line_at, :] * wind_gain, row, *old)
            for rows, value in zip(places, fresh):
                tile_ref[rows, lanes] = value
    choice = choice_ref[...]
    high, low = halves(tile_ref[...])
    made_ref[...] = jnp.dot(choice, high.astype(BF16), preferred_element_type=F32) + jnp.dot(
        choice, low.astype(BF16), preferred_element_type=F32
    )
    for fire in range(N_GX * N_GY):
        out_ref[fire] = made_ref[fire : fire + 1, :]


def fire_kernel(
    list_ref, phase_in, fuel_in, recv_ref, words_ref, wcol_ref, spread_ref,
    left_in, right_in, token_in, out_ref, msg_ref, left_out, right_out,
    phase_ref, fuel_ref, done_ref, column_ref, sums_ref, means_ref, flat_ref, line_ref, *rest,
):
    buffers, sem, sem_in = rest[:-2], rest[-2], rest[-1]
    sides = [buffers[at::WIDE] for at in range(WIDE)]
    left_out[...] = left_in[...]
    right_out[...] = right_in[...]
    loads = []
    for at, (low, high) in enumerate(((0, 2), (2, 8), (8, 32))):
        some = pl.ds(low, high - low)
        loads.append(
            (
                pltpu.make_async_copy(phase_in.at[some], phase_ref.at[some], sem_in.at[at]),
                pltpu.make_async_copy(fuel_in.at[some], fuel_ref.at[some], sem_in.at[3 + at]),
            )
        )
        for load in loads[-1]:
            load.start()
    lane24 = lanes_of(24)
    knot = sublanes_of(24)
    knot = (knot & 7) + (knot >> 3)
    unfold = (lane24 >= 12 * knot) & (lane24 < 12 * knot + 12)
    place = lax.broadcasted_iota(jnp.int32, (64, 256), 1)
    place = (place & 127) % 12
    me = lax.axis_index("gx") * N_GY + lax.axis_index("gy")
    entries = jnp.broadcast_to(list_ref[0, pl.ds(me, 1), :].astype(F32), (32, 32))
    across = lax.broadcasted_iota(jnp.int32, (32, 32), 1)
    along_slots = lax.broadcasted_iota(jnp.int32, (32, 32), 0)
    tiles = jnp.sum(jnp.where(across == along_slots, entries, 0.0), axis=1, keepdims=True)
    words = words_ref[...]
    row8, lane8 = sublanes_of(), lanes_of()

    tiles = jnp.broadcast_to(tiles, (32, 256)).astype(jnp.int32)
    target = lax.broadcasted_iota(jnp.int32, (32, 256), 1)
    owner, col = tiles >> 5, tiles & 15
    from_left = (owner - 1 == target - 64) & (col == 0) & ((owner & 7) > 0)
    from_right = (owner + 1 == target - 128) & (col == 15) & ((owner & 7) < 7)
    from_left = from_left & (target >= 64) & (target < 128)
    from_right = from_right & (target >= 128) & (target < 192)
    taken = ((owner == target) & (target < 64)) | from_left | from_right
    taken = jnp.where(taken & (tiles >= 0), 1.0, 0.0).astype(BF16)
    for device in range(N_GX * N_GY):
        flat_ref[device : device + 1, :] = recv_ref[device]
    sent = flat_ref[...]
    sent = jnp.concatenate(
        [
            jnp.where(place < 10, sent, 0.0), jnp.where(place == 10, sent, 0.0),
            jnp.where(place == 11, sent, 0.0), jnp.zeros((64, 256), F32),
        ],
        axis=0,
    )
    high, low = halves(sent)
    lines = jnp.dot(taken, high.astype(BF16), preferred_element_type=F32) + jnp.dot(
        taken, low.astype(BF16), preferred_element_type=F32
    )
    line_ref[0:32, :] = lines[:, 0:128]
    line_ref[32:64, :] = lines[:, 128:256]

    def columns(at, carry):
        parts = []
        for spot in range(16):
            for comp in range(2):
                line = line_ref[pl.ds(32 * comp + 16 * at + spot, 1), :]
                parts.append(jnp.where(unfold, jnp.broadcast_to(line, (24, 128)), 0.0))
        high, low = halves(jnp.concatenate(parts, axis=0))
        both = jnp.dot(high.astype(BF16), wcol_ref[...], preferred_element_type=F32) + jnp.dot(
            low.astype(BF16), wcol_ref[...], preferred_element_type=F32
        )
        for spot in range(16):
            column_ref[16 * at + spot] = both[48 * spot : 48 * spot + 48]
        return carry

    def result(slot):
        return pltpu.make_async_copy(done_ref.at[slot], out_ref.at[slot], sem.at[slot])

    def block(at):
        return slice(8 * at, 8 * at + 8)

    def store(target, at, values):
        field, behind, beyond = target
        turned = [pltpu.roll(value, 1, 1) for value in values]
        for k, value in enumerate(values):
            field[block(at + k), :] = value
        backs = [jnp.where(lane8 == 0, 0.0, x - y) for x, y in zip(values, turned)]
        aheads = [pltpu.roll(back, 127, 1) for back in backs]
        for k, (back, ahead) in enumerate(zip(backs, aheads)):
            behind[block(at + k), :] = back
            beyond[block(at + k), :] = ahead

    def begin(slot, side):
        gust, rate, word = side[:3]
        runs = [column_ref[slot, 8 * at : 8 * at + 8, :] for at in range(6)]
        steps = [runs[at + 1] - runs[at] for at in (0, 1, 3, 4)]
        for first in range(0, 16, 8):
            blocks = range(first, first + 8)
            places = [pl.ds(j, 8, stride=16) for j in blocks]
            fuels = [fuel_ref[slot, there, :] for there in places]
            packed = [
                jnp.take_along_axis(words, fuel, axis=1, mode="promise_in_bounds")
                for fuel in fuels
            ]
            store(side[3:6], first, [phase_ref[slot, there, :] for there in places])
            bases = [(x & 31).astype(F32) * np.float32(0.05 * fire_time) for x in packed]
            for j, x, base in zip(blocks, packed, bases):
                rate[block(j), :] = base
                word[block(j), :] = x
            low = first // 8
            for comp in range(2):
                run, step = runs[3 * comp + low], steps[2 * comp + low]
                parts = [np.float32((j + 0.5) / 16 + 0.5 - low) for j in blocks]
                winds = [run + part * step for part in parts]
                for j, wind, base in zip(blocks, winds, bases):
                    gust[block(16 * comp + j), :] = wind * base

    def advance(side, source, keep):
        gust, rate = side[:2]
        field, behind, beyond = source
        edge = field[block(0), :] - pltpu.roll(field[block(15), :], 1, 0)
        edge = jnp.where(row8 == 0, 0.0, edge)
        last = pltpu.roll(edge, 7, 0)
        for first in range(0, 16, 4):
            blocks = range(first, first + 4)
            fields = [field[block(j), :] for j in range(first, min(first + 4 + 1, 16))]
            aheads = [y - x for x, y in zip(fields, fields[1:])]
            if first == 16 - 4:
                aheads.append(last)
            backs = [edge] + aheads[:-1]
            edge = aheads[-1]
            side_backs = [behind[block(j), :] for j in blocks]
            side_aheads = [beyond[block(j), :] for j in blocks]
            a = [jnp.maximum(x, 0.0) for x in backs]
            b = [jnp.minimum(x, 0.0) for x in aheads]
            upwinds = [x * x + y * y for x, y in zip(a, b)]
            c = [jnp.maximum(x, 0.0) for x in side_backs]
            d = [jnp.minimum(x, 0.0) for x in side_aheads]
            upwinds = [u + (x * x + y * y) for u, x, y in zip(upwinds, c, d)]
            inverses = [lax.rsqrt(jnp.maximum(u, 1e-36)) for u in upwinds]
            row_slopes = [x + y for x, y in zip(backs, aheads)]
            col_slopes = [x + y for x, y in zip(side_backs, side_aheads)]
            squares = [x * x + y * y for x, y in zip(row_slopes, col_slopes)]
            factors = [lax.rsqrt(jnp.maximum(x, 4.0)) for x in squares]
            along = [
                gust[block(j), :] * x + gust[block(16 + j), :] * y
                for j, x, y in zip(blocks, row_slopes, col_slopes)
            ]
            roots = [u * x for u, x in zip(upwinds, inverses)]
            speeds = [
                rate[block(j), :] + jnp.maximum(x * f, 0.0)
                for j, x, f in zip(blocks, along, factors)
            ]
            keep(first, [x - v * r for x, v, r in zip(fields, speeds, roots)])

    def finish(slot, side):
        word = side[2]
        sums = [[], []]

        def keep(first, values):
            for k, value in enumerate(values):
                done_ref[slot, pl.ds(first + k, 8, stride=16), :] = value
            burning = [jnp.exp(value) for value in values]
            burning = [1.0 + value for value in burning]
            guesses = [pl.reciprocal(value, approx=True) for value in burning]
            burning = [y * (2.0 - x * y) for x, y in zip(burning, guesses)]
            packed = [word[block(first + k), :] for k in range(len(values))]
            heats = [((x >> 5) & 63).astype(F32) * y for x, y in zip(packed, burning)]
            smokes = [(x >> 11).astype(F32) * y for x, y in zip(packed, burning)]
            for total, terms in zip(sums, (heats, smokes)):
                while len(terms) > 1:
                    terms = [x + y for x, y in zip(terms[::2], terms[1::2])]
                total.append(terms[0])

        advance(side, side[6:9], keep)
        result(slot).start()
        sums_ref[slot, :, 0:128] = sum(sums[0])
        sums_ref[slot, :, 128:256] = sum(sums[1])

    def into(target):
        return lambda first, values: store(target, first, values)

    lax.fori_loop(0, 2, columns, 0)

    def several(at, carry):
        slot = WIDE * at
        for start, some in zip((0, 2 // WIDE, 8 // WIDE), loads):

            @pl.when(at == start)
            def _():
                for load in some:
                    load.wait()

        for spot, side in enumerate(sides):
            begin(slot + spot, side)
        for step in range(SUB - 1):
            for side in sides:
                pair_of = (side[3:6], side[6:9])
                advance(side, pair_of[step % 2], into(pair_of[1 - step % 2]))
        for spot, side in enumerate(sides):
            finish(slot + spot, side)
        return carry

    lax.fori_loop(0, 32 // WIDE, several, 0)
    high, low = halves(sums_ref[...].reshape(256, 256))
    spread = spread_ref[...]
    means_ref[...] = (
        jnp.dot(high.astype(BF16), spread, preferred_element_type=F32)
        + jnp.dot(low.astype(BF16), spread, preferred_element_type=F32)
    ) * np.float32(0.1 / 256)
    dense = means_ref[pl.ds(0, 32, stride=8), :]
    for row in range(1, 8):
        dense = dense + pltpu.roll(means_ref[pl.ds(row, 32, stride=8), :], 16 * row, 1)
    tile_row = list_ref[0, pl.ds(me, 1), :]
    owners = jnp.broadcast_to(tile_row >> 5, (64, 32))
    col = jnp.broadcast_to(tile_row & 15, (64, 32))
    live = jnp.broadcast_to(tile_row, (64, 32)) >= 0
    device = lax.broadcasted_iota(jnp.int32, (64, 32), 0)
    to_left = live & (owners - 1 == device) & (col == 0) & ((owners & 7) > 0)
    to_right = live & (owners + 1 == device) & (col == 15) & ((owners & 7) < 7)
    spot = lax.broadcasted_iota(jnp.int32, (32, 128), 1) & 15
    picked = []
    for chosen, kept in (
        (live & (owners == device), None), (to_left, spot == 0), (to_right, spot == 7),
    ):
        chosen = jnp.where(chosen, 1.0, 0.0).astype(BF16)
        high, low = halves(dense if kept is None else jnp.where(kept, dense, 0.0))
        picked.append(
            jnp.dot(chosen, high.astype(BF16), preferred_element_type=F32)
            + jnp.dot(chosen, low.astype(BF16), preferred_element_type=F32)
        )
    flat_ref[:, 0:128] = picked[0]
    flat_ref[:, 128:256] = picked[1] + picked[2]
    for device in range(N_GX * N_GY):
        msg_ref[device] = flat_ref[device : device + 1, :]

    def settle(slot, carry):
        result(slot).wait()
        return carry

    lax.fori_loop(0, 32, settle, 0)


def place_kernel(where_ref, flux_ref, heat_ref, side_ref, smoke_ref, first_ref, last_ref):
    lane, sub = lanes_of(), sublanes_of()
    key = lane // 8
    heat_from = sub * 16 + lane % 8
    zero = jnp.zeros((8, 128), F32)

    def tile(at, lanes):
        fire = where_ref[0, at]
        line = flux_ref[jnp.maximum(fire, 0), :, lanes]
        return jnp.where(fire >= 0, jnp.broadcast_to(line, (8, 128)), 0.0)

    def find(value, index):
        return jnp.take_along_axis(value, index, axis=1, mode="promise_in_bounds")

    own, beside = slice(0, 128), slice(128, 256)
    for half in range(2):
        rows = slice(8 * half, 8 * half + 8)
        heat = smoke = zero
        for col in range(16):
            value = tile(16 * half + (col ^ 7), own)
            heat = jnp.where(key == col, find(value, heat_from), heat)
            smoke = jnp.where(key == col, find(value, heat_from + 8), smoke)
        rim_left = find(tile(41 + 8 * half, beside), heat_from)
        rim_right = find(tile(40 + 8 * half, beside), heat_from)
        left = pltpu.roll(jnp.where(lane == 127, rim_left, heat), 1, 1)
        right = pltpu.roll(jnp.where(lane == 0, rim_right, heat), 127, 1)
        heat_ref[rows, :] = heat
        smoke_ref[rows, :] = smoke
        side_ref[rows, :] = 0.5 * (right - left)
        if half == 0:
            first_ref[...] = heat[0:1]
        else:
            last_ref[...] = heat[7:8]


def rows_kernel(air_ref, first_ref, last_ref, sem):
    copies = (
        pltpu.make_async_copy(air_ref.at[:, 0, :], first_ref, sem.at[0]),
        pltpu.make_async_copy(air_ref.at[:, 15, :], last_ref, sem.at[1]),
    )
    for copy in copies:
        copy.start()
    for copy in copies:
        copy.wait()


def sides_kernel(air_ref, left_ref, right_ref):
    lane, sub = lanes_of(), sublanes_of()
    pick = jnp.where((lane == 127 * sub) & (sub < 2), 1.0, 0.0)
    columns = air_ref[...].reshape(3 * LEV * 16, 128)
    picked = 0.0
    for part in halves(columns):
        picked += lax.dot_general(
            pick.astype(BF16), part.astype(BF16), (((1,), (1,)), ((), ())),
            preferred_element_type=F32,
        )
    left_ref[...] = picked[0:1]
    right_ref[...] = picked[1:2]


def air_kernel(
    air_ref, above_ref, below_ref, left_ref, right_ref, token_in, out_ref, token_ref
):
    token_ref[...] = token_in[...]
    for side, ref in enumerate((left_ref, right_ref)):
        for at in range(30):
            level, line = 3 * LEV + 2 * side + at // 16, at % 16
            out_ref[level, line : line + 1, :] = ref[:, 128 * at : 128 * at + 128]
    lane = lax.broadcasted_iota(jnp.int32, (8, 16, 128), 2)
    row = lax.broadcasted_iota(jnp.int32, (8, 16, 128), 1)

    def chunk(at, carry):
        fields = []
        for part in range(3):
            start = part * LEV + at * 8
            mid = air_ref[pl.ds(start, 8)]
            above = above_ref[pl.ds(start, 8), :][:, None, :]
            below = below_ref[pl.ds(start, 8), :][:, None, :]
            up = jnp.where(row == 0, above, pltpu.roll(mid, 1, 1))
            down = jnp.where(row == 15, below, pltpu.roll(mid, 15, 1))
            left = jnp.where(lane == 0, 0.0, pltpu.roll(mid, 1, 2))
            right = jnp.where(lane == 127, 0.0, pltpu.roll(mid, 127, 2))
            fields.append((mid, up, down, left, right))
        for part in range(2):
            mid, up, down, left, right = fields[part]
            around = (up + down) + (left + right)
            out_ref[pl.ds(part * LEV + at * 8, 8)] = mid + viscosity * (around - 4.0 * mid)
        u, v = fields[0][0], fields[1][0]
        mid, up, down, left, right = fields[2]
        upwind = (
            jnp.maximum(u, 0.0) * (mid - up)
            + jnp.minimum(u, 0.0) * (down - mid)
            + jnp.maximum(v, 0.0) * (mid - left)
            + jnp.minimum(v, 0.0) * (right - mid)
        )
        out_ref[pl.ds(2 * LEV + at * 8, 8)] = mid - courant * upwind
        return carry

    lax.fori_loop(0, LEV // 8, chunk, 0)


def rims_kernel(part_ref, left_ref, right_ref, out_ref):
    sub, lane = sublanes_of(), lanes_of()
    expand = jnp.where((sub < 2) & (lane == 0), 1.0, 0.0) + jnp.where(
        (sub >= 2) & (sub < 4) & (lane == 127), 1.0, 0.0
    )
    expand = expand.astype(BF16)

    def chunk(at, carry):
        for part in range(3):
            spot = pl.ds(pl.multiple_of(part * (LEV * 16) + at * 128, 128), 128)
            left, right = left_ref[:, spot], right_ref[:, spot]
            if part < 2:
                left, right = viscosity * left, viscosity * right
            else:
                line = LEV // 8 + at
                level, line = 3 * LEV + (line >> 4), pl.ds(line & 15, 1)
                left = courant * jnp.maximum(part_ref[level, line, :], 0.0) * left
                right = -courant * jnp.minimum(part_ref[level + 2, line, :], 0.0) * right
            left_high, left_low = halves(left)
            right_high, right_low = halves(right)
            rims = jnp.where(sub == 0, left_high, 0.0)
            rims = jnp.where(sub == 1, left_low, rims)
            rims = jnp.where(sub == 2, right_high, rims)
            rims = jnp.where(sub == 3, right_low, rims)
            rim = lax.dot_general(
                rims.astype(BF16), expand, (((0,), (0,)), ((), ())), preferred_element_type=F32
            ).reshape(8, 16, 128)
            levels = pl.ds(part * LEV + at * 8, 8)
            out_ref[levels] = part_ref[levels] + rim
        return carry

    lax.fori_loop(0, LEV // 8, chunk, 0, unroll=2)


def final_kernel(
    part_ref, heat_ref, side_ref, smoke_ref, above_ref, below_ref, prof_ref,
    out_ref, made_ref, sem,
):
    heat = heat_ref[...]
    row = sublanes_of(16)
    up = jnp.where(row == 0, above_ref[...], pltpu.roll(heat, 1, 0))
    down = jnp.where(row == 15, below_ref[...], pltpu.roll(heat, 15, 0))
    sources = (0.5 * (down - up), side_ref[...], smoke_ref[...])
    copies = []
    for part in range(3):
        for half in range(2):
            first = part * LEV + half * (LEV // 2)

            def one(at, carry):
                for spot in range(8):
                    level = half * (LEV // 2) + 8 * at + spot
                    weight = prof_ref[pl.ds(level, 1), :]
                    before = part_ref[part * LEV + level]
                    made_ref[part * LEV + level] = before + weight * sources[part]
                return carry

            lax.fori_loop(0, LEV // 16, one, 0)
            some = pl.ds(first, LEV // 2)
            copies.append(
                pltpu.make_async_copy(
                    made_ref.at[some], out_ref.at[some], sem.at[2 * part + half]
                )
            )
            copies[-1].start()
    for copy in copies:
        copy.wait()


def constants():
    spots = (np.arange(128) + 0.5) / 16 + 0.5
    weights = np.maximum(0.0, 1.0 - np.abs(spots[:, None] - np.arange(10)[None, :]))
    wcol = np.zeros((128, 128), np.float32)
    for row in range(10):
        wcol[12 * row : 12 * row + 10, :] = weights.T
        wcol[12 * row + 10, :] = weights[:, 0]
        wcol[12 * row + 11, :] = weights[:, 9]
    spread = np.zeros((256, 128), np.float32)
    for c in range(128):
        spread[c, c // 16] = 1.0
        spread[128 + c, 8 + c // 16] = 1.0
    words = np.zeros((8, 128), np.int32)
    tables = (spread_rates * 20, heat_yields * 10, smoke_yields * 10)
    rates, heats, smokes = (np.rint(table).astype(np.int32) for table in tables)
    words[:, :13] = rates + 32 * heats + 2048 * smokes
    levels = np.arange(LEV, dtype=np.float32)
    profile = np.exp(-levels * np.float32(8.0) / np.float32(LEV))
    profile = np.broadcast_to((np.float32(0.5) * profile)[:, None], (LEV, 128))
    return wcol, spread, words, np.ascontiguousarray(profile)


def neighbours(last, first, axes, count):
    ends = count - 1
    before = lax.ppermute(last, axes, [(i, i + 1) for i in range(ends)])
    after = lax.ppermute(first, axes, [(i + 1, i) for i in range(ends)])
    return before, after


def on_device(air, level_set, fuel, tile_list):
    wcol, spread, words, profile = constants()
    rows = ("grp", "gx")
    levels = air.reshape(3 * LEV, 16, 128)

    first, last = pl.pallas_call(
        rows_kernel,
        out_shape=(shape(3 * LEV, 128), shape(3 * LEV, 128)),
        in_specs=[HBM], out_specs=(VMEM,) * 2, scratch_shapes=[pltpu.SemaphoreType.DMA((2,))],
        compiler_params=room(60), name="rows", cost_estimate=cost(10**5, 10**6),
    )(levels)
    air_above, air_below = neighbours(last, first, rows, N_GRP * N_GX)

    left, right = pl.pallas_call(
        sides_kernel, out_shape=(shape(1, 3 * LEV * 16), shape(1, 3 * LEV * 16)),
        in_specs=[VMEM], out_specs=(VMEM,) * 2, compiler_params=room(4),
        name="sides", cost_estimate=cost(10**8, 2 * 10**6),
    )(levels)
    table, choice, where = pl.pallas_call(
        table_kernel, out_shape=(
            shape(128, 256), shape(64, 128, dtype=BF16), shape(1, 128, dtype=jnp.int32)
        ),
        in_specs=[VMEM, HBM], out_specs=(VMEM,) * 3,
        scratch_shapes=[pltpu.VMEM((2, 16, 128), F32), pltpu.SemaphoreType.DMA((2,))],
        compiler_params=room(2), name="table", cost_estimate=cost(10**6, 10**6),
    )(tile_list, levels)
    windows, token = pl.pallas_call(
        windows_kernel,
        out_shape=(shape(N_GX * N_GY, 1, 256), shape(8, 128)),
        in_specs=[VMEM] * 5, out_specs=(VMEM,) * 2,
        scratch_shapes=[pltpu.VMEM((128, 256), F32), pltpu.VMEM((64, 256), F32)],
        compiler_params=room(2), name="windows", cost_estimate=cost(10**6, 10**6),
    )(table, choice, air_above, air_below, left)
    windows = lax.all_to_all(windows, ("gx", "gy"), split_axis=0, concat_axis=0, tiled=True)
    moved, token = pl.pallas_call(
        air_kernel, out_shape=(shape(3 * LEV + 4, 16, 128), shape(8, 128)),
        in_specs=[VMEM] * 6, out_specs=(VMEM, VMEM),
        compiler_params=room(8), name="air", cost_estimate=cost(2 * 10**8, 4 * 10**6),
    )(levels, air_above, air_below, left, right, token)

    phases, message, edge_left, edge_right = pl.pallas_call(
        fire_kernel,
        out_shape=(
            shape(32, 128, 128), shape(N_GX * N_GY, 1, 256),
            shape(1, 3 * LEV * 16), shape(1, 3 * LEV * 16),
        ),
        in_specs=[VMEM, HBM, HBM] + [VMEM] * 7, out_specs=(HBM, VMEM, VMEM, VMEM),
        scratch_shapes=[
            pltpu.VMEM((32, 128, 128), F32),
            pltpu.VMEM((32, 128, 128), jnp.int32),
            pltpu.VMEM((32, 128, 128), F32),
            pltpu.VMEM((32, 48, 128), F32),
            pltpu.VMEM((32, 8, 256), F32),
            pltpu.VMEM((256, 128), F32),
            pltpu.VMEM((64, 256), F32),
            pltpu.VMEM((64, 128), F32),
        ]
        + [pltpu.VMEM((256, 128), F32)] * WIDE
        + [pltpu.VMEM((128, 128), F32)] * WIDE
        + [pltpu.VMEM((128, 128), jnp.int32)] * WIDE
        + [pltpu.VMEM((128, 128), F32)] * (6 * WIDE)
        + [pltpu.SemaphoreType.DMA((32,)), pltpu.SemaphoreType.DMA((6,))],
        compiler_params=room(60), name="fire", cost_estimate=cost(10**9, 8 * 10**6),
    )(
        tile_list, level_set, fuel, windows, jnp.asarray(words), jnp.asarray(wcol, BF16),
        jnp.asarray(spread, BF16), left, right, token,
    )
    fluxes = lax.all_to_all(message, ("gx", "gy"), split_axis=0, concat_axis=0, tiled=True)
    air_left, air_right = neighbours(edge_right, edge_left, "gy", N_GY)
    rimmed = pl.pallas_call(
        rims_kernel, out_shape=shape(3 * LEV, 16, 128), in_specs=[VMEM] * 3, out_specs=VMEM,
        compiler_params=room(8), name="rims", cost_estimate=cost(2 * 10**8, 4 * 10**6),
    )(moved, air_left, air_right)
    heat, side, smoke, heat_first, heat_last = pl.pallas_call(
        place_kernel,
        out_shape=(shape(16, 128), shape(16, 128), shape(16, 128), shape(1, 128), shape(1, 128)),
        in_specs=[SMEM, VMEM], out_specs=(VMEM,) * 5, compiler_params=room(4),
        name="place", cost_estimate=cost(10**6, 10**6),
    )(where, fluxes)
    heat_above, heat_below = neighbours(heat_last, heat_first, rows, N_GRP * N_GX)
    result = pl.pallas_call(
        final_kernel, out_shape=shape(3 * LEV, 16, 128), in_specs=[VMEM] * 7, out_specs=HBM,
        scratch_shapes=[pltpu.VMEM((3 * LEV, 16, 128), F32), pltpu.SemaphoreType.DMA((6,))],
        compiler_params=room(8), name="final", cost_estimate=cost(10**6, 4 * 10**6),
    )(
        rimmed, heat, side, smoke, heat_above, heat_below, jnp.asarray(profile)
    )
    return (result.reshape(3, LEV, 16, 128), phases)


def solution(mesh):
    in_specs = (
        P(None, None, ("grp", "gx"), "gy"),
        P(("grp", "gx", "gy"), None, None),
        P(("grp", "gx", "gy"), None, None),
        P("grp", None, None),
    )
    out_specs = (P(None, None, ("grp", "gx"), "gy"), P(("grp", "gx", "gy"), None, None))
    return jax.shard_map(
        on_device, mesh=mesh, in_specs=in_specs, out_specs=out_specs, check_vma=False
    )
```

```python
import jax
import jax.numpy as jnp
import numpy as np
from jax import lax
from jax.experimental import pallas as pl
from jax.experimental.pallas import tpu as pltpu
from jax.sharding import PartitionSpec as P

SUB = 4
LEV = 80
N_GRP, N_GX, N_GY = 4, 8, 8
WIDE = 2

spread_rates = np.array(
    [0.3, 0.5, 0.9, 1.2, 0.6, 0.4, 0.7, 0.35, 0.25, 0.45, 0.55, 0.8, 1.0], np.float32
)
heat_yields = np.array(
    [1.0, 2.5, 4.0, 3.0, 1.5, 2.0, 5.0, 1.2, 0.8, 3.5, 2.2, 4.5, 2.8], np.float32
)
smoke_yields = np.array(
    [0.5, 1.5, 2.5, 1.0, 3.0, 0.8, 2.0, 1.8, 0.6, 2.6, 1.1, 3.4, 1.4], np.float32
)
courant = 0.1
viscosity = 0.1
buoyancy = 0.5
source_step = 0.5
fire_time = 0.1
wind_gain = 0.3

F32 = jnp.float32
BF16 = jnp.bfloat16
VMEM = pl.BlockSpec(memory_space=pltpu.VMEM)
SMEM = pl.BlockSpec(memory_space=pltpu.SMEM)
HBM = pl.BlockSpec(memory_space=pltpu.HBM)


def room(mib):
    return pltpu.CompilerParams(vmem_limit_bytes=mib * 1024 * 1024)


def shape(*dims, dtype=F32):
    return jax.ShapeDtypeStruct(dims, dtype)


def cost(flops, moved):
    return pl.CostEstimate(flops=flops, bytes_accessed=moved, transcendentals=0)


def lanes_of(rows=8):
    return lax.broadcasted_iota(jnp.int32, (rows, 128), 1)


def sublanes_of(rows=8):
    return lax.broadcasted_iota(jnp.int32, (rows, 128), 0)


def halves(value):
    high = value.astype(BF16).astype(F32)
    return high, value - high


def spread_line(line, row, low, high, rims):
    lane, sub = lanes_of(), sublanes_of()
    line = jnp.broadcast_to(line, (8, 128))
    here = (lane >= 12 * row) & (lane < 12 * row + 10)
    fanned = pltpu.roll(line, 0, 1, stride=8, stride_axis=0)
    first = pltpu.roll(fanned, (12 * row + 73) % 128, 1)
    second = pltpu.roll(fanned, (12 * row + 9) % 128, 1)
    low = jnp.where(here & ((sub < 7) | (lane > 12 * row)), first, low)
    high = jnp.where(here & ((sub > 0) | (lane < 12 * row + 9)), second, high)
    edges = pltpu.roll(line, (12 * row + 11) % 128, 1)
    rims = jnp.where((lane == 12 * row + 10 + sub) & (sub < 2), edges, rims)
    return low, high, rims


def table_kernel(list_ref, air_ref, tile_ref, choice_ref, where_ref, surf_ref, sem):
    copies = [
        pltpu.make_async_copy(air_ref.at[LEV * comp], surf_ref.at[comp], sem.at[comp])
        for comp in range(2)
    ]
    for copy in copies:
        copy.start()
    gx, gy = lax.axis_index("gx"), lax.axis_index("gy")
    me = gx * N_GY + gy
    left, right = gy > 0, gy < N_GY - 1
    k = lax.broadcasted_iota(jnp.int32, (1, 128), 1)
    codes = jnp.where(k < 32, me * 32 + (k ^ 7), -5)
    singles = (
        (40, right, me + 1, 0), (41, left, me - 1, 15), (48, right, me + 1, 16),
        (49, left, me - 1, 31),
    )
    for at, there, device, tile in singles:
        codes = jnp.where((k == at) & there, device * 32 + tile, codes)
    listed = list_ref[0]
    choice = jnp.zeros((64, 128), F32)
    for slot in range(32):
        entry = jnp.broadcast_to(listed[:, slot : slot + 1], (64, 128))
        choice = jnp.where(entry == codes, 1.0, choice)
    choice_ref[...] = choice.astype(BF16)
    device = sublanes_of(64).astype(F32) + 1.0
    holder = jnp.sum(choice * device, axis=0, keepdims=True) - 1.0
    where_ref[...] = holder.astype(jnp.int32)
    tile_ref[...] = jnp.zeros(tile_ref.shape, F32)
    for copy in copies:
        copy.wait()
    none = jnp.zeros((8, 128), F32)
    for comp in range(2):
        lanes = slice(128 * comp, 128 * comp + 128)
        field = surf_ref[comp] * wind_gain
        for half in range(2):
            found = [none, none, none]
            for row in range(10):
                at = 8 * half + row - 1
                if 0 <= at < 16:
                    found = spread_line(field[at : at + 1], row, *found)
            tile_ref[16 * half : 16 * half + 8, lanes] = found[0]
            tile_ref[16 * half + 8 : 16 * half + 16, lanes] = found[1]
            tile_ref[40 + 8 * half : 48 + 8 * half, lanes] = found[2]


def windows_kernel(
    table_ref, choice_ref, above_ref, below_ref, left_ref, out_ref, token_ref, tile_ref, made_ref
):
    token_ref[...] = jnp.zeros((8, 128), F32) + left_ref[0:1, 0:128] * 0.0
    tile_ref[...] = table_ref[...]
    for comp in range(2):
        lanes = slice(128 * comp, 128 * comp + 128)
        line_at = slice(LEV * comp, LEV * comp + 1)
        for half, (ref, row) in enumerate(((above_ref, 0), (below_ref, 9))):
            places = (
                slice(16 * half, 16 * half + 8),
                slice(16 * half + 8, 16 * half + 16),
                slice(40 + 8 * half, 48 + 8 * half),
            )
            old = [tile_ref[rows, lanes] for rows in places]
            fresh = spread_line(ref[line_at, :] * wind_gain, row, *old)
            for rows, value in zip(places, fresh):
                tile_ref[rows, lanes] = value
    choice = choice_ref[...]
    high, low = halves(tile_ref[...])
    made_ref[...] = jnp.dot(choice, high.astype(BF16), preferred_element_type=F32) + jnp.dot(
        choice, low.astype(BF16), preferred_element_type=F32
    )
    for fire in range(N_GX * N_GY):
        out_ref[fire] = made_ref[fire : fire + 1, :]


def fire_kernel(
    list_ref, phase_in, fuel_in, recv_ref, words_ref, wcol_ref, spread_ref,
    left_in, right_in, token_in, out_ref, msg_ref, left_out, right_out,
    phase_ref, fuel_ref, done_ref, column_ref, sums_ref, means_ref, flat_ref, line_ref, *rest,
):
    buffers, sem, sem_in = rest[:-2], rest[-2], rest[-1]
    sides = [buffers[at::WIDE] for at in range(WIDE)]
    left_out[...] = left_in[...]
    right_out[...] = right_in[...]
    loads = []
    for at, (low, high) in enumerate(((0, 2), (2, 8), (8, 32))):
        some = pl.ds(low, high - low)
        loads.append(
            (
                pltpu.make_async_copy(phase_in.at[some], phase_ref.at[some], sem_in.at[at]),
                pltpu.make_async_copy(fuel_in.at[some], fuel_ref.at[some], sem_in.at[3 + at]),
            )
        )
        for load in loads[-1]:
            load.start()
    lane24 = lanes_of(24)
    knot = sublanes_of(24)
    knot = (knot & 7) + (knot >> 3)
    unfold = (lane24 >= 12 * knot) & (lane24 < 12 * knot + 12)
    place = lax.broadcasted_iota(jnp.int32, (64, 256), 1)
    place = (place & 127) % 12
    me = lax.axis_index("gx") * N_GY + lax.axis_index("gy")
    entries = jnp.broadcast_to(list_ref[0, pl.ds(me, 1), :].astype(F32), (32, 32))
    across = lax.broadcasted_iota(jnp.int32, (32, 32), 1)
    along_slots = lax.broadcasted_iota(jnp.int32, (32, 32), 0)
    tiles = jnp.sum(jnp.where(across == along_slots, entries, 0.0), axis=1, keepdims=True)
    words = words_ref[...]
    row8, lane8 = sublanes_of(), lanes_of()

    tiles = jnp.broadcast_to(tiles, (32, 256)).astype(jnp.int32)
    target = lax.broadcasted_iota(jnp.int32, (32, 256), 1)
    owner, col = tiles >> 5, tiles & 15
    from_left = (owner - 1 == target - 64) & (col == 0) & ((owner & 7) > 0)
    from_right = (owner + 1 == target - 128) & (col == 15) & ((owner & 7) < 7)
    from_left = from_left & (target >= 64) & (target < 128)
    from_right = from_right & (target >= 128) & (target < 192)
    taken = ((owner == target) & (target < 64)) | from_left | from_right
    taken = jnp.where(taken & (tiles >= 0), 1.0, 0.0).astype(BF16)
    for device in range(N_GX * N_GY):
        flat_ref[device : device + 1, :] = recv_ref[device]
    sent = flat_ref[...]
    sent = jnp.concatenate(
        [
            jnp.where(place < 10, sent, 0.0), jnp.where(place == 10, sent, 0.0),
            jnp.where(place == 11, sent, 0.0), jnp.zeros((64, 256), F32),
        ],
        axis=0,
    )
    high, low = halves(sent)
    lines = jnp.dot(taken, high.astype(BF16), preferred_element_type=F32) + jnp.dot(
        taken, low.astype(BF16), preferred_element_type=F32
    )
    line_ref[0:32, :] = lines[:, 0:128]
    line_ref[32:64, :] = lines[:, 128:256]

    def columns(at, carry):
        parts = []
        for spot in range(8):
            for comp in range(2):
                line = line_ref[pl.ds(32 * comp + 8 * at + spot, 1), :]
                parts.append(jnp.where(unfold, jnp.broadcast_to(line, (24, 128)), 0.0))
        high, low = halves(jnp.concatenate(parts, axis=0))
        both = jnp.dot(high.astype(BF16), wcol_ref[...], preferred_element_type=F32) + jnp.dot(
            low.astype(BF16), wcol_ref[...], preferred_element_type=F32
        )
        for spot in range(8):
            column_ref[8 * at + spot] = both[48 * spot : 48 * spot + 48]
        return carry

    def result(slot):
        return pltpu.make_async_copy(done_ref.at[slot], out_ref.at[slot], sem.at[slot])

    def block(at):
        return slice(8 * at, 8 * at + 8)

    def store(target, at, values):
        for k, value in enumerate(values):
            target[block(at + k), :] = value

    def begin(slot, side):
        gust, rate, word = side[:3]
        runs = [column_ref[slot, 8 * at : 8 * at + 8, :] for at in range(6)]
        steps = [runs[at + 1] - runs[at] for at in (0, 1, 3, 4)]
        for first in range(0, 16, 8):
            blocks = range(first, first + 8)
            places = [pl.ds(j, 8, stride=16) for j in blocks]
            fuels = [fuel_ref[slot, there, :] for there in places]
            packed = [
                jnp.take_along_axis(words, fuel, axis=1, mode="promise_in_bounds")
                for fuel in fuels
            ]
            store(side[3], first, [phase_ref[slot, there, :] for there in places])
            bases = [(x & 31).astype(F32) * np.float32(0.05 * fire_time) for x in packed]
            for j, x, base in zip(blocks, packed, bases):
                rate[block(j), :] = base
                word[block(j), :] = x
            low = first // 8
            for comp in range(2):
                run, step = runs[3 * comp + low], steps[2 * comp + low]
                parts = [np.float32((j + 0.5) / 16 + 0.5 - low) for j in blocks]
                winds = [run + part * step for part in parts]
                for j, wind, base in zip(blocks, winds, bases):
                    gust[block(16 * comp + j), :] = wind * base

    def advance(side, source, keep):
        gust, rate = side[:2]
        field = source
        edge = field[block(0), :] - pltpu.roll(field[block(15), :], 1, 0)
        edge = jnp.where(row8 == 0, 0.0, edge)
        last = pltpu.roll(edge, 7, 0)
        for first in range(0, 16, 4):
            blocks = range(first, first + 4)
            fields = [field[block(j), :] for j in range(first, min(first + 4 + 1, 16))]
            aheads = [y - x for x, y in zip(fields, fields[1:])]
            if first == 16 - 4:
                aheads.append(last)
            backs = [edge] + aheads[:-1]
            edge = aheads[-1]
            side_backs = [
                jnp.where(lane8 == 0, 0.0, x - pltpu.roll(x, 1, 1)) for x, _ in zip(fields, blocks)
            ]
            side_aheads = [pltpu.roll(x, 127, 1) for x in side_backs]
            a = [jnp.maximum(x, 0.0) for x in backs]
            b = [jnp.minimum(x, 0.0) for x in aheads]
            upwinds = [x * x + y * y for x, y in zip(a, b)]
            c = [jnp.maximum(x, 0.0) for x in side_backs]
            d = [jnp.minimum(x, 0.0) for x in side_aheads]
            upwinds = [u + (x * x + y * y) for u, x, y in zip(upwinds, c, d)]
            inverses = [lax.rsqrt(jnp.maximum(u, 1e-36)) for u in upwinds]
            row_slopes = [x + y for x, y in zip(backs, aheads)]
            col_slopes = [x + y for x, y in zip(side_backs, side_aheads)]
            squares = [x * x + y * y for x, y in zip(row_slopes, col_slopes)]
            factors = [lax.rsqrt(jnp.maximum(x, 4.0)) for x in squares]
            along = [
                gust[block(j), :] * x + gust[block(16 + j), :] * y
                for j, x, y in zip(blocks, row_slopes, col_slopes)
            ]
            roots = [u * x for u, x in zip(upwinds, inverses)]
            speeds = [
                rate[block(j), :] + jnp.maximum(x * f, 0.0)
                for j, x, f in zip(blocks, along, factors)
            ]
            keep(first, [x - v * r for x, v, r in zip(fields, speeds, roots)])

    def finish(slot, side):
        word = side[2]
        sums = [[], []]

        def keep(first, values):
            for k, value in enumerate(values):
                done_ref[slot, pl.ds(first + k, 8, stride=16), :] = value
            burning = [jnp.exp(value) for value in values]
            burning = [1.0 / (1.0 + value) for value in burning]
            packed = [word[block(first + k), :] for k in range(len(values))]
            heats = [((x >> 5) & 63).astype(F32) * y for x, y in zip(packed, burning)]
            smokes = [(x >> 11).astype(F32) * y for x, y in zip(packed, burning)]
            for total, terms in zip(sums, (heats, smokes)):
                while len(terms) > 1:
                    terms = [x + y for x, y in zip(terms[::2], terms[1::2])]
                total.append(terms[0])

        advance(side, side[4], keep)
        result(slot).start()
        sums_ref[slot, :, 0:128] = sum(sums[0])
        sums_ref[slot, :, 128:256] = sum(sums[1])

    def into(target):
        return lambda first, values: store(target, first, values)

    lax.fori_loop(0, 4, columns, 0)

    def several(at, carry):
        slot = WIDE * at
        for start, some in zip((0, 2 // WIDE, 8 // WIDE), loads):

            @pl.when(at == start)
            def _():
                for load in some:
                    load.wait()

        for spot, side in enumerate(sides):
            begin(slot + spot, side)
        for step in range(SUB - 1):
            for side in sides:
                pair_of = (side[3], side[4])
                advance(side, pair_of[step % 2], into(pair_of[1 - step % 2]))
        for spot, side in enumerate(sides):
            finish(slot + spot, side)
        return carry

    lax.fori_loop(0, 32 // WIDE, several, 0)
    high, low = halves(sums_ref[...].reshape(256, 256))
    spread = spread_ref[...]
    means_ref[...] = (
        jnp.dot(high.astype(BF16), spread, preferred_element_type=F32)
        + jnp.dot(low.astype(BF16), spread, preferred_element_type=F32)
    ) * np.float32(0.1 / 256)
    dense = means_ref[pl.ds(0, 32, stride=8), :]
    for row in range(1, 8):
        dense = dense + pltpu.roll(means_ref[pl.ds(row, 32, stride=8), :], 16 * row, 1)
    tile_row = list_ref[0, pl.ds(me, 1), :]
    owners = jnp.broadcast_to(tile_row >> 5, (64, 32))
    col = jnp.broadcast_to(tile_row & 15, (64, 32))
    live = jnp.broadcast_to(tile_row, (64, 32)) >= 0
    device = lax.broadcasted_iota(jnp.int32, (64, 32), 0)
    to_left = live & (owners - 1 == device) & (col == 0) & ((owners & 7) > 0)
    to_right = live & (owners + 1 == device) & (col == 15) & ((owners & 7) < 7)
    spot = lax.broadcasted_iota(jnp.int32, (32, 128), 1) & 15
    picked = []
    for chosen, kept in (
        (live & (owners == device), None), (to_left, spot == 0), (to_right, spot == 7),
    ):
        chosen = jnp.where(chosen, 1.0, 0.0).astype(BF16)
        high, low = halves(dense if kept is None else jnp.where(kept, dense, 0.0))
        picked.append(
            jnp.dot(chosen, high.astype(BF16), preferred_element_type=F32)
            + jnp.dot(chosen, low.astype(BF16), preferred_element_type=F32)
        )
    flat_ref[:, 0:128] = picked[0]
    flat_ref[:, 128:256] = picked[1] + picked[2]
    for device in range(N_GX * N_GY):
        msg_ref[device] = flat_ref[device : device + 1, :]

    def settle(slot, carry):
        result(slot).wait()
        return carry

    lax.fori_loop(0, 32, settle, 0)


def place_kernel(where_ref, flux_ref, heat_ref, side_ref, smoke_ref, first_ref, last_ref):
    lane, sub = lanes_of(), sublanes_of()
    key = lane // 8
    heat_from = sub * 16 + lane % 8
    zero = jnp.zeros((8, 128), F32)

    def tile(at, lanes):
        fire = where_ref[0, at]
        line = flux_ref[jnp.maximum(fire, 0), :, lanes]
        return jnp.where(fire >= 0, jnp.broadcast_to(line, (8, 128)), 0.0)

    def find(value, index):
        return jnp.take_along_axis(value, index, axis=1, mode="promise_in_bounds")

    own, beside = slice(0, 128), slice(128, 256)
    for half in range(2):
        rows = slice(8 * half, 8 * half + 8)
        heat = smoke = zero
        for col in range(16):
            value = tile(16 * half + (col ^ 7), own)
            heat = jnp.where(key == col, find(value, heat_from), heat)
            smoke = jnp.where(key == col, find(value, heat_from + 8), smoke)
        rim_left = find(tile(41 + 8 * half, beside), heat_from)
        rim_right = find(tile(40 + 8 * half, beside), heat_from)
        left = pltpu.roll(jnp.where(lane == 127, rim_left, heat), 1, 1)
        right = pltpu.roll(jnp.where(lane == 0, rim_right, heat), 127, 1)
        heat_ref[rows, :] = heat
        smoke_ref[rows, :] = smoke
        side_ref[rows, :] = 0.5 * (right - left)
        if half == 0:
            first_ref[...] = heat[0:1]
        else:
            last_ref[...] = heat[7:8]


def rows_kernel(air_ref, first_ref, last_ref, sem):
    copies = (
        pltpu.make_async_copy(air_ref.at[:, 0, :], first_ref, sem.at[0]),
        pltpu.make_async_copy(air_ref.at[:, 15, :], last_ref, sem.at[1]),
    )
    for copy in copies:
        copy.start()
    for copy in copies:
        copy.wait()


def sides_kernel(air_ref, left_ref, right_ref):
    lane, sub = lanes_of(), sublanes_of()
    pick = jnp.where((lane == 127 * sub) & (sub < 2), 1.0, 0.0)
    columns = air_ref[...].reshape(3 * LEV * 16, 128)
    picked = 0.0
    for part in halves(columns):
        picked += lax.dot_general(
            pick.astype(BF16), part.astype(BF16), (((1,), (1,)), ((), ())),
            preferred_element_type=F32,
        )
    left_ref[...] = picked[0:1]
    right_ref[...] = picked[1:2]


def air_kernel(
    air_ref, above_ref, below_ref, left_ref, right_ref, token_in, out_ref, token_ref
):
    token_ref[...] = token_in[...]
    for side, ref in enumerate((left_ref, right_ref)):
        for at in range(30):
            level, line = 3 * LEV + 2 * side + at // 16, at % 16
            out_ref[level, line : line + 1, :] = ref[:, 128 * at : 128 * at + 128]
    lane = lax.broadcasted_iota(jnp.int32, (8, 16, 128), 2)
    row = lax.broadcasted_iota(jnp.int32, (8, 16, 128), 1)

    def chunk(at, carry):
        fields = []
        for part in range(3):
            start = part * LEV + at * 8
            mid = air_ref[pl.ds(start, 8)]
            above = above_ref[pl.ds(start, 8), :][:, None, :]
            below = below_ref[pl.ds(start, 8), :][:, None, :]
            up = jnp.where(row == 0, above, pltpu.roll(mid, 1, 1))
            down = jnp.where(row == 15, below, pltpu.roll(mid, 15, 1))
            left = jnp.where(lane == 0, 0.0, pltpu.roll(mid, 1, 2))
            right = jnp.where(lane == 127, 0.0, pltpu.roll(mid, 127, 2))
            fields.append((mid, up, down, left, right))
        for part in range(2):
            mid, up, down, left, right = fields[part]
            around = (up + down) + (left + right)
            out_ref[pl.ds(part * LEV + at * 8, 8)] = mid + viscosity * (around - 4.0 * mid)
        u, v = fields[0][0], fields[1][0]
        mid, up, down, left, right = fields[2]
        upwind = (
            jnp.maximum(u, 0.0) * (mid - up)
            + jnp.minimum(u, 0.0) * (down - mid)
            + jnp.maximum(v, 0.0) * (mid - left)
            + jnp.minimum(v, 0.0) * (right - mid)
        )
        out_ref[pl.ds(2 * LEV + at * 8, 8)] = mid - courant * upwind
        return carry

    lax.fori_loop(0, LEV // 8, chunk, 0)


def rims_kernel(part_ref, left_ref, right_ref, out_ref):
    sub, lane = sublanes_of(), lanes_of()
    expand = jnp.where((sub < 2) & (lane == 0), 1.0, 0.0) + jnp.where(
        (sub >= 2) & (sub < 4) & (lane == 127), 1.0, 0.0
    )
    expand = expand.astype(BF16)

    def chunk(at, carry):
        for part in range(3):
            spot = pl.ds(pl.multiple_of(part * (LEV * 16) + at * 128, 128), 128)
            left, right = left_ref[:, spot], right_ref[:, spot]
            if part < 2:
                left, right = viscosity * left, viscosity * right
            else:
                line = LEV // 8 + at
                level, line = 3 * LEV + (line >> 4), pl.ds(line & 15, 1)
                left = courant * jnp.maximum(part_ref[level, line, :], 0.0) * left
                right = -courant * jnp.minimum(part_ref[level + 2, line, :], 0.0) * right
            left_high, left_low = halves(left)
            right_high, right_low = halves(right)
            rims = jnp.where(sub == 0, left_high, 0.0)
            rims = jnp.where(sub == 1, left_low, rims)
            rims = jnp.where(sub == 2, right_high, rims)
            rims = jnp.where(sub == 3, right_low, rims)
            rim = lax.dot_general(
                rims.astype(BF16), expand, (((0,), (0,)), ((), ())), preferred_element_type=F32
            ).reshape(8, 16, 128)
            levels = pl.ds(part * LEV + at * 8, 8)
            out_ref[levels] = part_ref[levels] + rim
        return carry

    lax.fori_loop(0, LEV // 8, chunk, 0, unroll=2)


def final_kernel(
    part_ref, heat_ref, side_ref, smoke_ref, above_ref, below_ref, prof_ref,
    out_ref, made_ref, sem,
):
    heat = heat_ref[...]
    row = sublanes_of(16)
    up = jnp.where(row == 0, above_ref[...], pltpu.roll(heat, 1, 0))
    down = jnp.where(row == 15, below_ref[...], pltpu.roll(heat, 15, 0))
    sources = (0.5 * (down - up), side_ref[...], smoke_ref[...])
    copies = []
    for part in range(3):
        for half in range(2):
            first = part * LEV + half * (LEV // 2)

            def one(at, carry):
                for spot in range(8):
                    level = half * (LEV // 2) + 8 * at + spot
                    weight = prof_ref[pl.ds(level, 1), :]
                    before = part_ref[part * LEV + level]
                    made_ref[part * LEV + level] = before + weight * sources[part]
                return carry

            lax.fori_loop(0, LEV // 16, one, 0)
            some = pl.ds(first, LEV // 2)
            copies.append(
                pltpu.make_async_copy(
                    made_ref.at[some], out_ref.at[some], sem.at[2 * part + half]
                )
            )
            copies[-1].start()
    for copy in copies:
        copy.wait()


def constants():
    spots = (np.arange(128) + 0.5) / 16 + 0.5
    weights = np.maximum(0.0, 1.0 - np.abs(spots[:, None] - np.arange(10)[None, :]))
    wcol = np.zeros((128, 128), np.float32)
    for row in range(10):
        wcol[12 * row : 12 * row + 10, :] = weights.T
        wcol[12 * row + 10, :] = weights[:, 0]
        wcol[12 * row + 11, :] = weights[:, 9]
    spread = np.zeros((256, 128), np.float32)
    for c in range(128):
        spread[c, c // 16] = 1.0
        spread[128 + c, 8 + c // 16] = 1.0
    words = np.zeros((8, 128), np.int32)
    tables = (spread_rates * 20, heat_yields * 10, smoke_yields * 10)
    rates, heats, smokes = (np.rint(table).astype(np.int32) for table in tables)
    words[:, :13] = rates + 32 * heats + 2048 * smokes
    levels = np.arange(LEV, dtype=np.float32)
    profile = np.exp(-levels * np.float32(8.0) / np.float32(LEV))
    profile = np.broadcast_to((np.float32(0.5) * profile)[:, None], (LEV, 128))
    return wcol, spread, words, np.ascontiguousarray(profile)


def neighbours(last, first, axes, count):
    ends = count - 1
    before = lax.ppermute(last, axes, [(i, i + 1) for i in range(ends)])
    after = lax.ppermute(first, axes, [(i + 1, i) for i in range(ends)])
    return before, after


def on_device(air, level_set, fuel, tile_list):
    wcol, spread, words, profile = constants()
    rows = ("grp", "gx")
    levels = air.reshape(3 * LEV, 16, 128)

    first, last = pl.pallas_call(
        rows_kernel,
        out_shape=(shape(3 * LEV, 128), shape(3 * LEV, 128)),
        in_specs=[HBM], out_specs=(VMEM,) * 2, scratch_shapes=[pltpu.SemaphoreType.DMA((2,))],
        compiler_params=room(60), name="rows", cost_estimate=cost(10**5, 10**6),
    )(levels)
    air_above, air_below = neighbours(last, first, rows, N_GRP * N_GX)

    left, right = pl.pallas_call(
        sides_kernel, out_shape=(shape(1, 3 * LEV * 16), shape(1, 3 * LEV * 16)),
        in_specs=[VMEM], out_specs=(VMEM,) * 2, compiler_params=room(4),
        name="sides", cost_estimate=cost(10**8, 2 * 10**6),
    )(levels)
    table, choice, where = pl.pallas_call(
        table_kernel, out_shape=(
            shape(128, 256), shape(64, 128, dtype=BF16), shape(1, 128, dtype=jnp.int32)
        ),
        in_specs=[VMEM, HBM], out_specs=(VMEM,) * 3,
        scratch_shapes=[pltpu.VMEM((2, 16, 128), F32), pltpu.SemaphoreType.DMA((2,))],
        compiler_params=room(2), name="table", cost_estimate=cost(10**6, 10**6),
    )(tile_list, levels)
    windows, token = pl.pallas_call(
        windows_kernel,
        out_shape=(shape(N_GX * N_GY, 1, 256), shape(8, 128)),
        in_specs=[VMEM] * 5, out_specs=(VMEM,) * 2,
        scratch_shapes=[pltpu.VMEM((128, 256), F32), pltpu.VMEM((64, 256), F32)],
        compiler_params=room(2), name="windows", cost_estimate=cost(10**6, 10**6),
    )(table, choice, air_above, air_below, left)
    windows = lax.all_to_all(windows, ("gx", "gy"), split_axis=0, concat_axis=0, tiled=True)
    moved, token = pl.pallas_call(
        air_kernel, out_shape=(shape(3 * LEV + 4, 16, 128), shape(8, 128)),
        in_specs=[VMEM] * 6, out_specs=(VMEM, VMEM),
        compiler_params=room(8), name="air", cost_estimate=cost(2 * 10**8, 4 * 10**6),
    )(levels, air_above, air_below, left, right, token)

    phases, message, edge_left, edge_right = pl.pallas_call(
        fire_kernel,
        out_shape=(
            shape(32, 128, 128), shape(N_GX * N_GY, 1, 256),
            shape(1, 3 * LEV * 16), shape(1, 3 * LEV * 16),
        ),
        in_specs=[VMEM, HBM, HBM] + [VMEM] * 7, out_specs=(HBM, VMEM, VMEM, VMEM),
        scratch_shapes=[
            pltpu.VMEM((32, 128, 128), F32),
            pltpu.VMEM((32, 128, 128), jnp.int32),
            pltpu.VMEM((32, 128, 128), F32),
            pltpu.VMEM((32, 48, 128), F32),
            pltpu.VMEM((32, 8, 256), F32),
            pltpu.VMEM((256, 128), F32),
            pltpu.VMEM((64, 256), F32),
            pltpu.VMEM((64, 128), F32),
        ]
        + [pltpu.VMEM((256, 128), F32)] * WIDE
        + [pltpu.VMEM((128, 128), F32)] * WIDE
        + [pltpu.VMEM((128, 128), jnp.int32)] * WIDE
        + [pltpu.VMEM((128, 128), F32)] * (2 * WIDE)
        + [pltpu.SemaphoreType.DMA((32,)), pltpu.SemaphoreType.DMA((6,))],
        compiler_params=room(60), name="fire", cost_estimate=cost(10**9, 8 * 10**6),
    )(
        tile_list, level_set, fuel, windows, jnp.asarray(words), jnp.asarray(wcol, BF16),
        jnp.asarray(spread, BF16), left, right, token,
    )
    fluxes = lax.all_to_all(message, ("gx", "gy"), split_axis=0, concat_axis=0, tiled=True)
    air_left, air_right = neighbours(edge_right, edge_left, "gy", N_GY)
    rimmed = pl.pallas_call(
        rims_kernel, out_shape=shape(3 * LEV, 16, 128), in_specs=[VMEM] * 3, out_specs=VMEM,
        compiler_params=room(8), name="rims", cost_estimate=cost(2 * 10**8, 4 * 10**6),
    )(moved, air_left, air_right)
    heat, side, smoke, heat_first, heat_last = pl.pallas_call(
        place_kernel,
        out_shape=(shape(16, 128), shape(16, 128), shape(16, 128), shape(1, 128), shape(1, 128)),
        in_specs=[SMEM, VMEM], out_specs=(VMEM,) * 5, compiler_params=room(4),
        name="place", cost_estimate=cost(10**6, 10**6),
    )(where, fluxes)
    heat_above, heat_below = neighbours(heat_last, heat_first, rows, N_GRP * N_GX)
    result = pl.pallas_call(
        final_kernel, out_shape=shape(3 * LEV, 16, 128), in_specs=[VMEM] * 7, out_specs=HBM,
        scratch_shapes=[pltpu.VMEM((3 * LEV, 16, 128), F32), pltpu.SemaphoreType.DMA((6,))],
        compiler_params=room(8), name="final", cost_estimate=cost(10**6, 4 * 10**6),
    )(
        rimmed, heat, side, smoke, heat_above, heat_below, jnp.asarray(profile)
    )
    return (result.reshape(3, LEV, 16, 128), phases)


def solution(mesh):
    in_specs = (
        P(None, None, ("grp", "gx"), "gy"),
        P(("grp", "gx", "gy"), None, None),
        P(("grp", "gx", "gy"), None, None),
        P("grp", None, None),
    )
    out_specs = (P(None, None, ("grp", "gx"), "gy"), P(("grp", "gx", "gy"), None, None))
    return jax.shard_map(
        on_device, mesh=mesh, in_specs=in_specs, out_specs=out_specs, check_vma=False
    )
```
